32 devices in a mesh: dp: 8 (over z, x), own: 4 (over y, core).
Axes of the slice: x: 2, y: 2, z: 4, core: 2. Of those that a mesh axis runs over, the one named last changes fastest.
Arguments:
- frames: bfloat16 [8192, 21, 21, 64], P(('dp', 'own')), may hold values from -6 to 6
- actions: int32 [32, 256], P(('dp', 'own')), may hold values from 0 to 17
- dones: int32 [32, 256], P(('dp', 'own')), may hold values 0 or 1
- lengths: int32 [32], P(('dp', 'own')), may hold values from 32 to 256, as said below
- rewards: float32 [32, 256], P(('dp', 'own')), may hold values from -6 to 6
- old_values: float32 [32, 256], P(('dp', 'own')), may hold values from -6 to 6
- old_logp: float32 [32, 256], P(('dp', 'own')), may hold values from -3.6 to -2.2
- conv_first: float32 [256, 32], replicated, may hold values from -0.375 to 0.375
- conv_second: float32 [512, 64], replicated, may hold values from -0.25 to 0.25
- conv_third: float32 [576, 64], replicated, may hold values from -0.25 to 0.25
- dense_hidden: float32 [3136, 512], P('dp', 'own'), may hold values from -0.109375 to 0.109375
- dense_heads: float32 [512, 19], replicated, may hold values from -1 to 1
- bias_all: float32 [691], replicated, may hold values from -1.5 to 1.5
- mean_first: float32 [256, 32], replicated, may hold values from -0.01953125 to 0.01953125
- mean_second: float32 [512, 64], replicated, may hold values from -0.01953125 to 0.01953125
- mean_third: float32 [576, 64], replicated, may hold values from -0.01953125 to 0.01953125
- mean_dense: float32 [3136, 512], P('dp', 'own'), may hold values from -0.015625 to 0.015625
- mean_heads: float32 [512, 19], replicated, may hold values from -0.0390625 to 0.0390625
- mean_bias: float32 [691], replicated, may hold values from -0.02734375 to 0.02734375
- square_first: float32 [256, 32], replicated, may hold values from 1.0986329e-05 to 4.3945314e-05
- square_second: float32 [512, 64], replicated, may hold values from 1.0986329e-05 to 4.3945314e-05
- square_third: float32 [576, 64], replicated, may hold values from 1.0986329e-05 to 4.3945314e-05
- square_dense: float32 [3136, 512], P('dp', 'own'), may hold values from 7.6293945e-06 to 3.0517578e-05
- square_heads: float32 [512, 19], replicated, may hold values from 4.3945314e-05 to 0.00017578126
- square_bias: float32 [691], replicated, may hold values from 1.953125e-05 to 7.8125e-05
- left_first: float32 [256, 256], replicated, may hold values from -1 to 1, as said below
- right_first: float32 [32, 32], replicated, may hold values from -1 to 1, as said below
- left_second: float32 [512, 512], replicated, may hold values from -1 to 1, as said below
- right_second: float32 [64, 64], replicated, may hold values from -1 to 1, as said below
- left_third: float32 [576, 576], replicated, may hold values from -1 to 1, as said below
- right_third: float32 [64, 64], replicated, may hold values from -1 to 1, as said below
- right_dense: float32 [4, 128, 128], P('own'), may hold values from -1 to 1, as said below
- left_heads: float32 [512, 512], replicated, may hold values from -1 to 1, as said below
- right_heads: float32 [19, 19], replicated, may hold values from -1 to 1, as said below
Outputs:
- frames_grad: bfloat16 [8192, 21, 21, 64], P(('dp', 'own'))
- grad_first: float32 [256, 32], replicated
- grad_second: float32 [512, 64], replicated
- grad_third: float32 [576, 64], replicated
- grad_dense: float32 [3136, 512], P('dp', 'own')
- grad_heads: float32 [512, 19], replicated
- grad_bias: float32 [691], replicated
- momentum_first: float32 [256, 32], replicated
- momentum_second: float32 [512, 64], replicated
- momentum_third: float32 [576, 64], replicated
- momentum_dense: float32 [3136, 512], P('dp', 'own')
- momentum_heads: float32 [512, 19], replicated
- momentum_bias: float32 [691], replicated
- variance_first: float32 [256, 32], replicated
- variance_second: float32 [512, 64], replicated
- variance_third: float32 [576, 64], replicated
- variance_dense: float32 [3136, 512], P('dp', 'own')
- variance_heads: float32 [512, 19], replicated
- variance_bias: float32 [691], replicated
- updated_first: float32 [256, 32], replicated
- updated_second: float32 [512, 64], replicated
- updated_third: float32 [576, 64], replicated
- updated_dense: float32 [3136, 512], P('dp', 'own')
- updated_heads: float32 [512, 19], replicated
- updated_bias: float32 [691], replicated
The draws below stay inside these ranges and needn't reach their ends.
Inputs may be any that keep to these rules, and one draw needn't show every extreme that they name: `lengths`: the last trajectory has all 256 steps valid. `left_first`: an orthogonal matrix. `right_first`: an orthogonal matrix. `left_second`: an orthogonal matrix. `right_second`: an orthogonal matrix. `left_third`: an orthogonal matrix. `right_third`: an orthogonal matrix. `right_dense`: each block is an orthogonal matrix. `left_heads`: an orthogonal matrix. `right_heads`: an orthogonal matrix.
All inputs are finite; a program needn't handle non-finite values. No bound on the sum of `dones` on one device may be relied on, other than what follows from the above.
Results may differ from the reference program's by a relative error of at most 0.013.
The reference program's roundings to bfloat16 on the way count: a program that leaves them out, or rounds other values in their place, can miss the bound.
Values may be sent and summed in bfloat16 or wider, within the bound.
No kernel may reach another device: no remote copies, remote signals or barrier semaphores. Data moves between devices by JAX's collectives and lax.ppermute only.
A program may use at most 384 MiB of HBM per device.

```python
import math
import jax
import jax.numpy as jnp
from jax import lax

GRID = 21
PLANES = 64
C1 = 32
C2 = 64
HID = 512
ACT = 18
FCB = 128
STEPS = 256
STEP = 10
TRAJ_DEV = 1
TRAJ = 32
TOKENS = 8192
FLAT = 3136
K1 = 256
K2 = 512
K3 = 576
HEADS = 19
BIAS = 691
N_DP = 8
N_OWN = 4


def basis_matrix(key, size):
    sign_key, order_key = jax.random.split(key)
    signs = (2 * jax.random.randint(sign_key, (size,), 0, 2) - 1).astype(jnp.float32)
    order = jax.random.permutation(order_key, size)
    rows = jnp.arange(size).astype(jnp.float32)[:, None]
    freq = order.astype(jnp.float32)[None, :]
    table = jnp.cos(jnp.pi * (rows + 0.5) * freq / size)
    scale = jnp.where(order[None, :] == 0, jnp.sqrt(1.0 / size), jnp.sqrt(2.0 / size))
    return (signs[:, None] * table * scale).astype(jnp.float32)


def draw_lengths(key, part):
    key = jax.random.fold_in(key, 5)
    index = jnp.arange(TRAJ)
    device = index // TRAJ_DEV
    data = device // N_OWN
    owner = device % N_OWN
    rise = (N_DP - 1 + 2 * data) * (N_OWN - 1 + 2 * owner)
    top = jnp.maximum(STEPS * rise // (9 * (N_DP - 1) * (N_OWN - 1)), STEPS // 8)
    bottom = jnp.maximum(top * 2 // 3, STEPS // 8)
    drawn = jax.random.randint(key, (TRAJ,), 0, 1 << 20) % (top - bottom + 1) + bottom
    return jnp.where(index == TRAJ - 1, STEPS, drawn).astype(jnp.int32)


def draw_left_first(key, part):
    key = jax.random.fold_in(key, 11)
    return basis_matrix(key, K1)


def draw_right_first(key, part):
    key = jax.random.fold_in(key, 12)
    return basis_matrix(key, C1)


def draw_left_second(key, part):
    key = jax.random.fold_in(key, 13)
    return basis_matrix(key, K2)


def draw_right_second(key, part):
    key = jax.random.fold_in(key, 14)
    return basis_matrix(key, C2)


def draw_left_third(key, part):
    key = jax.random.fold_in(key, 15)
    return basis_matrix(key, K3)


def draw_right_third(key, part):
    key = jax.random.fold_in(key, 16)
    return basis_matrix(key, C2)


def draw_right_dense(key, part):
    key = jax.random.fold_in(key, 17)
    keys = jax.random.split(key, HID // FCB)
    return jax.vmap(lambda one_key: basis_matrix(one_key, FCB))(keys)


def draw_left_heads(key, part):
    key = jax.random.fold_in(key, 18)
    return basis_matrix(key, HID)


def draw_right_heads(key, part):
    key = jax.random.fold_in(key, 19)
    return basis_matrix(key, HEADS)


def touch_ends(entries, rng, least, largest):
    extent = entries.shape
    spot = [jax.random.randint(jax.random.fold_in(rng, axis), (), 0, extent[axis]) for axis in range(len(extent))]
    entries = entries.at[tuple(spot)].set(least)
    longest = extent.index(max(extent))
    spot[longest] = (spot[longest] + 1) % extent[longest]
    return entries.at[tuple(spot)].set(largest)


def block_levels(key, shape, cuts, least, high):
    def one(dim, shards_of):
        heights = jax.random.uniform(jax.random.fold_in(jax.random.fold_in(key, 6), dim), (shards_of,), jnp.float32, least / len(cuts), high / len(cuts))
        return jnp.repeat(jnp.exp(heights), shape[dim] // shards_of).reshape((-1,) + (1,) * (len(shape) - dim - 1))

    gain = one(*cuts[0])
    for cut in cuts[1:]:
        gain = gain * one(*cut)
    return gain


def noise(key, shape, spread, bound, cuts=(), held_as=jnp.bfloat16):
    values = jax.random.normal(key, shape, jnp.float32) * spread
    if len(cuts) > 0:
        values = block_levels(key, shape, cuts, -0.22, 0.18) * values
    return jnp.clip(values, min=-bound, max=bound).astype(held_as)


def setup_inputs(seed: int = 0) -> dict:
    streams_of = jax.random.split(jax.random.key(seed), 35)
    frames = noise(streams_of[0], (TOKENS, GRID, GRID, PLANES), 1.0, 6.0, ((0, 32),))
    actions = touch_ends(jax.random.randint(streams_of[1], (TRAJ, STEPS), 0, ACT), jax.random.fold_in(streams_of[1], 1), 0, ACT - 1).astype(jnp.int32)
    dones = touch_ends((jax.random.randint(streams_of[2], (TRAJ, STEPS), 0, 16) < 1).astype(jnp.int32), jax.random.fold_in(streams_of[2], 1), 0, 1)
    lengths = draw_lengths(jax.random.fold_in(streams_of[34], 71), 0)
    rewards = noise(streams_of[4], (TRAJ, STEPS), 1.0, 6.0, ((0, 32),), jnp.float32)
    old_values = noise(streams_of[5], (TRAJ, STEPS), 1.0, 6.0, ((0, 32),), jnp.float32)
    old_logp = jnp.clip(-3.6 + 1.3999999 * jax.random.uniform(streams_of[6], (TRAJ, STEPS), jnp.float32) ** block_levels(streams_of[6], (TRAJ, STEPS), ((0, 32),), -0.2, 0.2), -3.6, -2.2)
    conv_first = noise(streams_of[7], (K1, C1), K1 ** -0.5, 0.375, (), jnp.float32)
    conv_second = noise(streams_of[8], (K2, C2), K2 ** -0.5, 0.25, (), jnp.float32)
    conv_third = noise(streams_of[9], (K3, C2), K3 ** -0.5, 0.25, (), jnp.float32)
    dense_hidden = noise(streams_of[10], (FLAT, HID), FLAT ** -0.5, 0.109375, ((0, 8), (1, 4)), jnp.float32)
    dense_heads = noise(streams_of[11], (HID, HEADS), (HID // 16) ** -0.5, 1.0, (), jnp.float32)
    bias_all = noise(streams_of[12], (BIAS,), 0.3, 1.5, (), jnp.float32)
    mean_first = noise(streams_of[13], (K1, C1), (0.3 / TOKENS ** 0.5), 0.01953125, (), jnp.float32)
    mean_second = noise(streams_of[14], (K2, C2), (0.3 / TOKENS ** 0.5), 0.01953125, (), jnp.float32)
    mean_third = noise(streams_of[15], (K3, C2), (0.3 / TOKENS ** 0.5), 0.01953125, (), jnp.float32)
    mean_dense = noise(streams_of[16], (FLAT, HID), (0.25 / TOKENS ** 0.5), 0.015625, ((0, 8), (1, 4)), jnp.float32)
    mean_heads = noise(streams_of[17], (HID, HEADS), (0.6 / TOKENS ** 0.5), 0.0390625, (), jnp.float32)
    mean_bias = noise(streams_of[18], (BIAS,), (0.4 / TOKENS ** 0.5), 0.02734375, (), jnp.float32)
    square_first = jnp.clip(jnp.exp(jax.random.uniform(streams_of[19], (K1, C1), jnp.float32, math.log(1.0986328561557457e-05), math.log(4.394531424622983e-05))), 1.0986328561557457e-05, 4.394531424622983e-05)
    square_second = jnp.clip(jnp.exp(jax.random.uniform(streams_of[20], (K2, C2), jnp.float32, math.log(1.0986328561557457e-05), math.log(4.394531424622983e-05))), 1.0986328561557457e-05, 4.394531424622983e-05)
    square_third = jnp.clip(jnp.exp(jax.random.uniform(streams_of[21], (K3, C2), jnp.float32, math.log(1.0986328561557457e-05), math.log(4.394531424622983e-05))), 1.0986328561557457e-05, 4.394531424622983e-05)
    square_dense = jnp.clip(jnp.exp(math.log(3.0517578125e-05) - 1.3862944 * jax.random.uniform(streams_of[22], (FLAT, HID), jnp.float32) ** block_levels(streams_of[22], (FLAT, HID), ((0, 8), (1, 4)), -0.2, 0.2)), 7.62939453125e-06, 3.0517578125e-05)
    square_heads = jnp.clip(jnp.exp(jax.random.uniform(streams_of[23], (HID, HEADS), jnp.float32, math.log(4.394531424622983e-05), math.log(0.00017578126))), 4.394531424622983e-05, 0.00017578126)
    square_bias = jnp.clip(jnp.exp(jax.random.uniform(streams_of[24], (BIAS,), jnp.float32, math.log(1.9531249563442543e-05), math.log(7.812499825377017e-05))), 1.9531249563442543e-05, 7.812499825377017e-05)
    left_first = draw_left_first(jax.random.fold_in(streams_of[34], 71), 0)
    right_first = draw_right_first(jax.random.fold_in(streams_of[34], 71), 0)
    left_second = draw_left_second(jax.random.fold_in(streams_of[34], 71), 0)
    right_second = draw_right_second(jax.random.fold_in(streams_of[34], 71), 0)
    left_third = draw_left_third(jax.random.fold_in(streams_of[34], 71), 0)
    right_third = draw_right_third(jax.random.fold_in(streams_of[34], 71), 0)
    right_dense = draw_right_dense(jax.random.fold_in(streams_of[34], 71), 0)
    left_heads = draw_left_heads(jax.random.fold_in(streams_of[34], 71), 0)
    right_heads = draw_right_heads(jax.random.fold_in(streams_of[34], 71), 0)
    return {"frames": frames, "actions": actions, "dones": dones, "lengths": lengths, "rewards": rewards, "old_values": old_values, "old_logp": old_logp, "conv_first": conv_first, "conv_second": conv_second, "conv_third": conv_third, "dense_hidden": dense_hidden, "dense_heads": dense_heads, "bias_all": bias_all, "mean_first": mean_first, "mean_second": mean_second, "mean_third": mean_third, "mean_dense": mean_dense, "mean_heads": mean_heads, "mean_bias": mean_bias, "square_first": square_first, "square_second": square_second, "square_third": square_third, "square_dense": square_dense, "square_heads": square_heads, "square_bias": square_bias, "left_first": left_first, "right_first": right_first, "left_second": left_second, "right_second": right_second, "left_third": left_third, "right_third": right_third, "right_dense": right_dense, "left_heads": left_heads, "right_heads": right_heads}


GAMMA = 0.99
LAMBDA = 0.95
CLIP = 0.1
ENTROPY_COEF = 0.01
VALUE_COEF = 0.5
BETA = 0.5
EPSILON = 1e-08
RATE = 1.0
BIAS_RATE = 0.1
HIGH = lax.Precision.HIGHEST

@jax.custom_vjp
def low(v):
    return lax.optimization_barrier(v.astype(jnp.bfloat16)).astype(jnp.float32)

@jax.custom_vjp
def low_back(v):
    return v

def low_keep(v):
    return (low(v), None)

def low_pass(kept, grad):
    return (grad,)

def back_keep(v):
    return (v, None)

def back_low(kept, grad):
    return (low(grad),)
low.defvjp(low_keep, low_pass)
low_back.defvjp(back_keep, back_low)

def advantage_terms(lengths, dones, rewards, old_values):
    count_traj = rewards.shape[0]
    position = lax.broadcasted_iota(jnp.int32, rewards.shape, 1)
    mask = (position < lengths[:, None]).astype(jnp.float32)
    next_live = (position + 1 < lengths[:, None]).astype(jnp.float32)
    shifted = jnp.concatenate([old_values[:, 1:], jnp.zeros((count_traj, 1), jnp.float32)], axis=1)
    going = 1.0 - dones.astype(jnp.float32)
    delta = rewards + GAMMA * going * shifted * next_live - old_values

    def back_step(carry, item):
        delta_t, going_t, mask_t = item
        value = mask_t * (delta_t + GAMMA * LAMBDA * going_t * carry)
        return (value, value)
    _, advantage = lax.scan(back_step, jnp.zeros((count_traj,), jnp.float32), (delta.T, going.T, mask.T), reverse=True)
    advantage = advantage.T
    return (mask, advantage, advantage + old_values)

def policy_loss(heads, actions, norm_adv, returns, mask, old_logp, count):
    acts = heads.shape[1] - 1
    logits = heads[:, :acts]
    value = heads[:, acts]
    logp_all = jax.nn.log_softmax(logits, axis=-1)
    choose = (lax.broadcasted_iota(jnp.int32, logits.shape, 1) == actions[:, None]).astype(jnp.float32)
    logp = lax.optimization_barrier(jnp.sum(logp_all * choose, axis=-1))
    entropy = -lax.optimization_barrier(jnp.sum(jnp.exp(logp_all) * logp_all, axis=-1))
    ratio = jnp.exp(logp - old_logp)
    soft = 1.0 + CLIP * jnp.tanh((ratio - 1.0) / CLIP)
    policy = -jnp.minimum(ratio * norm_adv, soft * norm_adv)
    each = policy + VALUE_COEF * 0.5 * (value - returns) ** 2 - ENTROPY_COEF * entropy
    return jnp.sum(mask * each) / count

def cell_patches(inputs, kernel, out):
    return jnp.concatenate([inputs[:, i:i + out, j:j + out, :] for i in range(kernel) for j in range(kernel)], axis=-1)

def fold_cells(inputs):
    count_rows, height, width, chans = inputs.shape
    shaped = inputs.reshape(count_rows, height // 2, 2, width // 2, 2, chans).transpose(0, 1, 3, 2, 4, 5)
    return shaped.reshape(count_rows, height // 2, width // 2, 4 * chans)

def project(inputs, weight):
    shape = inputs.shape
    out = jnp.dot(inputs.reshape(-1, shape[-1]), weight, precision=HIGH)
    return out.reshape(shape[:-1] + (weight.shape[1],))

def network(params, frames):
    first, second, third, dense, heads, bias_all = params
    c_one = first.shape[1]
    c_two = second.shape[1]
    hid = dense.shape[1]
    bias_one = bias_all[:c_one]
    bias_two = bias_all[c_one:c_one + c_two]
    bias_three = bias_all[c_one + c_two:c_one + 2 * c_two]
    bias_dense = bias_all[c_one + 2 * c_two:c_one + 2 * c_two + hid]
    bias_heads = bias_all[c_one + 2 * c_two + hid:]
    grid = frames.shape[1]
    patches_one = cell_patches(frames, 2, grid - 1)
    act_one = low(jax.nn.gelu(low_back(project(patches_one, low(first)) + bias_one)))
    folded = fold_cells(act_one)
    patches_two = cell_patches(folded, 2, folded.shape[1] - 1)
    act_two = low(jax.nn.gelu(low_back(project(patches_two, low(second)) + bias_two)))
    patches_three = cell_patches(act_two, 3, act_two.shape[1] - 2)
    act_three = low(jax.nn.gelu(low_back(project(patches_three, low(third)) + bias_three)))
    flat = act_three.reshape(act_three.shape[0], -1)
    hidden = low(jax.nn.gelu(low_back(project(flat, low(dense)) + bias_dense)))
    return low_back(project(hidden, low(heads)) + bias_heads)

def adam_terms(grad, mean, square):
    momentum = BETA * mean + (1.0 - BETA) * grad
    variance = BETA * square + (1.0 - BETA) * grad * grad
    fix = 1.0 - BETA ** STEP
    direction = momentum / fix / (jnp.sqrt(variance / fix) + EPSILON)
    return (momentum, variance, direction)

def rotated_step(weight, grad, mean, square, left, right, rate):
    turned = jnp.dot(jnp.dot(left.T, grad, precision=HIGH), right, precision=HIGH)
    momentum, variance, direction = adam_terms(turned, mean, square)
    back = jnp.dot(jnp.dot(left, direction, precision=HIGH), right.T, precision=HIGH)
    return (momentum, variance, weight - rate * back)

def dense_step(weight, grad, mean, square, blocks, rate):
    split = grad.reshape(grad.shape[0], blocks.shape[0], blocks.shape[1])
    turned = jnp.einsum('rbk,bkl->rbl', split, blocks, precision=HIGH).reshape(grad.shape)
    momentum, variance, direction = adam_terms(turned, mean, square)
    back = jnp.einsum('rbl,bkl->rbk', direction.reshape(split.shape), blocks, precision=HIGH).reshape(grad.shape)
    return (momentum, variance, weight - rate * back)

def reference(frames, actions, dones, lengths, rewards, old_values, old_logp, conv_first, conv_second, conv_third, dense_hidden, dense_heads, bias_all, mean_first, mean_second, mean_third, mean_dense, mean_heads, mean_bias, square_first, square_second, square_third, square_dense, square_heads, square_bias, left_first, right_first, left_second, right_second, left_third, right_third, right_dense, left_heads, right_heads):
    mask, advantage, returns = advantage_terms(lengths, dones, rewards, old_values)
    count = jnp.sum(mask)
    centre = jnp.sum(mask * advantage) / count
    var = jnp.sum(mask * (advantage - centre) ** 2) / count
    norm_adv = (advantage - centre) * lax.rsqrt(var + 1e-05)
    params = (conv_first, conv_second, conv_third, dense_hidden, dense_heads, bias_all)
    traj = actions.shape[0]
    steps = actions.shape[1]
    shaped = frames.reshape((traj, steps) + frames.shape[1:])

    def one_traj(totals, item):
        traj_frames, traj_actions, traj_adv, traj_returns, traj_mask, traj_logp = item

        def loss_of(weights, inputs):
            return policy_loss(network(weights, inputs), traj_actions, traj_adv, traj_returns, traj_mask, traj_logp, count)
        _, back = jax.vjp(loss_of, params, traj_frames.astype(jnp.float32))
        weight_grads, input_grads = back(jnp.float32(1.0))
        totals = jax.tree.map(lambda a, b: a + b, totals, weight_grads)
        return (totals, input_grads.astype(jnp.bfloat16))
    zeros = jax.tree.map(jnp.zeros_like, params)
    grads, input_grads = lax.scan(one_traj, zeros, (shaped, actions, norm_adv, returns, mask, old_logp))
    frames_grad = input_grads.reshape(frames.shape)
    grad_first, grad_second, grad_third, grad_dense, grad_heads, grad_bias = grads
    mom_one, var_one, new_one = rotated_step(conv_first, grad_first, mean_first, square_first, left_first, right_first, RATE / math.sqrt(K1))
    mom_two, var_two, new_two = rotated_step(conv_second, grad_second, mean_second, square_second, left_second, right_second, RATE / math.sqrt(K2))
    mom_three, var_three, new_three = rotated_step(conv_third, grad_third, mean_third, square_third, left_third, right_third, RATE / math.sqrt(K3))
    mom_dense, var_dense, new_dense = dense_step(dense_hidden, grad_dense, mean_dense, square_dense, right_dense, RATE / math.sqrt(FLAT))
    mom_heads, var_heads, new_heads = rotated_step(dense_heads, grad_heads, mean_heads, square_heads, left_heads, right_heads, RATE / math.sqrt(HID))
    mom_bias, var_bias, bias_dir = adam_terms(grad_bias, mean_bias, square_bias)
    new_bias = bias_all - BIAS_RATE * bias_dir
    return (frames_grad, grad_first, grad_second, grad_third, grad_dense, grad_heads, grad_bias, mom_one, mom_two, mom_three, mom_dense, mom_heads, mom_bias, var_one, var_two, var_three, var_dense, var_heads, var_bias, new_one, new_two, new_three, new_dense, new_heads, new_bias)
```

```python
import functools
import math

import jax
import jax.numpy as jnp
from jax import lax
from jax.experimental import pallas as pl
from jax.experimental.pallas import tpu as pltpu
from jax.sharding import PartitionSpec as P

STEP = 10
GAMMA = 0.99
LAMBDA = 0.95
CLIP = 0.1
ENTROPY_COEF = 0.01
VALUE_COEF = 0.5
BETA = 0.5
EPSILON = 1e-08
RATE = 1.0
BIAS_RATE = 0.1
HIGH = lax.Precision.HIGHEST
ROOT = math.sqrt(2.0 / math.pi)
CUBE = 0.044715
BF = jnp.bfloat16
F32 = jnp.float32
MIB = 2**20

NN = (((1,), (0,)), ((), ()))
NT = (((1,), (1,)), ((), ()))
TN = (((0,), (0,)), ((), ()))


def dot(a, b, dims=NN, precision=None):
    return lax.dot_general(a, b, dims, precision=precision, preferred_element_type=F32)


def params(limit=48, **more):
    return pltpu.CompilerParams(vmem_limit_bytes=limit * MIB, **more)


def gelu_both(x):
    x2 = x * x
    t = jnp.tanh(x * (ROOT + (ROOT * CUBE) * x2))
    h = 0.5 * x
    act = h + h * t
    slope = (0.5 + 0.5 * t) + h * (1.0 - t * t) * (ROOT + (3.0 * ROOT * CUBE) * x2)
    return act, slope


def wide(column, rows, n):
    k = column.shape[0]
    tall = jnp.concatenate([column] * (rows // k), axis=0) if rows > k else column
    return jnp.concatenate([tall] * (n // 128), axis=1)


def band_forward(weight, kernel, feats, count):
    ch = weight.shape[1]
    w = weight.astype(BF).T.reshape(ch, kernel, kernel, feats)
    parts = [
        jnp.pad(w, ((0, 0), (0, 0), (j, count - 1 - j), (0, 0))) for j in range(count)
    ]
    return jnp.stack(parts).reshape(count * ch, kernel * (kernel + count - 1) * feats)


def band_square(weight, feats):
    ch = weight.shape[1]
    w = weight.astype(BF).T.reshape(ch, 2, 2, feats)
    parts = [
        jnp.pad(w, ((0, 0), (dy, 1 - dy), (dx, 1 - dx), (0, 0)))
        for dy in range(2)
        for dx in range(2)
    ]
    return jnp.stack(parts).reshape(4 * ch, 9 * feats)


def band_back(weight, kernel, feats, count):
    ch = weight.shape[1]
    w = weight.astype(BF).reshape(kernel, kernel, feats, ch)[::-1, ::-1].transpose(2, 0, 1, 3)
    parts = [
        jnp.pad(w, ((0, 0), (0, 0), (i, count - 1 - i), (0, 0))) for i in range(count)
    ]
    return jnp.stack(parts).reshape(count * feats, kernel * (kernel + count - 1) * ch)


def advantage_kernel(lengths_ref, dones_ref, rewards_ref, values_ref, adv_ref, stat_ref):
    n = rewards_ref.shape[1]
    length = lengths_ref[0]
    position = lax.broadcasted_iota(jnp.int32, (8, n), 1)
    live = position < length
    mask = jnp.where(live, 1.0, 0.0)
    next_live = jnp.where(position + 1 < length, 1.0, 0.0)
    values = jnp.broadcast_to(values_ref[...], (8, n))
    rewards = jnp.broadcast_to(rewards_ref[...], (8, n))
    going = 1.0 - jnp.broadcast_to(dones_ref[...], (8, n)).astype(F32)

    def ahead(v, k, fill):
        return jnp.concatenate([v[:, k:], jnp.full((8, k), fill, F32)], axis=1)

    delta = rewards + GAMMA * going * ahead(values, 1, 0.0) * next_live - values
    total = mask * delta
    carry = mask * (GAMMA * LAMBDA) * going
    k = 1
    while k < n:
        total = total + carry * ahead(total, k, 0.0)
        carry = carry * ahead(carry, k, 0.0)
        k *= 2
    adv_ref[...] = total[0:1]
    count = jnp.sum(mask, axis=1, keepdims=True)
    mean = jnp.sum(mask * total, axis=1, keepdims=True) / count
    spread = jnp.sum(mask * (total - mean) ** 2, axis=1, keepdims=True)
    lane = lax.broadcasted_iota(jnp.int32, (8, 128), 1)
    stat = jnp.where(lane == 0, count, jnp.where(lane == 1, mean, jnp.where(lane == 2, spread, 0.0)))
    stat_ref[...] = stat[0:1]


def advantages(lengths, dones, rewards, old_values):
    n = rewards.shape[1]
    vmem = pl.BlockSpec(memory_space=pltpu.VMEM)
    return pl.pallas_call(
        advantage_kernel,
        out_shape=(jax.ShapeDtypeStruct((1, n), F32), jax.ShapeDtypeStruct((1, 128), F32)),
        in_specs=[pl.BlockSpec(memory_space=pltpu.SMEM), vmem, vmem, vmem],
        out_specs=(vmem, vmem),
        name="advantages",
    )(lengths, dones, rewards, old_values)


def join_stats(mine, other):
    n_a, m_a, s_a = mine[0, 0], mine[0, 1], mine[0, 2]
    n_b, m_b, s_b = other[0, 0], other[0, 1], other[0, 2]
    count = n_a + n_b
    mean = (n_a * m_a + n_b * m_b) / count
    gap = m_a - m_b
    spread = (s_a + s_b) + gap * gap * (n_a * n_b) / count
    lane = lax.broadcasted_iota(jnp.int32, mine.shape, 1)
    return jnp.where(lane == 0, count, jnp.where(lane == 1, mean, jnp.where(lane == 2, spread, 0.0)))


def conv_one_kernel(top_ref, bottom_ref, band_ref, bias_ref, act_ref, slope_ref):
    n = act_ref.shape[-1]
    cells = act_ref.shape[1]
    bias = wide(bias_ref[0:32, :], 128, n)
    for col in range(cells):
        span = slice(col * 128, col * 128 + 192)
        patch = jnp.concatenate(
            [top_ref[0, span, :], top_ref[1, span, :], bottom_ref[0, span, :]], axis=0
        )
        act, slope = gelu_both(dot(band_ref[...], patch) + bias)
        act_ref[0, col] = act.astype(BF)
        slope_ref[0, col] = slope.astype(BF)


def conv_one(frames, band, bias):
    grid, _, n = frames.shape
    half = grid // 2
    whole = lambda r: (0, 0)
    row = pl.BlockSpec((1, half, 128, n), lambda r: (r, 0, 0, 0))
    shape = jax.ShapeDtypeStruct((half, half, 128, n), BF)
    return pl.pallas_call(
        conv_one_kernel,
        out_shape=(shape, shape),
        grid=(half,),
        in_specs=[
            pl.BlockSpec((2,) + frames.shape[1:], lambda r: (r, 0, 0)),
            pl.BlockSpec((1,) + frames.shape[1:], lambda r: (2 * r + 2, 0, 0)),
            pl.BlockSpec(band.shape, whole),
            pl.BlockSpec(bias.shape, whole),
        ],
        out_specs=(row, row),
        compiler_params=params(),
        name="conv_one",
    )(frames, frames, band, bias)


def conv_two_three_kernel(
    top_ref, bottom_ref, band_two_ref, band_three_ref, bias_ref,
    act_ref, slope_ref, flat_ref, slope_three_ref, keep_ref,
):
    n = act_ref.shape[-1]
    step = pl.program_id(0)
    bias_two = wide(bias_ref[32:96, :], 192, n)
    for part in range(3):
        span = slice(3 * part, 3 * part + 4)
        patch = jnp.concatenate(
            [top_ref[0, span].reshape(512, n), bottom_ref[0, span].reshape(512, n)], axis=0
        )
        act, slope = gelu_both(dot(band_two_ref[...], patch) + bias_two)
        rows = slice(part * 192, part * 192 + 192)
        act = act.astype(BF)
        act_ref[0, rows, :] = act
        keep_ref[step, rows, :] = act
        slope_ref[0, rows, :] = slope.astype(BF)

    @pl.when(step >= 2)
    def _():
        bias_three = wide(bias_ref[96:160, :], 256, n)
        for first, start in ((0, 0), (1, 3)):
            patch = jnp.concatenate(
                [keep_ref[step - 2 + a, start * 64 : start * 64 + 384, :] for a in range(3)], axis=0
            )
            pre = dot(band_three_ref[first * 64 :, :], patch) + bias_three[first * 64 :]
            act, slope = gelu_both(pre)
            rows = slice((start + first) * 64, (start + 4) * 64)
            flat_ref[rows, :] = act.astype(BF)
            slope_three_ref[rows, :] = slope.astype(BF)


def conv_two_three(act_one, band_two, band_three, bias):
    n = act_one.shape[-1]
    whole = lambda r: (0, 0)
    row = pl.BlockSpec((1, 576, n), lambda r: (r, 0, 0))
    late = pl.BlockSpec((448, n), lambda r: (jnp.maximum(r - 2, 0), 0))
    two = jax.ShapeDtypeStruct((9, 576, n), BF)
    three = jax.ShapeDtypeStruct((3136, n), BF)
    return pl.pallas_call(
        conv_two_three_kernel,
        out_shape=(two, two, three, three),
        grid=(9,),
        in_specs=[
            pl.BlockSpec((1,) + act_one.shape[1:], lambda r: (r, 0, 0, 0)),
            pl.BlockSpec((1,) + act_one.shape[1:], lambda r: (r + 1, 0, 0, 0)),
            pl.BlockSpec(band_two.shape, whole),
            pl.BlockSpec(band_three.shape, whole),
            pl.BlockSpec(bias.shape, whole),
        ],
        out_specs=(row, row, late, late),
        scratch_shapes=[pltpu.VMEM((9, 576, n), BF)],
        compiler_params=params(),
        name="conv_two_three",
    )(act_one, act_one, band_two, band_three, bias)


def head_gradient(heads, actions, adv, values, old_logp, mask, count, centre, var):
    rows, n = heads.shape
    acts = rows - 1
    norm_adv = (adv - centre) * lax.rsqrt(var + 1e-05)
    returns = adv + values
    index = lax.broadcasted_iota(jnp.int32, (rows, n), 0)
    is_logit = index < acts
    top = jnp.max(jnp.where(is_logit, heads, -jnp.inf), axis=0, keepdims=True)
    shifted = heads - top
    grown = jnp.where(is_logit, jnp.exp(jnp.where(is_logit, shifted, 0.0)), 0.0)
    total = jnp.sum(grown, axis=0, keepdims=True)
    logp_all = jnp.where(is_logit, shifted - jnp.log(total), 0.0)
    prob = jnp.where(is_logit, jnp.exp(logp_all), 0.0)
    chosen = jnp.where(index == actions, 1.0, 0.0)
    logp = jnp.sum(logp_all * chosen, axis=0, keepdims=True)
    plogp = jnp.sum(prob * logp_all, axis=0, keepdims=True)
    value = jnp.sum(jnp.where(index == acts, heads, 0.0), axis=0, keepdims=True)
    ratio = jnp.exp(logp - old_logp)
    bent = jnp.tanh((ratio - 1.0) / CLIP)
    soft = 1.0 + CLIP * bent
    plain = ratio * norm_adv
    clipped = soft * norm_adv
    share = jnp.where(plain < clipped, 1.0, jnp.where(plain > clipped, 0.0, 0.5))
    by_ratio = -norm_adv * (share + (1.0 - share) * (1.0 - bent * bent))
    scale = mask / count
    by_logp = by_ratio * ratio
    by_logit = by_logp * (chosen - prob) + ENTROPY_COEF * prob * (logp_all - plogp)
    by_value = VALUE_COEF * (value - returns)
    return jnp.where(is_logit, by_logit, by_value) * scale


def dense_kernel(
    place_ref, lengths_ref, flat_ref, slope_three_ref, pieces_ref, heads_ref, bias_ref,
    actions_ref, adv_ref, values_ref, logp_ref, stat_ref,
    d_three_ref, keep_ref, send_ref, grad_heads_ref, sum_three_ref, sum_dense_ref, sum_heads_ref,
    weight_ref, d_dense_ref,
):
    n = flat_ref.shape[-1]
    n_dp, n_own, rows, cols = pieces_ref.shape
    dp, own = place_ref[0], place_ref[1]
    for i in range(n_dp):
        for j in range(n_own):
            weight_ref[i * rows : (i + 1) * rows, j * cols : (j + 1) * cols] = pieces_ref[
                i ^ dp, j ^ own
            ]
    hid = n_own * cols
    bias_dense = wide(bias_ref[160 : 160 + hid, :], hid, n)
    bias_heads = wide(bias_ref[160 + hid : 160 + hid + 19, :], 19, n)
    pre = dot(weight_ref[...], flat_ref[...], TN) + bias_dense
    hidden, slope = gelu_both(pre)
    hidden = hidden.astype(BF)
    head_weight = heads_ref[...].astype(BF)
    heads = dot(head_weight, hidden) + bias_heads
    position = lax.broadcasted_iota(jnp.int32, (1, n), 1)
    mask = jnp.where(position < lengths_ref[0], 1.0, 0.0)
    count = stat_ref[0:1, 0:1]
    centre = stat_ref[0:1, 1:2]
    var = stat_ref[0:1, 2:3] / count
    d_heads = head_gradient(
        heads, actions_ref[...], adv_ref[...], values_ref[...], logp_ref[...], mask, count, centre, var
    ).astype(BF)
    ones = jnp.ones((8, n), BF)
    grad_heads_ref[...] = dot(d_heads, hidden, NT)
    sum_heads_ref[...] = dot(ones, d_heads, NT)[0:1]
    d_dense = (dot(head_weight, d_heads, TN) * slope).astype(BF)
    sum_dense_ref[...] = dot(ones, d_dense, NT)[0:1]
    for j in range(n_own):
        d_dense_ref[j] = d_dense[j * cols : (j + 1) * cols]
    for k in range(n_own):
        block = dot(flat_ref[...], d_dense_ref[own ^ k], NT).astype(BF)
        if k % 2 == 0:
            keep_ref[k // 2] = block
        else:
            send_ref[k // 2] = block
    total = jnp.zeros((64, n), F32)
    for part in range(7):
        span = slice(part * 448, part * 448 + 448)
        d_three = (dot(weight_ref[span, :], d_dense) * slope_three_ref[span, :].astype(F32)).astype(BF)
        d_three_ref[span, :] = d_three
        back = d_three.astype(F32)
        for c in range(7):
            total = total + back[c * 64 : c * 64 + 64]
    sum_three_ref[...] = dot(jnp.ones((8, n), F32), total, NT, HIGH)[0:1]


def dense(place, lengths, flat, slope_three, pieces, heads, bias, actions, adv, values, logp, stat):
    n = flat.shape[-1]
    n_dp, n_own, rows, cols = pieces.shape
    hid = n_own * cols
    full = n_dp * rows
    vmem = pl.BlockSpec(memory_space=pltpu.VMEM)
    smem = pl.BlockSpec(memory_space=pltpu.SMEM)
    half = jax.ShapeDtypeStruct((n_own // 2, full, cols), BF)
    return pl.pallas_call(
        dense_kernel,
        out_shape=(
            jax.ShapeDtypeStruct((full, n), BF),
            half,
            half,
            jax.ShapeDtypeStruct(heads.shape, F32),
            jax.ShapeDtypeStruct((1, 64), F32),
            jax.ShapeDtypeStruct((1, hid), F32),
            jax.ShapeDtypeStruct((1, heads.shape[0]), F32),
        ),
        in_specs=[smem, smem] + [vmem] * 10,
        out_specs=(vmem,) * 7,
        scratch_shapes=[pltpu.VMEM((full, hid), BF), pltpu.VMEM((n_own, cols, n), BF)],
        compiler_params=params(56),
        name="dense",
    )(place, lengths, flat, slope_three, pieces, heads, bias, actions, adv, values, logp, stat)


def conv_three_back_kernel(
    d_three_ref, act_ref, slope_ref, band_ref, d_two_ref, grad_ref, sum_ref, pad_ref, acc_ref, tot_ref
):
    n = act_ref.shape[-1]
    step = pl.program_id(0)

    @pl.when(step == 0)
    def _():
        pad_ref[...] = jnp.zeros_like(pad_ref)
        acc_ref[...] = jnp.zeros_like(acc_ref)
        tot_ref[...] = jnp.zeros_like(tot_ref)
        for r in range(7):
            pad_ref[r + 2, 128 : 128 + 448, :] = d_three_ref[r * 448 : r * 448 + 448, :]

    total = tot_ref[...]
    for part in range(3):
        patch = jnp.concatenate(
            [pad_ref[step + a, part * 192 : part * 192 + 320, :] for a in range(3)], axis=0
        )
        rows = slice(part * 192, part * 192 + 192)
        d_two = (dot(band_ref[...], patch) * slope_ref[0, rows, :].astype(F32)).astype(BF)
        d_two_ref[0, rows, :] = d_two
        back = d_two.astype(F32)
        total = total + (back[0:64] + back[64:128]) + back[128:192]
    tot_ref[...] = total

    @pl.when(step < 7)
    def _():
        row = pad_ref[step + 2, 128 : 128 + 448, :]
        second = jnp.concatenate([jnp.zeros((64, n), BF), row[256:448]], axis=0)
        for d_rows, start in ((row[0:256], 0), (second, 3)):
            cells = jnp.concatenate(
                [act_ref[step + a, start * 64 : start * 64 + 384, :] for a in range(3)], axis=0
            )
            acc_ref[...] += dot(d_rows, cells, NT)

    @pl.when(step == 8)
    def _():
        for a in range(3):
            out = None
            for c in range(4):
                piece = acc_ref[c * 64 : c * 64 + 64, a * 384 + c * 64 : a * 384 + c * 64 + 192]
                out = piece if out is None else out + piece
            grad_ref[:, a * 192 : a * 192 + 192] = out
        sum_ref[...] = dot(jnp.ones((8, n), F32), tot_ref[...], NT, HIGH)[0:1]


def conv_three_back(d_three, act_two, slope_two, band):
    n = act_two.shape[-1]
    whole = lambda r: (0, 0)
    row = pl.BlockSpec((1, 576, n), lambda r: (r, 0, 0))
    return pl.pallas_call(
        conv_three_back_kernel,
        out_shape=(
            jax.ShapeDtypeStruct(act_two.shape, BF),
            jax.ShapeDtypeStruct((64, 576), F32),
            jax.ShapeDtypeStruct((1, 64), F32),
        ),
        grid=(9,),
        in_specs=[
            pl.BlockSpec(d_three.shape, whole),
            pl.BlockSpec(act_two.shape, lambda r: (0, 0, 0)),
            row,
            pl.BlockSpec(band.shape, whole),
        ],
        out_specs=(row, pl.BlockSpec((64, 576), whole), pl.BlockSpec((1, 64), whole)),
        scratch_shapes=[
            pltpu.VMEM((11, 704, n), BF),
            pltpu.VMEM((256, 1152), F32),
            pltpu.VMEM((64, n), F32),
        ],
        compiler_params=params(),
        name="conv_three_back",
    )(d_three, act_two, slope_two, band)


def conv_two_back_kernel(
    d_two_ref, top_ref, bottom_ref, slope_ref, band_ref, d_one_ref, grad_ref, sum_ref,
    pad_ref, acc_ref, tot_ref,
):
    n = d_one_ref.shape[-1]
    step = pl.program_id(0)

    @pl.when(step == 0)
    def _():
        pad_ref[...] = jnp.zeros_like(pad_ref)
        acc_ref[...] = jnp.zeros_like(acc_ref)
        tot_ref[...] = jnp.zeros_like(tot_ref)
        for r in range(9):
            pad_ref[r + 1, 64 : 64 + 576, :] = d_two_ref[r]

    total = tot_ref[...]
    for col in range(10):
        patch = jnp.concatenate(
            [pad_ref[step + a, col * 64 : col * 64 + 128, :] for a in range(2)], axis=0
        )
        d_one = (dot(band_ref[...], patch) * slope_ref[0, col].astype(F32)).astype(BF)
        d_one_ref[0, col] = d_one
        total = total + d_one.astype(F32)
    tot_ref[...] = total

    @pl.when(step < 9)
    def _():
        for part in range(3):
            span = slice(3 * part, 3 * part + 4)
            cells = jnp.concatenate(
                [top_ref[0, span].reshape(512, n), bottom_ref[0, span].reshape(512, n)], axis=0
            )
            rows = pad_ref[step + 1, 64 + part * 192 : 64 + part * 192 + 192, :]
            acc_ref[...] += dot(rows, cells, NT)

    @pl.when(step == 9)
    def _():
        for a in range(2):
            out = None
            for c in range(3):
                piece = acc_ref[c * 64 : c * 64 + 64, a * 512 + c * 128 : a * 512 + c * 128 + 256]
                out = piece if out is None else out + piece
            grad_ref[:, a * 256 : a * 256 + 256] = out
        sums = dot(jnp.ones((8, n), F32), tot_ref[...], NT, HIGH)[0:1]
        sum_ref[...] = (sums[:, 0:32] + sums[:, 32:64]) + (sums[:, 64:96] + sums[:, 96:128])


def conv_two_back(d_two, act_one, slope_one, band):
    n = act_one.shape[-1]
    half = act_one.shape[0]
    whole = lambda r: (0, 0)
    row = pl.BlockSpec((1,) + act_one.shape[1:], lambda r: (r, 0, 0, 0))
    return pl.pallas_call(
        conv_two_back_kernel,
        out_shape=(
            jax.ShapeDtypeStruct(act_one.shape, BF),
            jax.ShapeDtypeStruct((64, 512), F32),
            jax.ShapeDtypeStruct((1, 32), F32),
        ),
        grid=(half,),
        in_specs=[
            pl.BlockSpec(d_two.shape, lambda r: (0, 0, 0)),
            row,
            pl.BlockSpec((1,) + act_one.shape[1:], lambda r: (jnp.minimum(r + 1, half - 1), 0, 0, 0)),
            row,
            pl.BlockSpec(band.shape, whole),
        ],
        out_specs=(row, pl.BlockSpec((64, 512), whole), pl.BlockSpec((1, 32), whole)),
        scratch_shapes=[
            pltpu.VMEM((11, 704, n), BF),
            pltpu.VMEM((192, 1024), F32),
            pltpu.VMEM((128, n), F32),
        ],
        compiler_params=params(),
        name="conv_two_back",
    )(d_two, act_one, act_one, slope_one, band)


def conv_one_grad_kernel(top_ref, bottom_ref, d_one_ref, grad_ref, acc_ref):
    n = d_one_ref.shape[-1]
    step = pl.program_id(0)

    @pl.when(step == 0)
    def _():
        acc_ref[...] = jnp.zeros_like(acc_ref)

    for pair in range(d_one_ref.shape[1] // 2):
        span = slice(pair * 256, pair * 256 + 320)
        cells = jnp.concatenate(
            [top_ref[0, span, :], top_ref[1, span, :], bottom_ref[0, span, :]], axis=0
        )
        rows = d_one_ref[0, 2 * pair : 2 * pair + 2].reshape(256, n)
        acc_ref[...] += dot(rows, cells, NT)

    @pl.when(step == pl.num_programs(0) - 1)
    def _():
        for a in range(2):
            out = None
            for k in range(2):
                for dy in range(2):
                    for dx in range(2):
                        row = ((k * 2 + dy) * 2 + dx) * 32
                        lane = (dy + a) * 320 + (2 * k + dx) * 64
                        piece = acc_ref[row : row + 32, lane : lane + 128]
                        out = piece if out is None else out + piece
            grad_ref[:, a * 128 : a * 128 + 128] = out


def conv_one_grad(frames, d_one):
    n = frames.shape[-1]
    half = d_one.shape[0]
    return pl.pallas_call(
        conv_one_grad_kernel,
        out_shape=jax.ShapeDtypeStruct((32, 256), F32),
        grid=(half,),
        in_specs=[
            pl.BlockSpec((2,) + frames.shape[1:], lambda r: (r, 0, 0)),
            pl.BlockSpec((1,) + frames.shape[1:], lambda r: (2 * r + 2, 0, 0)),
            pl.BlockSpec((1,) + d_one.shape[1:], lambda r: (r, 0, 0, 0)),
        ],
        out_specs=pl.BlockSpec((32, 256), lambda r: (0, 0)),
        scratch_shapes=[pltpu.VMEM((256, 960), F32)],
        compiler_params=params(),
        name="conv_one_grad",
    )(frames, frames, d_one)


def frames_back_kernel(above_ref, here_ref, band_ref, out_ref):
    n = out_ref.shape[-1]
    step = pl.program_id(0)
    last = pl.num_programs(0) - 1
    cells = here_ref.shape[1]
    zero = jnp.zeros((32, n), BF)

    def slab(ref, dy, first, alive):
        parts = []
        for c in range(first, first + 4):
            if c < 0 or c >= 2 * cells:
                parts.append(zero)
            else:
                start = (dy * 2 + c % 2) * 32
                parts.append(ref[0, c // 2, start : start + 32, :])
        whole = jnp.concatenate(parts, axis=0)
        return whole if alive is None else jnp.where(alive, whole, jnp.zeros_like(whole))

    for block in range(7):
        first = 3 * block - 1
        up = slab(above_ref, 1, first, step > 0)
        mid = slab(here_ref, 0, first, step < last)
        rows = slice(block * 192, block * 192 + 192)
        out_ref[0, rows, :] = dot(band_ref[...], jnp.concatenate([up, mid], axis=0)).astype(BF)

    @pl.when(step < last)
    def _():
        for block in range(7):
            first = 3 * block - 1
            mid = slab(here_ref, 0, first, None)
            low = slab(here_ref, 1, first, None)
            rows = slice(block * 192, block * 192 + 192)
            out_ref[1, rows, :] = dot(band_ref[...], jnp.concatenate([mid, low], axis=0)).astype(BF)


def frames_back(d_one, band, shape):
    half = d_one.shape[0]
    block = (1,) + d_one.shape[1:]
    return pl.pallas_call(
        frames_back_kernel,
        out_shape=jax.ShapeDtypeStruct(shape, BF),
        grid=(half + 1,),
        in_specs=[
            pl.BlockSpec(block, lambda r: (jnp.maximum(r - 1, 0), 0, 0, 0)),
            pl.BlockSpec(block, lambda r: (jnp.minimum(r, half - 1), 0, 0, 0)),
            pl.BlockSpec(band.shape, lambda r: (0, 0)),
        ],
        out_specs=pl.BlockSpec((2,) + shape[1:], lambda r: (r, 0, 0)),
        compiler_params=params(),
        name="frames_back",
    )(d_one, d_one, band)


def adam_terms(grad, mean, square):
    momentum = BETA * mean + (1.0 - BETA) * grad
    variance = BETA * square + (1.0 - BETA) * grad * grad
    fix = 1.0 - BETA**STEP
    direction = momentum / fix / (jnp.sqrt(variance / fix) + EPSILON)
    return (momentum, variance, direction)


def turned_step(weight, grad, mean, square, left, right):
    rate = RATE / math.sqrt(weight.shape[1])
    turned = dot(dot(right, grad, TN, HIGH), left, NN, HIGH)
    momentum, variance, direction = adam_terms(turned, mean, square)
    back = dot(dot(right, direction, NN, HIGH), left, NT, HIGH)
    return momentum, variance, weight - rate * back


def step_kernel(*refs):
    ins, outs = refs[:6], refs[6:]
    results = turned_step(*[ref[...] for ref in ins])
    for ref, value in zip(outs, results):
        ref[...] = value


def rotated_step(weight, grad, mean, square, left, right):
    vmem = pl.BlockSpec(memory_space=pltpu.VMEM)
    shape = jax.ShapeDtypeStruct(grad.shape, F32)
    return pl.pallas_call(
        step_kernel,
        out_shape=(shape,) * 3,
        in_specs=[vmem] * 6,
        out_specs=(vmem,) * 3,
        compiler_params=params(),
        name="rotated_step",
    )(weight.T, grad, mean.T, square.T, left, right)


def dense_step_kernel(weight_ref, grad_ref, mean_ref, square_ref, block_ref, mom_ref, var_ref, new_ref, *, rate):
    turned = dot(grad_ref[...], block_ref[0], NN, HIGH)
    momentum, variance, direction = adam_terms(turned, mean_ref[...], square_ref[...])
    mom_ref[...] = momentum
    var_ref[...] = variance
    new_ref[...] = weight_ref[...] - rate * dot(direction, block_ref[0], NT, HIGH)


def dense_step(weight, grad, mean, square, block, rate):
    vmem = pl.BlockSpec(memory_space=pltpu.VMEM)
    shape = jax.ShapeDtypeStruct(grad.shape, F32)
    return pl.pallas_call(
        functools.partial(dense_step_kernel, rate=rate),
        out_shape=(shape,) * 3,
        in_specs=[vmem] * 5,
        out_specs=(vmem,) * 3,
        compiler_params=params(),
        name="dense_step",
    )(weight, grad, mean, square, block)


def swap(x, axis, bit, size):
    return lax.ppermute(x, axis, [(i, i ^ bit) for i in range(size)])


def bits_of(size):
    return [1 << b for b in range(size.bit_length() - 1)]


def gather_pieces(piece, n_dp, n_own):
    pieces = piece[None, None]
    for bit in bits_of(n_dp):
        pieces = jnp.concatenate([pieces, swap(pieces, "dp", bit, n_dp)], axis=0)
    for bit in bits_of(n_own):
        pieces = jnp.concatenate([pieces, swap(pieces, "own", bit, n_own)], axis=1)
    return pieces


def sum_everywhere(x, n_dp, n_own):
    for bit in bits_of(n_own):
        x = x + swap(x, "own", bit, n_own)
    for bit in bits_of(n_dp):
        x = x + swap(x, "dp", bit, n_dp)
    return x


def add_low(a, b):
    return (a.astype(F32) + b.astype(F32)).astype(BF)


def scatter_sum(keep, send, n_dp, n_own):
    own, dp = lax.axis_index("own"), lax.axis_index("dp")
    block = add_low(keep, swap(send, "own", 1, n_own))
    size = n_own // 2
    bit = n_own // 2
    while size > 1:
        size //= 2
        block = add_low(block[:size], swap(block[size:], "own", bit, n_own))
        bit //= 2
    block = block[0]
    rows = block.shape[0] // n_dp
    blocks = block.reshape((2,) * len(bits_of(n_dp)) + (rows, block.shape[1]))
    for bit in bits_of(n_dp):
        axis = blocks.ndim - 3
        mine = (dp // bit) % 2
        kept = lax.dynamic_index_in_dim(blocks, mine, axis, keepdims=False)
        gone = lax.dynamic_index_in_dim(blocks, 1 - mine, axis, keepdims=False)
        came = swap(gone, "dp", bit, n_dp)
        if blocks.ndim > 3:
            blocks = add_low(kept, came)
        else:
            blocks = kept.astype(F32) + came.astype(F32)
    return blocks


def shards(
    frames, actions, dones, lengths, rewards, old_values, old_logp,
    conv_first, conv_second, conv_third, dense_hidden, dense_heads, bias_all,
    mean_first, mean_second, mean_third, mean_dense, mean_heads, mean_bias,
    square_first, square_second, square_third, square_dense, square_heads, square_bias,
    left_first, right_first, left_second, right_second, left_third, right_third,
    right_dense, left_heads, right_heads, *, n_dp, n_own,
):
    tokens, grid = frames.shape[0], frames.shape[1]
    planes = frames.shape[3]
    place = jnp.stack([lax.axis_index("dp"), lax.axis_index("own")]).astype(jnp.int32)
    pieces = gather_pieces(dense_hidden.astype(BF), n_dp, n_own)
    adv, stat = advantages(lengths, dones, rewards, old_values)
    for bit in bits_of(n_own):
        stat = join_stats(stat, swap(stat, "own", bit, n_own))
    for bit in bits_of(n_dp):
        stat = join_stats(stat, swap(stat, "dp", bit, n_dp))
    bias = jnp.broadcast_to(bias_all[:, None], (bias_all.shape[0], 128))
    cells = frames.transpose(1, 2, 3, 0).reshape(grid, grid * planes, tokens)
    act_one, slope_one = conv_one(cells, band_square(conv_first, planes), bias)
    act_two, slope_two, flat, slope_three = conv_two_three(
        act_one, band_forward(conv_second, 2, 128, 3), band_forward(conv_third, 3, 64, 4), bias
    )
    d_three, keep, send, here_heads, sum_three, sum_dense, sum_heads = dense(
        place, lengths, flat, slope_three, pieces, dense_heads.T, bias,
        actions, adv, old_values, old_logp, stat,
    )
    grad_dense = scatter_sum(keep, send, n_dp, n_own)
    d_two, here_third, sum_two = conv_three_back(d_three, act_two, slope_two, band_back(conv_third, 3, 64, 3))
    d_one, here_second, sum_one = conv_two_back(d_two, act_one, slope_one, band_back(conv_second, 2, 128, 1))
    here_first = conv_one_grad(cells, d_one)
    frames_grad = frames_back(d_one, band_back(conv_first, 2, planes, 3), cells.shape)
    frames_grad = frames_grad.reshape(grid, grid, planes, tokens).transpose(3, 0, 1, 2)
    here_bias = jnp.concatenate([sum_one, sum_two, sum_three, sum_dense, sum_heads], axis=1)
    here = (here_first, here_second, here_third, here_heads, here_bias)
    packed = jnp.concatenate([h.reshape(-1) for h in here])
    packed = sum_everywhere(packed, n_dp, n_own)
    grads = []
    start = 0
    for h in here:
        grads.append(packed[start : start + h.size].reshape(h.shape))
        start += h.size
    grad_first, grad_second, grad_third, grad_heads, grad_bias = grads
    one = rotated_step(conv_first, grad_first, mean_first, square_first, left_first, right_first)
    two = rotated_step(conv_second, grad_second, mean_second, square_second, left_second, right_second)
    three = rotated_step(conv_third, grad_third, mean_third, square_third, left_third, right_third)
    top = rotated_step(dense_heads, grad_heads, mean_heads, square_heads, left_heads, right_heads)
    flat_rows = dense_hidden.shape[0] * n_dp
    wide_step = dense_step(
        dense_hidden, grad_dense, mean_dense, square_dense, right_dense, RATE / math.sqrt(flat_rows)
    )
    grad_bias = grad_bias.reshape(-1)
    mom_bias, var_bias, bias_dir = adam_terms(grad_bias, mean_bias, square_bias)
    new_bias = bias_all - BIAS_RATE * bias_dir
    outs = [frames_grad, grad_first.T, grad_second.T, grad_third.T, grad_dense, grad_heads.T, grad_bias]
    for index, bias_part in enumerate((mom_bias, var_bias, new_bias)):
        outs += [one[index].T, two[index].T, three[index].T, wide_step[index], top[index].T, bias_part]
    return tuple(outs)


def solution(mesh):
    n_dp, n_own = mesh.shape["dp"], mesh.shape["own"]
    both = ("dp", "own")
    rep = P()
    in_specs = (
        (P(both, None, None, None), P(both, None), P(both, None), P(both))
        + (P(both, None),) * 3
        + (rep, rep, rep, P("dp", "own"), rep, rep) * 3
        + (rep,) * 6
        + (P("own", None, None), rep, rep)
    )
    out_specs = (P(both, None, None, None),) + (rep, rep, rep, P("dp", "own"), rep, rep) * 4
    body = functools.partial(shards, n_dp=n_dp, n_own=n_own)
    return jax.shard_map(body, mesh=mesh, in_specs=in_specs, out_specs=out_specs, check_vma=False)
```

```python
import functools
import math

import jax
import jax.numpy as jnp
from jax import lax
from jax.experimental import pallas as pl
from jax.experimental.pallas import tpu as pltpu
from jax.sharding import PartitionSpec as P

STEP = 10
GAMMA = 0.99
LAMBDA = 0.95
CLIP = 0.1
ENTROPY_COEF = 0.01
VALUE_COEF = 0.5
BETA = 0.5
EPSILON = 1e-08
RATE = 1.0
BIAS_RATE = 0.1
HIGH = lax.Precision.HIGHEST
ROOT = math.sqrt(2.0 / math.pi)
CUBE = 0.044715
BF = jnp.bfloat16
F32 = jnp.float32
MIB = 2**20

NN = (((1,), (0,)), ((), ()))
NT = (((1,), (1,)), ((), ()))
TN = (((0,), (0,)), ((), ()))


def dot(a, b, dims=NN, precision=None):
    return lax.dot_general(a, b, dims, precision=precision, preferred_element_type=F32)


def params(limit=16, **more):
    return pltpu.CompilerParams(vmem_limit_bytes=limit * MIB, **more)


def cost(us):
    return pl.CostEstimate(flops=int(us * 1e9), bytes_accessed=0, transcendentals=0)


def near(shape, dtype):
    return pltpu.VMEM(shape, dtype)


def held(x):
    return pltpu.with_memory_space_constraint(x, pltpu.VMEM)


def far(x):
    return pltpu.with_memory_space_constraint(x, pltpu.HBM)


def vmem():
    return pl.BlockSpec(memory_space=pltpu.VMEM)


def smem():
    return pl.BlockSpec(memory_space=pltpu.SMEM)


def anywhere():
    return pl.BlockSpec(memory_space=pl.ANY)


def start_rows(source, target, sems):
    for r in range(source.shape[0]):
        pltpu.make_async_copy(source.at[r], target.at[r], sems.at[r]).start()


def start_row(source, target, sems, r):
    pltpu.make_async_copy(source.at[r], target.at[r], sems.at[r]).start()


def wait_row(source, target, sems, r):
    pltpu.make_async_copy(source.at[r], target.at[r], sems.at[r]).wait()


def wait_rows(source, target, sems):
    for r in range(source.shape[0]):
        wait_row(source, target, sems, r)


def dma(count):
    return pltpu.SemaphoreType.DMA((count,))


def gelu_both(x):
    x2 = x * x
    t = jnp.tanh(x * (ROOT + (ROOT * CUBE) * x2))
    h = 0.5 * x
    act = h + h * t
    slope = (0.5 + 0.5 * t) + h * (1.0 - t * t) * (ROOT + (3.0 * ROOT * CUBE) * x2)
    return act, slope


def wide(column, rows, n):
    k = column.shape[0]
    tall = jnp.concatenate([column] * (rows // k), axis=0) if rows > k else column
    return jnp.concatenate([tall] * (n // 128), axis=1)


def lanes(parts):
    return jnp.concatenate([p for p in parts if p.shape[1] > 0], axis=1)


def band_forward(w, kernel, feats, count):
    ch = w.shape[0]
    run = kernel * feats
    rows = []
    for j in range(count):
        parts = []
        for a in range(kernel):
            parts.append(jnp.zeros((ch, j * feats), F32))
            parts.append(w[:, a * run : (a + 1) * run])
            parts.append(jnp.zeros((ch, (count - 1 - j) * feats), F32))
        rows.append(lanes(parts))
    return jnp.concatenate(rows, axis=0).astype(BF)


def band_square(w, feats):
    ch = w.shape[0]
    rows = []
    for dy in range(2):
        for dx in range(2):
            lead = (dy * 3 + dx) * feats
            rows.append(
                lanes(
                    [
                        jnp.zeros((ch, lead), F32),
                        w[:, : 2 * feats],
                        jnp.zeros((ch, feats), F32),
                        w[:, 2 * feats :],
                        jnp.zeros((ch, 4 * feats - lead), F32),
                    ]
                )
            )
    return jnp.concatenate(rows, axis=0).astype(BF)


def band_back(w, kernel, feats, count):
    ch = w.shape[0]
    turned = w.T
    zero = jnp.zeros((feats, ch), F32)
    rows = []
    for i in range(count):
        parts = []
        for a in range(kernel):
            for j in range(kernel + count - 1):
                b = j - i
                if 0 <= b < kernel:
                    spot = ((kernel - 1 - a) * kernel + (kernel - 1 - b)) * feats
                    parts.append(turned[spot : spot + feats])
                else:
                    parts.append(zero)
        rows.append(lanes(parts))
    return jnp.concatenate(rows, axis=0).astype(BF)


def first_kernel(
    lengths_ref, dones_ref, rewards_ref, values_ref, weight_ref, bias_ref, adv_ref, piece_ref, bias_out_ref
):
    n = rewards_ref.shape[1]
    length = lengths_ref[0]
    position = lax.broadcasted_iota(jnp.int32, (8, n), 1)
    live = position < length
    mask = jnp.where(live, 1.0, 0.0)
    next_live = jnp.where(position + 1 < length, 1.0, 0.0)
    values = jnp.broadcast_to(values_ref[...], (8, n))
    rewards = jnp.broadcast_to(rewards_ref[...], (8, n))
    going = 1.0 - jnp.broadcast_to(dones_ref[...], (8, n)).astype(F32)

    def ahead(v, k, fill):
        return jnp.concatenate([v[:, k:], jnp.full((8, k), fill, F32)], axis=1)

    delta = rewards + GAMMA * going * ahead(values, 1, 0.0) * next_live - values
    total = mask * delta
    carry = mask * (GAMMA * LAMBDA) * going
    k = 1
    while k < n:
        total = total + carry * ahead(total, k, 0.0)
        carry = carry * ahead(carry, k, 0.0)
        k *= 2
    adv_ref[...] = total[0:1]
    count = jnp.sum(mask, axis=1, keepdims=True)
    mean = jnp.sum(mask * total, axis=1, keepdims=True) / count
    spread = jnp.sum(mask * (total - mean) ** 2, axis=1, keepdims=True)
    lane = lax.broadcasted_iota(jnp.int32, (8, 128), 1)
    stat = jnp.where(lane == 0, count, jnp.where(lane == 1, mean, jnp.where(lane == 2, spread, 0.0)))
    top = stat.astype(BF).astype(F32)
    mid = (stat - top).astype(BF).astype(F32)
    low = ((stat - top) - mid).astype(BF).astype(F32)
    line = lax.broadcasted_iota(jnp.int32, (8, 128), 0)
    terms = jnp.where(line == 0, top, jnp.where(line == 1, mid, jnp.where(line == 2, low, 0.0)))
    rows = weight_ref.shape[0]
    tail = piece_ref.shape[0] - 16
    piece_ref[...] = jnp.zeros_like(piece_ref)
    piece_ref[0:rows, :] = weight_ref[...].astype(BF)
    piece_ref[tail:, :] = jnp.concatenate([terms, jnp.zeros((8, 128), F32)], axis=0).astype(BF)
    size = bias_ref.shape[1]
    padded = bias_out_ref.shape[0]
    line = jnp.concatenate([bias_ref[...], jnp.zeros((1, padded - size), F32)], axis=1)
    bias_out_ref[...] = jnp.broadcast_to(line, (128, padded)).T


def first(lengths, dones, rewards, old_values, weight, bias):
    n = rewards.shape[1]
    rows = -(-weight.shape[0] // 16) * 16 + 16
    return pl.pallas_call(
        first_kernel,
        out_shape=(
            jax.ShapeDtypeStruct((1, n), F32),
            jax.ShapeDtypeStruct((rows, 128), BF),
            jax.ShapeDtypeStruct((-(-bias.shape[1] // 128) * 128, 128), F32),
        ),
        in_specs=[smem()] + [vmem()] * 5,
        out_specs=(vmem(),) * 3,
        cost_estimate=cost(3),
        name="first",
    )(lengths, dones, rewards, old_values, weight, bias)


def conv_one_kernel(
    frames_ref, weight_ref, bias_ref, act_ref, act_far_ref, slope_far_ref,
    band_ref, cells_ref, slope_ref, in_sems, act_sems, slope_sems,
):
    n = act_ref.shape[-1]
    half = act_ref.shape[0]
    step = pl.program_id(0)

    @pl.when(step == 0)
    def _():
        start_rows(frames_ref, cells_ref, in_sems)
        band_ref[...] = band_square(weight_ref[...], 64)
        wait_row(frames_ref, cells_ref, in_sems, 0)

    wait_row(frames_ref, cells_ref, in_sems, 2 * step + 1)
    wait_row(frames_ref, cells_ref, in_sems, 2 * step + 2)
    bias = wide(bias_ref[0:32, :], 128, n)
    for col in range(half):
        span = slice(col * 128, col * 128 + 192)
        patch = jnp.concatenate([cells_ref[2 * step + a, span, :] for a in range(3)], axis=0)
        act, slope = gelu_both(dot(band_ref[...], patch) + bias)
        act_ref[step, col] = act.astype(BF)
        slope_ref[step, col] = slope.astype(BF)
    start_row(act_ref, act_far_ref, act_sems, step)
    start_row(slope_ref, slope_far_ref, slope_sems, step)

    @pl.when(step == half - 1)
    def _():
        wait_rows(act_ref, act_far_ref, act_sems)
        wait_rows(slope_ref, slope_far_ref, slope_sems)


def conv_one(frames, weight, bias):
    grid, _, n = frames.shape
    half = grid // 2
    shape = (half, half, 128, n)
    return pl.pallas_call(
        conv_one_kernel,
        out_shape=(near(shape, BF), pltpu.HBM(shape, BF), pltpu.HBM(shape, BF)),
        grid=(half,),
        in_specs=[anywhere(), vmem(), vmem()],
        out_specs=(vmem(), anywhere(), anywhere()),
        scratch_shapes=[
            pltpu.VMEM((128, 576), BF),
            pltpu.VMEM(frames.shape, BF),
            pltpu.VMEM(shape, BF),
            dma(grid),
            dma(half),
            dma(half),
        ],
        compiler_params=params(36),
        cost_estimate=cost(12),
        name="conv_one",
    )(far(frames), weight, bias)


def conv_two_kernel(
    one_ref, weight_ref, bias_ref, act_ref, act_far_ref, slope_far_ref,
    band_ref, slope_ref, act_sems, slope_sems,
):
    n = act_ref.shape[-1]
    step = pl.program_id(0)

    @pl.when(step == 0)
    def _():
        band_ref[...] = band_forward(weight_ref[...], 2, 128, 3)

    bias = wide(bias_ref[32:96, :], 192, n)
    for part in range(3):
        span = slice(3 * part, 3 * part + 4)
        patch = jnp.concatenate(
            [one_ref[step + a, span].reshape(512, n) for a in range(2)], axis=0
        )
        act, slope = gelu_both(dot(band_ref[...], patch) + bias)
        rows = slice(part * 192, part * 192 + 192)
        act_ref[step, rows, :] = act.astype(BF)
        slope_ref[step, rows, :] = slope.astype(BF)
    start_row(act_ref, act_far_ref, act_sems, step)
    start_row(slope_ref, slope_far_ref, slope_sems, step)

    @pl.when(step == 8)
    def _():
        wait_rows(act_ref, act_far_ref, act_sems)
        wait_rows(slope_ref, slope_far_ref, slope_sems)


def conv_two(act_one, weight, bias):
    n = act_one.shape[-1]
    shape = (9, 576, n)
    return pl.pallas_call(
        conv_two_kernel,
        out_shape=(near(shape, BF), pltpu.HBM(shape, BF), pltpu.HBM(shape, BF)),
        grid=(9,),
        in_specs=[vmem()] * 3,
        out_specs=(vmem(), anywhere(), anywhere()),
        scratch_shapes=[pltpu.VMEM((192, 1024), BF), pltpu.VMEM(shape, BF), dma(9), dma(9)],
        compiler_params=params(24),
        cost_estimate=cost(7),
        name="conv_two",
    )(held(act_one), weight, bias)


def conv_three_kernel(two_ref, weight_ref, bias_ref, flat_ref, slope_ref, band_ref):
    n = flat_ref.shape[-1]
    step = pl.program_id(0)

    @pl.when(step == 0)
    def _():
        band_ref[...] = band_forward(weight_ref[...], 3, 64, 4)

    bias = wide(bias_ref[96:160, :], 256, n)
    for drop, start in ((0, 0), (1, 3)):
        patch = jnp.concatenate(
            [two_ref[step + a, start * 64 : start * 64 + 384, :] for a in range(3)], axis=0
        )
        pre = dot(band_ref[drop * 64 :, :], patch) + bias[drop * 64 :]
        act, slope = gelu_both(pre)
        rows = pl.ds(pl.multiple_of(step * 448, 64) + (start + drop) * 64, 256 - drop * 64)
        flat_ref[rows, :] = act.astype(BF)
        slope_ref[rows, :] = slope.astype(BF)


def conv_three(act_two, weight, bias):
    n = act_two.shape[-1]
    shape = near((3136, n), BF)
    return pl.pallas_call(
        conv_three_kernel,
        out_shape=(shape, shape),
        grid=(7,),
        in_specs=[vmem()] * 3,
        out_specs=(vmem(), vmem()),
        scratch_shapes=[pltpu.VMEM((256, 1152), BF)],
        compiler_params=params(),
        cost_estimate=cost(5),
        name="conv_three",
    )(held(act_two), weight, bias)


def head_gradient(heads, actions, adv, values, old_logp, mask, count, centre, var):
    rows, n = heads.shape
    acts = rows - 1
    norm_adv = (adv - centre) * lax.rsqrt(var + 1e-05)
    returns = adv + values
    index = lax.broadcasted_iota(jnp.int32, (rows, n), 0)
    is_logit = index < acts
    top = jnp.max(jnp.where(is_logit, heads, -jnp.inf), axis=0, keepdims=True)
    shifted = heads - top
    grown = jnp.where(is_logit, jnp.exp(jnp.where(is_logit, shifted, 0.0)), 0.0)
    total = jnp.sum(grown, axis=0, keepdims=True)
    logp_all = jnp.where(is_logit, shifted - jnp.log(total), 0.0)
    prob = jnp.where(is_logit, jnp.exp(logp_all), 0.0)
    chosen = jnp.where(index == actions, 1.0, 0.0)
    logp = jnp.sum(logp_all * chosen, axis=0, keepdims=True)
    plogp = jnp.sum(prob * logp_all, axis=0, keepdims=True)
    value = jnp.sum(jnp.where(index == acts, heads, 0.0), axis=0, keepdims=True)
    ratio = jnp.exp(logp - old_logp)
    bent = jnp.tanh((ratio - 1.0) / CLIP)
    soft = 1.0 + CLIP * bent
    plain = ratio * norm_adv
    clipped = soft * norm_adv
    share = jnp.where(plain < clipped, 1.0, jnp.where(plain > clipped, 0.0, 0.5))
    by_ratio = -norm_adv * (share + (1.0 - share) * (1.0 - bent * bent))
    scale = mask / count
    by_logp = by_ratio * ratio
    by_logit = by_logp * (chosen - prob) + ENTROPY_COEF * prob * (logp_all - plogp)
    by_value = VALUE_COEF * (value - returns)
    return jnp.where(is_logit, by_logit, by_value) * scale


def dense_kernel(*refs, places, n_dp, n_own, rows):
    place_ref, lengths_ref, flat_ref, slope_three_ref, heads_ref, bias_ref = refs[:6]
    actions_ref, adv_ref, values_ref, logp_ref = refs[6:10]
    piece_refs = refs[10 : 10 + len(places)]
    d_three_ref, keep_ref, send_ref, grad_heads_ref, sums_ref, sum_heads_ref = refs[10 + len(places) : -4]
    blocks_ref, weight_ref, d_dense_ref, sems = refs[-4:]
    n = flat_ref.shape[-1]
    cols = 128
    dp, own = place_ref[0], place_ref[1]
    stats = []
    copies = []
    for ref, spots in zip(piece_refs, places):
        for k, (i, j) in enumerate(spots):
            copies.append(
                pltpu.make_async_copy(ref.at[k], blocks_ref.at[i ^ dp, j ^ own], sems.at[len(copies)])
            )
    for copy in copies:
        copy.start()
    for copy in copies:
        copy.wait()
    for i in range(n_dp):
        for j in range(n_own):
            tail = blocks_ref[i, j, blocks_ref.shape[2] - 16 :].astype(F32)
            stats.append((tail[0:1] + tail[1:2]) + tail[2:3])
    stats = jnp.concatenate(stats, axis=0)
    each = stats[:, 0:1]
    count = jnp.sum(each, axis=0, keepdims=True)
    centre = jnp.sum(each * stats[:, 1:2], axis=0, keepdims=True) / count
    gap = stats[:, 1:2] - centre
    var = jnp.sum(stats[:, 2:3] + each * gap * gap, axis=0, keepdims=True) / count
    for i in range(n_dp):
        for j in range(n_own):
            weight_ref[i * rows : (i + 1) * rows, j * cols : (j + 1) * cols] = blocks_ref[i, j, 0:rows]
    hid = n_own * cols
    bias_dense = wide(bias_ref[160 : 160 + hid, :], hid, n)
    bias_heads = wide(bias_ref[160 + hid : 160 + hid + 19, :], 19, n)
    pre = dot(weight_ref[...], flat_ref[...], TN) + bias_dense
    hidden, slope = gelu_both(pre)
    hidden = hidden.astype(BF)
    head_weight = heads_ref[...].astype(BF)
    heads = dot(head_weight, hidden) + bias_heads
    position = lax.broadcasted_iota(jnp.int32, (1, n), 1)
    mask = jnp.where(position < lengths_ref[0], 1.0, 0.0)
    d_heads = head_gradient(
        heads, actions_ref[...], adv_ref[...], values_ref[...], logp_ref[...], mask, count, centre, var
    ).astype(BF)
    ones = jnp.ones((8, n), BF)
    grad_heads_ref[...] = dot(d_heads, hidden, NT)
    sum_heads_ref[...] = dot(ones, d_heads, NT)[0:1]
    d_dense = (dot(head_weight, d_heads, TN) * slope).astype(BF)
    sums_ref[0:1, 128 : 128 + hid] = dot(ones, d_dense, NT)[0:1]
    for j in range(n_own):
        d_dense_ref[j] = d_dense[j * cols : (j + 1) * cols]
    for half, ref in ((0, keep_ref), (1, send_ref)):
        for k in range(n_own // 4):
            both = [d_dense_ref[own ^ (4 * k + half)], d_dense_ref[own ^ (4 * k + 2 + half)]]
            block = dot(flat_ref[...], jnp.concatenate(both, axis=0), NT).astype(BF)
            for i in range(n_dp):
                rel = i ^ dp
                spot = (rel % 2) * (n_dp // 2) + rel // 2
                for m in range(2):
                    ref[2 * k + m, spot] = block[i * rows : (i + 1) * rows, m * cols : (m + 1) * cols]
    total = jnp.zeros((64, n), F32)
    for part in range(7):
        span = slice(part * 448, part * 448 + 448)
        d_three = (dot(weight_ref[span, :], d_dense) * slope_three_ref[span, :].astype(F32)).astype(BF)
        d_three_ref[span, :] = d_three
        back = d_three.astype(F32)
        for c in range(7):
            total = total + back[c * 64 : c * 64 + 64]
    sums_ref[0:1, 0:64] = dot(jnp.ones((8, n), F32), total, NT, HIGH)[0:1]
    sums_ref[0:1, 64:128] = jnp.zeros((1, 64), F32)


def dense(place, lengths, flat, slope_three, heads, bias, actions, adv, values, logp, pieces, n_dp, n_own, rows):
    n = flat.shape[-1]
    hid = n_own * 128
    full = n_dp * rows
    part = jax.ShapeDtypeStruct((n_own // 2, n_dp, rows, 128), BF)
    arrays = [p[0] for p in pieces]
    body = functools.partial(
        dense_kernel, places=[p[1] for p in pieces], n_dp=n_dp, n_own=n_own, rows=rows
    )
    return pl.pallas_call(
        body,
        out_shape=(
            near((full, n), BF),
            part,
            part,
            jax.ShapeDtypeStruct(heads.shape, F32),
            jax.ShapeDtypeStruct((1, 128 + hid), F32),
            jax.ShapeDtypeStruct((1, heads.shape[0]), F32),
        ),
        in_specs=[smem(), smem()] + [vmem()] * 8 + [anywhere()] * len(arrays),
        out_specs=(vmem(),) * 6,
        scratch_shapes=[
            pltpu.VMEM((n_dp, n_own) + arrays[0].shape[1:], BF),
            pltpu.VMEM((full, hid), BF),
            pltpu.VMEM((n_own, 128, n), BF),
            dma(n_dp * n_own),
        ],
        compiler_params=params(32),
        cost_estimate=cost(8),
        name="dense",
    )(place, lengths, held(flat), held(slope_three), heads, bias, actions, adv, values, logp, *arrays)


def conv_three_back_kernel(
    d_three_ref, act_far_ref, slope_far_ref, weight_ref, heads_ref,
    d_two_ref, pack_ref, sum_ref,
    band_ref, pad_ref, acc_ref, tot_ref, act_ref, slope_ref, act_sems, slope_sems,
):
    n = d_three_ref.shape[-1]
    step = pl.program_id(0)

    @pl.when(step == 0)
    def _():
        for r in range(9):
            start_row(slope_far_ref, slope_ref, slope_sems, r)
            start_row(act_far_ref, act_ref, act_sems, r)
        band_ref[...] = band_back(weight_ref[...], 3, 64, 3)
        pad_ref[...] = jnp.zeros_like(pad_ref)
        acc_ref[...] = jnp.zeros_like(acc_ref)
        tot_ref[...] = jnp.zeros_like(tot_ref)
        for r in range(7):
            pad_ref[r + 2, 128 : 128 + 448, :] = d_three_ref[r * 448 : r * 448 + 448, :]
        wait_row(act_far_ref, act_ref, act_sems, 0)
        wait_row(act_far_ref, act_ref, act_sems, 1)

    wait_row(slope_far_ref, slope_ref, slope_sems, step)
    total = tot_ref[...]
    for part in range(3):
        patch = jnp.concatenate(
            [pad_ref[step + a, part * 192 : part * 192 + 320, :] for a in range(3)], axis=0
        )
        rows = slice(part * 192, part * 192 + 192)
        d_two = (dot(band_ref[...], patch) * slope_ref[step, rows, :].astype(F32)).astype(BF)
        d_two_ref[step, rows, :] = d_two
        back = d_two.astype(F32)
        total = total + (back[0:64] + back[64:128]) + back[128:192]
    tot_ref[...] = total

    @pl.when(step < 7)
    def _():
        wait_row(act_far_ref, act_ref, act_sems, step + 2)
        row = pad_ref[step + 2, 128 : 128 + 448, :]
        second = jnp.concatenate([jnp.zeros((64, n), BF), row[256:448]], axis=0)
        for d_rows, start in ((row[0:256], 0), (second, 3)):
            span = slice(start * 64, start * 64 + 384)
            cells = jnp.concatenate([act_ref[step + a, span, :] for a in range(3)], axis=0)
            acc_ref[...] += dot(d_rows, cells, NT)

    @pl.when(step == 8)
    def _():
        for a in range(3):
            out = None
            for c in range(4):
                piece = acc_ref[c * 64 : c * 64 + 64, a * 384 + c * 64 : a * 384 + c * 64 + 192]
                out = piece if out is None else out + piece
            pack_ref[0:64, a * 192 : a * 192 + 192] = out.astype(BF)
        pack_ref[0:64, 576:640] = jnp.zeros((64, 64), BF)
        pack_ref[64:80, 0:512] = heads_ref[0:16, :].astype(BF)
        pack_ref[80:96, 0:512] = jnp.concatenate(
            [heads_ref[16:19, :], jnp.zeros((13, 512), F32)], axis=0
        ).astype(BF)
        pack_ref[64:96, 512:640] = jnp.zeros((32, 128), BF)
        sum_ref[...] = dot(jnp.ones((8, n), F32), tot_ref[...], NT, HIGH)[0:1]


def conv_three_back(d_three, act_two, slope_two, weight, heads):
    n = act_two.shape[-1]
    return pl.pallas_call(
        conv_three_back_kernel,
        out_shape=(
            near(act_two.shape, BF),
            jax.ShapeDtypeStruct((96, 640), BF),
            jax.ShapeDtypeStruct((1, 64), F32),
        ),
        grid=(9,),
        in_specs=[vmem(), anywhere(), anywhere(), vmem(), vmem()],
        out_specs=(vmem(),) * 3,
        scratch_shapes=[
            pltpu.VMEM((192, 960), BF),
            pltpu.VMEM((11, 704, n), BF),
            pltpu.VMEM((256, 1152), F32),
            pltpu.VMEM((64, n), F32),
            pltpu.VMEM(act_two.shape, BF),
            pltpu.VMEM(act_two.shape, BF),
            dma(9),
            dma(9),
        ],
        compiler_params=params(24),
        cost_estimate=cost(9),
        name="conv_three_back",
    )(held(d_three), act_two, slope_two, weight, heads)


def conv_two_back_kernel(
    d_two_ref, act_far_ref, slope_far_ref, weight_ref, d_one_ref, d_far_ref, grad_ref, sum_ref,
    band_ref, pad_ref, acc_ref, tot_ref, act_ref, slope_ref, act_sems, slope_sems, out_sems,
):
    n = d_one_ref.shape[-1]
    step = pl.program_id(0)

    @pl.when(step == 0)
    def _():
        for r in range(10):
            start_row(slope_far_ref, slope_ref, slope_sems, r)
            start_row(act_far_ref, act_ref, act_sems, r)
        band_ref[...] = band_back(weight_ref[...], 2, 128, 1)
        pad_ref[...] = jnp.zeros_like(pad_ref)
        acc_ref[...] = jnp.zeros_like(acc_ref)
        tot_ref[...] = jnp.zeros_like(tot_ref)
        for r in range(9):
            pad_ref[r + 1, 64 : 64 + 576, :] = d_two_ref[r]
        wait_row(act_far_ref, act_ref, act_sems, 0)

    wait_row(slope_far_ref, slope_ref, slope_sems, step)
    total = tot_ref[...]
    for col in range(10):
        patch = jnp.concatenate(
            [pad_ref[step + a, col * 64 : col * 64 + 128, :] for a in range(2)], axis=0
        )
        d_one = (dot(band_ref[...], patch) * slope_ref[step, col].astype(F32)).astype(BF)
        d_one_ref[step, col] = d_one
        total = total + d_one.astype(F32)
    tot_ref[...] = total
    start_row(d_one_ref, d_far_ref, out_sems, step)

    @pl.when(step < 9)
    def _():
        wait_row(act_far_ref, act_ref, act_sems, step + 1)
        for part in range(3):
            span = slice(3 * part, 3 * part + 4)
            cells = jnp.concatenate(
                [act_ref[step + a, span].reshape(512, n) for a in range(2)], axis=0
            )
            rows = pad_ref[step + 1, 64 + part * 192 : 64 + part * 192 + 192, :]
            acc_ref[...] += dot(rows, cells, NT)

    @pl.when(step == 9)
    def _():
        wait_rows(d_one_ref, d_far_ref, out_sems)
        for a in range(2):
            out = None
            for c in range(3):
                piece = acc_ref[c * 64 : c * 64 + 64, a * 512 + c * 128 : a * 512 + c * 128 + 256]
                out = piece if out is None else out + piece
            grad_ref[:, a * 256 : a * 256 + 256] = out.astype(BF)
        sums = dot(jnp.ones((8, n), F32), tot_ref[...], NT, HIGH)[0:1]
        sum_ref[...] = (sums[:, 0:32] + sums[:, 32:64]) + (sums[:, 64:96] + sums[:, 96:128])


def conv_two_back(d_two, act_one, slope_one, weight):
    n = act_one.shape[-1]
    shape = act_one.shape
    return pl.pallas_call(
        conv_two_back_kernel,
        out_shape=(
            near(shape, BF),
            pltpu.HBM(shape, BF),
            jax.ShapeDtypeStruct((64, 512), BF),
            jax.ShapeDtypeStruct((1, 32), F32),
        ),
        grid=(10,),
        in_specs=[vmem(), anywhere(), anywhere(), vmem()],
        out_specs=(vmem(), anywhere(), vmem(), vmem()),
        scratch_shapes=[
            pltpu.VMEM((128, 256), BF),
            pltpu.VMEM((11, 704, n), BF),
            pltpu.VMEM((192, 1024), F32),
            pltpu.VMEM((128, n), F32),
            pltpu.VMEM(shape, BF),
            pltpu.VMEM(shape, BF),
            dma(10),
            dma(10),
            dma(10),
        ],
        compiler_params=params(32),
        cost_estimate=cost(11),
        name="conv_two_back",
    )(held(d_two), act_one, slope_one, weight)


def conv_one_grad_kernel(
    frames_ref, d_one_ref, dense_ref, heads_ref, one_ref, two_ref, grad_ref, acc_ref, cells_ref, sems
):
    n = d_one_ref.shape[-1]
    step = pl.program_id(0)

    @pl.when(step == 0)
    def _():
        start_rows(frames_ref, cells_ref, sems)
        acc_ref[...] = jnp.zeros_like(acc_ref)
        wait_row(frames_ref, cells_ref, sems, 0)

    wait_row(frames_ref, cells_ref, sems, 2 * step + 1)
    wait_row(frames_ref, cells_ref, sems, 2 * step + 2)
    for pair in range(d_one_ref.shape[1] // 2):
        span = slice(pair * 256, pair * 256 + 320)
        cells = jnp.concatenate([cells_ref[2 * step + a, span, :] for a in range(3)], axis=0)
        rows = d_one_ref[step, 2 * pair : 2 * pair + 2].reshape(256, n)
        acc_ref[...] += dot(rows, cells, NT)

    @pl.when(step == pl.num_programs(0) - 1)
    def _():
        for a in range(2):
            out = None
            for k in range(2):
                for dy in range(2):
                    for dx in range(2):
                        row = ((k * 2 + dy) * 2 + dx) * 32
                        lane = (dy + a) * 320 + (2 * k + dx) * 64
                        piece = acc_ref[row : row + 32, lane : lane + 128]
                        out = piece if out is None else out + piece
            grad_ref[0:32, a * 128 : a * 128 + 128] = out
        grad_ref[32:40, :] = jnp.zeros((8, 256), F32)
        grad_ref[32:33, :] = dense_ref[0:1, 128:384]
        grad_ref[33:34, :] = dense_ref[0:1, 384:640]
        grad_ref[34:35, 0:64] = dense_ref[0:1, 0:64]
        grad_ref[35:36, 0:64] = two_ref[...]
        grad_ref[36:37, 0:32] = one_ref[...]
        grad_ref[37:38, 0:19] = heads_ref[...]


def conv_one_grad(frames, d_one, sums, sum_heads, sum_one, sum_two):
    return pl.pallas_call(
        conv_one_grad_kernel,
        out_shape=jax.ShapeDtypeStruct((40, 256), F32),
        grid=(d_one.shape[0],),
        in_specs=[anywhere()] + [vmem()] * 5,
        out_specs=vmem(),
        scratch_shapes=[
            pltpu.VMEM((256, 960), F32),
            pltpu.VMEM(frames.shape, BF),
            dma(frames.shape[0]),
        ],
        compiler_params=params(24),
        cost_estimate=cost(10),
        name="conv_one_grad",
    )(far(frames), held(d_one), sums, sum_heads, sum_one, sum_two)


def frames_back_kernel(*refs, begin, end, total):
    d_one_ref, weight_ref = refs[:2]
    out_ref, band_ref, here_ref, rows_ref, in_sems, out_sems = refs[-6:]
    n = rows_ref.shape[-1]
    step = pl.program_id(0)
    cells = here_ref.shape[1]
    zero = jnp.zeros((32, n), BF)
    lead = begin - 1
    kept = range(max(lead, 0), min(end, total - 1))

    def fetch(r):
        return pltpu.make_async_copy(d_one_ref.at[r], here_ref.at[r - lead], in_sems.at[r - lead])

    @pl.when(step == 0)
    def _():
        for r in kept:
            fetch(r).start()
        band_ref[...] = band_back(weight_ref[...], 2, 64, 3)
        if begin == 0:
            here_ref[0] = jnp.zeros_like(here_ref[0])
        else:
            fetch(lead).wait()
        if end == total:
            here_ref[end - 1 - lead] = jnp.zeros_like(here_ref[0])

    @pl.when(step + begin < total - 1)
    def _():
        fetch(step + begin).wait()

    def slab(at, dy, first):
        parts = []
        for c in range(first, first + 4):
            if c < 0 or c >= 2 * cells:
                parts.append(zero)
            else:
                spot = (dy * 2 + c % 2) * 32
                parts.append(here_ref[at, c // 2, spot : spot + 32, :])
        return jnp.concatenate(parts, axis=0)

    def row(up, low, at):
        for block in range(7):
            first = 3 * block - 1
            patch = jnp.concatenate([slab(*up, first), slab(*low, first)], axis=0)
            rows_ref[at, block * 192 : block * 192 + 192, :] = dot(band_ref[...], patch).astype(BF)

    def send(at):
        return pltpu.make_async_copy(rows_ref.at[at], out_ref.at[at + 2 * begin], out_sems.at[at])

    row((step, 1), (step + 1, 0), 2 * step)
    send(2 * step).start()

    @pl.when(step + begin < total - 1)
    def _():
        row((step + 1, 0), (step + 1, 1), 2 * step + 1)
        send(2 * step + 1).start()

    @pl.when(step == end - begin - 1)
    def _():
        for at in range(min(2 * end, 2 * total - 1) - 2 * begin):
            send(at).wait()


def frames_back(d_one, weight, shape, begin, end, so_far=None):
    total = d_one.shape[0] + 1
    old = [] if so_far is None else [so_far]
    count = end - begin
    return pl.pallas_call(
        functools.partial(frames_back_kernel, begin=begin, end=end, total=total),
        out_shape=pltpu.HBM(shape, BF),
        grid=(count,),
        in_specs=[anywhere(), vmem()] + [anywhere()] * len(old),
        out_specs=anywhere(),
        scratch_shapes=[
            pltpu.VMEM((192, 256), BF),
            pltpu.VMEM((count + 1,) + d_one.shape[1:], BF),
            pltpu.VMEM((2 * count,) + shape[1:], BF),
            dma(count + 1),
            dma(2 * count),
        ],
        input_output_aliases={2: 0} if old else {},
        compiler_params=params(24),
        cost_estimate=cost(count),
        name="frames_back",
    )(far(d_one), weight, *old)


def adam_terms(grad, mean, square):
    momentum = BETA * mean + (1.0 - BETA) * grad
    variance = BETA * square + (1.0 - BETA) * grad * grad
    fix = 1.0 - BETA**STEP
    direction = momentum / fix / (jnp.sqrt(variance / fix) + EPSILON)
    return (momentum, variance, direction)


def split(x):
    top = x.astype(BF)
    return top, (x - top.astype(F32)).astype(BF)


def dot3(a, b, dims=NN):
    a_top, a_low = split(a)
    b_top, b_low = split(b)
    return dot(a_top, b_top, dims) + (dot(a_top, b_low, dims) + dot(a_low, b_top, dims))


def turned_step(weight, grad, mean, square, left, right):
    rate = RATE / math.sqrt(weight.shape[1])
    turned = dot3(dot3(right, grad, TN), left)
    momentum, variance, direction = adam_terms(turned, mean, square)
    back = dot3(dot3(right, direction), left, NT)
    return momentum, variance, weight - rate * back


def steps_kernel(*refs, spots):
    count = len(spots)
    packs = 1 + max(spot[0] for spot in spots)
    ins, outs = refs[packs : packs + 5 * count], refs[packs + 5 * count :]
    for w, (pack, row, rows, cols) in enumerate(spots):
        grad = refs[pack][row : row + rows, 0:cols]
        weight, mean, square, left, right = [ref[...] for ref in ins[5 * w : 5 * w + 5]]
        results = (grad,) + turned_step(weight, grad, mean, square, left, right)
        for ref, value in zip(outs[4 * w : 4 * w + 4], results):
            ref[...] = value


def steps(packs, spots, groups):
    arrays = []
    shapes = []
    for weight, mean, square, left, right in groups:
        arrays += [weight.T, mean.T, square.T, left, right]
        shapes += [jax.ShapeDtypeStruct(weight.shape[::-1], F32)] * 4
    return pl.pallas_call(
        functools.partial(steps_kernel, spots=spots),
        out_shape=tuple(shapes),
        in_specs=[vmem()] * (len(packs) + len(arrays)),
        out_specs=(vmem(),) * len(shapes),
        compiler_params=params(24),
        cost_estimate=cost(5),
        name="steps",
    )(*packs, *arrays)


def dense_step_kernel(*refs, rate):
    weight_ref, mean_ref, square_ref, block_ref = refs[:4]
    grad_ref, mom_ref, var_ref, new_ref = refs[-4:]
    grad = None
    for ref in refs[4:-4]:
        part = ref[...].astype(F32)
        grad = part if grad is None else grad + part
    grad_ref[...] = grad
    turned = dot3(grad, block_ref[0])
    momentum, variance, direction = adam_terms(turned, mean_ref[...], square_ref[...])
    mom_ref[...] = momentum
    var_ref[...] = variance
    new_ref[...] = weight_ref[...] - rate * dot3(direction, block_ref[0], NT)


def dense_step(weight, mean, square, block, parts, rate):
    shape = jax.ShapeDtypeStruct(weight.shape, F32)
    return pl.pallas_call(
        functools.partial(dense_step_kernel, rate=rate),
        out_shape=(shape,) * 4,
        in_specs=[vmem()] * (4 + len(parts)),
        out_specs=(vmem(),) * 4,
        compiler_params=params(),
        cost_estimate=cost(3),
        name="dense_step",
    )(weight, mean, square, block, *parts)


def swap(x, axis, bit, size):
    return lax.ppermute(x, axis, [(i, i ^ bit) for i in range(size)])


def bits_of(size):
    return [1 << b for b in range(size.bit_length() - 1)]


def after(x, *others):
    return lax.optimization_barrier((x,) + others)[0]


def stage(x, axis, bits, size):
    if len(bits) == 1:
        return [swap(x, axis, bits[0], size)]
    one, two = bits
    return [swap(x, axis, bit, size) for bit in (one, two, one | two)]


def stage_sum(x, came):
    up = [v.astype(F32) for v in [x] + came]
    if len(up) == 2:
        return up[0] + up[1]
    return (up[0] + up[1]) + (up[2] + up[3])


def sum_stages(n_dp, n_own):
    bits = bits_of(n_dp)
    plan = [("own", tuple(bits_of(n_own)), n_own)]
    if len(bits) % 2:
        plan += [("dp", tuple(bits[k : k + 2]), n_dp) for k in range(1, len(bits), 2)]
        plan.append(("dp", (bits[0],), n_dp))
    else:
        plan += [("dp", tuple(bits[k : k + 2]), n_dp) for k in range(0, len(bits), 2)]
    return plan


def add_low(*terms):
    total = terms[0].astype(F32)
    for term in terms[1:]:
        total = total + term.astype(F32)
    return total.astype(BF)


def plain_gather(piece, n_dp, n_own):
    pieces = piece[None]
    spots = [(0, 0)]
    for bit in bits_of(n_dp):
        pieces = jnp.concatenate([pieces, swap(pieces, "dp", bit, n_dp)], axis=0)
        spots = spots + [(i ^ bit, j) for i, j in spots]
    for bit in bits_of(n_own):
        pieces = jnp.concatenate([pieces, swap(pieces, "own", bit, n_own)], axis=0)
        spots = spots + [(i, j ^ bit) for i, j in spots]
    return [(pieces, spots)]


def plain_scatter(keep, send, n_dp, n_own):
    block = add_low(keep, swap(send, "own", 1, n_own))
    bit = n_own // 2
    while bit > 1:
        half = block.shape[0] // 2
        block = add_low(block[:half], swap(block[half:], "own", bit, n_own))
        bit //= 2
    block = block[0]
    for bit in [1] + bits_of(n_dp)[:0:-1]:
        half = block.shape[0] // 2
        block = add_low(block[:half], swap(block[half:], "dp", bit, n_dp))
    return [block[0]]


def shards(
    frames, actions, dones, lengths, rewards, old_values, old_logp,
    conv_first, conv_second, conv_third, dense_hidden, dense_heads, bias_all,
    mean_first, mean_second, mean_third, mean_dense, mean_heads, mean_bias,
    square_first, square_second, square_third, square_dense, square_heads, square_bias,
    left_first, right_first, left_second, right_second, left_third, right_third,
    right_dense, left_heads, right_heads, *, n_dp, n_own,
):
    tokens, grid = frames.shape[0], frames.shape[1]
    planes = frames.shape[3]
    rows = dense_hidden.shape[0]
    tuned = (n_dp, n_own) == (8, 4)
    own_swap = lambda x, bit: swap(x, "own", bit, n_own)
    dp_swap = lambda x, bit: swap(x, "dp", bit, n_dp)
    place = jnp.stack([lax.axis_index("dp"), lax.axis_index("own")]).astype(jnp.int32)
    bias_row = bias_all.reshape(1, -1)
    adv, piece, bias = first(lengths, dones, rewards, old_values, dense_hidden, bias_row)
    cells = frames.transpose(1, 2, 3, 0).reshape(grid, grid * planes, tokens)

    if tuned:
        along_z = [dp_swap(piece, 2 * k) for k in (1, 2, 3)]
    act_one, act_one_far, slope_one = conv_one(cells, conv_first.T, bias)
    if tuned:
        z_spots = [[(0, 0), (2, 0)], [(4, 0), (6, 0)]]
        piece = after(piece, act_one_far)
        z_parts = [jnp.stack([piece, along_z[0]]), jnp.stack([along_z[1], along_z[2]])]
        act_one = after(act_one, *z_parts)
        x_parts = [dp_swap(z, 1) for z in z_parts]
        y_parts = [own_swap(z, 2) for z in z_parts]
        pieces = list(zip(z_parts, z_spots))
        pieces += [(own_swap(z, 1), [(i, j ^ 1) for i, j in sp]) for z, sp in pieces]
    else:
        pieces = plain_gather(piece, n_dp, n_own)
    act_two, act_two_far, slope_two = conv_two(act_one, conv_second.T, bias)
    if tuned:
        act_two, *arrived = lax.optimization_barrier((act_two, *x_parts, *y_parts))
        x_parts, y_parts = arrived[:2], arrived[2:]
        corner = [own_swap(x_parts[0], 2), dp_swap(y_parts[1], 1)]
        for parts, flip in ((x_parts, (1, 0)), (y_parts, (0, 2))):
            for part, spots in zip(parts, z_spots):
                spots = [(i ^ flip[0], j ^ flip[1]) for i, j in spots]
                pieces.append((part, spots))
                pieces.append((own_swap(part, 1), [(i, j ^ 1) for i, j in spots]))
    flat, slope_three = conv_three(act_two, conv_third.T, bias)
    if tuned:
        flat, *corner = lax.optimization_barrier((flat, *corner))
        for part, spots in zip(corner, z_spots):
            spots = [(i ^ 1, j ^ 2) for i, j in spots]
            pieces.append((part, spots))
            pieces.append((own_swap(part, 1), [(i, j ^ 1) for i, j in spots]))
    d_three, keep, send, here_heads, sums, sum_heads = dense(
        place, lengths, flat, slope_three, dense_heads.T, bias,
        actions, adv, old_values, old_logp, pieces, n_dp, n_own, rows,
    )

    plan = sum_stages(n_dp, n_own)

    def send_on(x, at, low):
        axis, bits, size = plan[at]
        x = x.astype(BF) if low else x
        return x, stage(x, axis, bits, size)

    def gather_up(state, other):
        x, came = state
        x, other = lax.optimization_barrier((x, other))
        return stage_sum(x, came)

    if tuned:
        came = own_swap(send, 1)
    d_two, pack_three, sum_two = conv_three_back(d_three, act_two_far, slope_two, conv_third.T, here_heads)
    if tuned:
        block = add_low(after(keep, d_two), came)
        by_y, by_x = own_swap(block[1, 4:6], 2), dp_swap(block[1, 6:8], 1)
        d_two = after(d_two, block)
    three = send_on(pack_three, 0, True)
    d_one, d_one_far, pack_two, sum_one = conv_two_back(d_two, act_one_far, slope_one, conv_second.T)
    if tuned:
        block = after(block, d_one)
        side_x = jnp.concatenate([add_low(block[0, 4:6], by_y), block[0, 6:8]])
        side_y = jnp.concatenate([block[1, 0:2], add_low(block[1, 2:4], by_x)])
        by_x, by_y = dp_swap(side_x, 1), own_swap(side_y, 2)
        d_one = after(d_one, side_x, side_y)
    three = send_on(gather_up(three, d_one_far), 1, True)
    d_one = after(d_one, three[0])
    two = send_on(pack_two, 0, True)
    pack_one = conv_one_grad(cells, d_one, sums, sum_heads, sum_one, sum_two)
    if tuned:
        column = add_low(after(block[0, 0:4], pack_one), by_x, by_y)
        parts = [column[0]] + [dp_swap(column[k], 2 * k) for k in (1, 2, 3)]
        d_one_far = after(d_one_far, column)
    else:
        parts = plain_scatter(keep, send, n_dp, n_own)
    three = send_on(gather_up(three, pack_one), 2, True)
    two = send_on(gather_up(two, pack_one), 1, True)
    one = send_on(pack_one, 0, False)
    d_one_far = after(d_one_far, three[0], two[0], one[0])
    shape = cells.shape
    back = frames_back(d_one_far, conv_first.T, shape, 0, 4)
    two = send_on(gather_up(two, back), 2, True)
    one = send_on(gather_up(one, back), 1, False)
    d_one_far = after(d_one_far, two[0], one[0])
    back = frames_back(d_one_far, conv_first.T, shape, 4, 8, back)
    one = send_on(gather_up(one, back), 2, False)
    d_one_far = after(d_one_far, one[0])
    back = frames_back(d_one_far, conv_first.T, shape, 8, grid // 2 + 1, back)

    def finish(state, low):
        for at in range(3, len(plan)):
            state = send_on(gather_up(state, back), at, low)
        return gather_up(state, back)

    frames_grad = back.reshape(grid, grid, planes, tokens).transpose(3, 0, 1, 2)
    grad_dense, *wide_step = dense_step(
        dense_hidden, mean_dense, square_dense, right_dense, parts, RATE / math.sqrt(rows * n_dp)
    )
    late = steps(
        [finish(three, True), finish(two, True)],
        [(0, 0, 64, 576), (0, 64, 19, 512), (1, 0, 64, 512)],
        [
            (conv_third, mean_third, square_third, left_third, right_third),
            (dense_heads, mean_heads, square_heads, left_heads, right_heads),
            (conv_second, mean_second, square_second, left_second, right_second),
        ],
    )
    third, top, second = late[0:4], late[4:8], late[8:12]
    pack_one = finish(one, False)
    first_step = steps(
        [pack_one], [(0, 0, 32, 256)], [(conv_first, mean_first, square_first, left_first, right_first)]
    )
    grad_bias = jnp.concatenate(
        [pack_one[36, 0:32], pack_one[35, 0:64], pack_one[34, 0:64], pack_one[32], pack_one[33], pack_one[37, 0:19]]
    )
    mom_bias, var_bias, bias_dir = adam_terms(grad_bias, mean_bias, square_bias)
    new_bias = bias_all - BIAS_RATE * bias_dir
    outs = [frames_grad]
    wide_step = [grad_dense] + list(wide_step)
    for index, bias_part in enumerate((grad_bias, mom_bias, var_bias, new_bias)):
        outs += [first_step[index].T, second[index].T, third[index].T, wide_step[index], top[index].T, bias_part]
    return tuple(outs)


def solution(mesh):
    n_dp, n_own = mesh.shape["dp"], mesh.shape["own"]
    both = ("dp", "own")
    rep = P()
    in_specs = (
        (P(both, None, None, None), P(both, None), P(both, None), P(both))
        + (P(both, None),) * 3
        + (rep, rep, rep, P("dp", "own"), rep, rep) * 3
        + (rep,) * 6
        + (P("own", None, None), rep, rep)
    )
    out_specs = (P(both, None, None, None),) + (rep, rep, rep, P("dp", "own"), rep, rep) * 4
    body = functools.partial(shards, n_dp=n_dp, n_own=n_own)
    return jax.shard_map(body, mesh=mesh, in_specs=in_specs, out_specs=out_specs, check_vma=False)
```

```python
import functools
import math

import jax
import jax.numpy as jnp
from jax import lax
from jax.experimental import pallas as pl
from jax.experimental.pallas import tpu as pltpu
from jax.sharding import PartitionSpec as P

STEP = 10
GAMMA = 0.99
LAMBDA = 0.95
CLIP = 0.1
ENTROPY_COEF = 0.01
VALUE_COEF = 0.5
BETA = 0.5
EPSILON = 1e-08
RATE = 1.0
BIAS_RATE = 0.1
HIGH = lax.Precision.HIGHEST
ROOT = math.sqrt(2.0 / math.pi)
CUBE = 0.044715
BF = jnp.bfloat16
F32 = jnp.float32
MIB = 2**20

NN = (((1,), (0,)), ((), ()))
NT = (((1,), (1,)), ((), ()))
TN = (((0,), (0,)), ((), ()))


def dot(a, b, dims=NN, precision=None):
    return lax.dot_general(a, b, dims, precision=precision, preferred_element_type=F32)


def params(limit=16, **more):
    return pltpu.CompilerParams(vmem_limit_bytes=limit * MIB, **more)


def cost(us):
    return pl.CostEstimate(flops=int(us * 1e9), bytes_accessed=0, transcendentals=0)


def near(shape, dtype):
    return pltpu.VMEM(shape, dtype)


def held(x):
    return pltpu.with_memory_space_constraint(x, pltpu.VMEM)


def far(x):
    return pltpu.with_memory_space_constraint(x, pltpu.HBM)


def vmem():
    return pl.BlockSpec(memory_space=pltpu.VMEM)


def smem():
    return pl.BlockSpec(memory_space=pltpu.SMEM)


def anywhere():
    return pl.BlockSpec(memory_space=pl.ANY)


def start_rows(source, target, sems):
    for r in range(source.shape[0]):
        pltpu.make_async_copy(source.at[r], target.at[r], sems.at[r]).start()


def start_row(source, target, sems, r):
    pltpu.make_async_copy(source.at[r], target.at[r], sems.at[r]).start()


def wait_row(source, target, sems, r):
    pltpu.make_async_copy(source.at[r], target.at[r], sems.at[r]).wait()


def wait_rows(source, target, sems):
    for r in range(source.shape[0]):
        wait_row(source, target, sems, r)


def dma(count):
    return pltpu.SemaphoreType.DMA((count,))


def gelu_both(x):
    x2 = x * x
    t = jnp.tanh(x * (ROOT + (ROOT * CUBE) * x2))
    h = 0.5 * x
    act = h + h * t
    slope = (0.5 + 0.5 * t) + h * (1.0 - t * t) * (ROOT + (3.0 * ROOT * CUBE) * x2)
    return act, slope


def wide(line, rows, n):
    k = line.shape[1]
    column = jnp.broadcast_to(line, (128, k)).T
    tall = jnp.concatenate([column] * (rows // k), axis=0) if rows > k else column
    return jnp.concatenate([tall] * (n // 128), axis=1)


def lanes(parts):
    return jnp.concatenate([p for p in parts if p.shape[1] > 0], axis=1)


def band_forward(w, kernel, feats, count):
    ch = w.shape[0]
    run = kernel * feats
    rows = []
    for j in range(count):
        parts = []
        for a in range(kernel):
            parts.append(jnp.zeros((ch, j * feats), F32))
            parts.append(w[:, a * run : (a + 1) * run])
            parts.append(jnp.zeros((ch, (count - 1 - j) * feats), F32))
        rows.append(lanes(parts))
    return jnp.concatenate(rows, axis=0).astype(BF)


def band_square(w, feats):
    ch = w.shape[0]
    rows = []
    for dy in range(2):
        for dx in range(2):
            lead = (dy * 3 + dx) * feats
            rows.append(
                lanes(
                    [
                        jnp.zeros((ch, lead), F32),
                        w[:, : 2 * feats],
                        jnp.zeros((ch, feats), F32),
                        w[:, 2 * feats :],
                        jnp.zeros((ch, 4 * feats - lead), F32),
                    ]
                )
            )
    return jnp.concatenate(rows, axis=0).astype(BF)


def band_back(w, kernel, feats, count):
    ch = w.shape[0]
    turned = w.T
    zero = jnp.zeros((feats, ch), F32)
    rows = []
    for i in range(count):
        parts = []
        for a in range(kernel):
            for j in range(kernel + count - 1):
                b = j - i
                if 0 <= b < kernel:
                    spot = ((kernel - 1 - a) * kernel + (kernel - 1 - b)) * feats
                    parts.append(turned[spot : spot + feats])
                else:
                    parts.append(zero)
        rows.append(lanes(parts))
    return jnp.concatenate(rows, axis=0).astype(BF)


def first_kernel(
    lengths_ref, dones_ref, rewards_ref, values_ref, weight_ref, adv_ref, piece_ref
):
    n = rewards_ref.shape[1]
    length = lengths_ref[0]
    position = lax.broadcasted_iota(jnp.int32, (8, n), 1)
    live = position < length
    mask = jnp.where(live, 1.0, 0.0)
    next_live = jnp.where(position + 1 < length, 1.0, 0.0)
    values = jnp.broadcast_to(values_ref[...], (8, n))
    rewards = jnp.broadcast_to(rewards_ref[...], (8, n))
    going = 1.0 - jnp.broadcast_to(dones_ref[...], (8, n)).astype(F32)

    def ahead(v, k, fill):
        return jnp.concatenate([v[:, k:], jnp.full((8, k), fill, F32)], axis=1)

    delta = rewards + GAMMA * going * ahead(values, 1, 0.0) * next_live - values
    total = mask * delta
    carry = mask * (GAMMA * LAMBDA) * going
    k = 1
    while k < n:
        total = total + carry * ahead(total, k, 0.0)
        carry = carry * ahead(carry, k, 0.0)
        k *= 2
    adv_ref[...] = total[0:1]
    count = jnp.sum(mask, axis=1, keepdims=True)
    mean = jnp.sum(mask * total, axis=1, keepdims=True) / count
    spread = jnp.sum(mask * (total - mean) ** 2, axis=1, keepdims=True)
    lane = lax.broadcasted_iota(jnp.int32, (8, 128), 1)
    stat = jnp.where(lane == 0, count, jnp.where(lane == 1, mean, jnp.where(lane == 2, spread, 0.0)))
    top = stat.astype(BF).astype(F32)
    mid = (stat - top).astype(BF).astype(F32)
    low = ((stat - top) - mid).astype(BF).astype(F32)
    line = lax.broadcasted_iota(jnp.int32, (8, 128), 0)
    terms = jnp.where(line == 0, top, jnp.where(line == 1, mid, jnp.where(line == 2, low, 0.0)))
    rows = weight_ref.shape[0]
    tail = piece_ref.shape[0] - 16
    piece_ref[...] = jnp.zeros_like(piece_ref)
    piece_ref[0:rows, :] = weight_ref[...].astype(BF)
    piece_ref[tail:, :] = jnp.concatenate([terms, jnp.zeros((8, 128), F32)], axis=0).astype(BF)


def first(lengths, dones, rewards, old_values, weight):
    n = rewards.shape[1]
    rows = -(-weight.shape[0] // 16) * 16 + 16
    return pl.pallas_call(
        first_kernel,
        out_shape=(
            jax.ShapeDtypeStruct((1, n), F32),
            jax.ShapeDtypeStruct((rows, 128), BF),
        ),
        in_specs=[smem()] + [vmem()] * 4,
        out_specs=(vmem(),) * 2,
        cost_estimate=cost(3),
        name="first",
    )(lengths, dones, rewards, old_values, weight)


def conv_one_kernel(
    frames_ref, weight_ref, bias_ref, act_ref, slope_far_ref,
    band_ref, wide_ref, cells_ref, slope_ref, in_sems, slope_sems,
):
    n = act_ref.shape[-1]
    half = act_ref.shape[0]
    step = pl.program_id(0)

    @pl.when(step == 0)
    def _():
        start_rows(frames_ref, cells_ref, in_sems)
        band_ref[...] = band_square(weight_ref[...], 64)
        wide_ref[...] = wide(bias_ref[:, 0:32], 128, n)
        wait_row(frames_ref, cells_ref, in_sems, 0)

    wait_row(frames_ref, cells_ref, in_sems, 2 * step + 1)
    wait_row(frames_ref, cells_ref, in_sems, 2 * step + 2)
    for col in range(half):
        span = slice(col * 128, col * 128 + 192)
        patch = jnp.concatenate([cells_ref[2 * step + a, span, :] for a in range(3)], axis=0)
        act, slope = gelu_both(dot(band_ref[...], patch) + wide_ref[...])
        act_ref[step, col] = act.astype(BF)
        slope_ref[step, col] = slope.astype(BF)
    start_row(slope_ref, slope_far_ref, slope_sems, step)

    @pl.when(step == half - 1)
    def _():
        wait_rows(slope_ref, slope_far_ref, slope_sems)


def conv_one(frames, weight, bias):
    grid, _, n = frames.shape
    half = grid // 2
    shape = (half, half, 128, n)
    return pl.pallas_call(
        conv_one_kernel,
        out_shape=(near(shape, BF), pltpu.HBM(shape, BF)),
        grid=(half,),
        in_specs=[anywhere(), vmem(), vmem()],
        out_specs=(vmem(), anywhere()),
        scratch_shapes=[
            pltpu.VMEM((128, 576), BF),
            pltpu.VMEM((128, n), F32),
            pltpu.VMEM(frames.shape, BF),
            pltpu.VMEM(shape, BF),
            dma(grid),
            dma(half),
        ],
        compiler_params=params(30),
        cost_estimate=cost(12),
        name="conv_one",
    )(far(frames), weight, bias)


def conv_two_kernel(
    one_ref, weight_ref, bias_ref, act_ref, slope_ref, one_far_ref, band_ref, wide_ref, sems
):
    n = act_ref.shape[-1]
    step = pl.program_id(0)

    @pl.when(step == 0)
    def _():
        start_rows(one_ref, one_far_ref, sems)
        band_ref[...] = band_forward(weight_ref[...], 2, 128, 3)
        wide_ref[...] = wide(bias_ref[:, 32:96], 192, n)

    for part in range(3):
        span = slice(3 * part, 3 * part + 4)
        patch = jnp.concatenate(
            [one_ref[step + a, span].reshape(512, n) for a in range(2)], axis=0
        )
        act, slope = gelu_both(dot(band_ref[...], patch) + wide_ref[...])
        rows = slice(part * 192, part * 192 + 192)
        act_ref[step, rows, :] = act.astype(BF)
        slope_ref[step, rows, :] = slope.astype(BF)

    @pl.when(step == 8)
    def _():
        wait_rows(one_ref, one_far_ref, sems)


def conv_two(act_one, weight, bias):
    n = act_one.shape[-1]
    shape = (9, 576, n)
    return pl.pallas_call(
        conv_two_kernel,
        out_shape=(near(shape, BF), near(shape, BF), pltpu.HBM(act_one.shape, BF)),
        grid=(9,),
        in_specs=[vmem()] * 3,
        out_specs=(vmem(), vmem(), anywhere()),
        scratch_shapes=[pltpu.VMEM((192, 1024), BF), pltpu.VMEM((192, n), F32), dma(10)],
        compiler_params=params(),
        cost_estimate=cost(7),
        name="conv_two",
    )(held(act_one), weight, bias)


def conv_three_kernel(
    two_ref, slope_two_ref, weight_ref, bias_ref,
    flat_far_ref, slope_far_ref, two_far_ref, slope_two_far_ref,
    band_ref, wide_ref, flat_ref, slope_ref, two_sems, slope_two_sems, flat_sems, slope_sems,
):
    n = two_ref.shape[-1]
    step = pl.program_id(0)

    @pl.when(step == 0)
    def _():
        start_rows(two_ref, two_far_ref, two_sems)
        start_rows(slope_two_ref, slope_two_far_ref, slope_two_sems)
        band_ref[...] = band_forward(weight_ref[...], 3, 64, 4)
        wide_ref[...] = wide(bias_ref[:, 96:160], 256, n)

    for drop, start in ((0, 0), (1, 3)):
        patch = jnp.concatenate(
            [two_ref[step + a, start * 64 : start * 64 + 384, :] for a in range(3)], axis=0
        )
        pre = dot(band_ref[drop * 64 :, :], patch) + wide_ref[drop * 64 :, :]
        act, slope = gelu_both(pre)
        rows = slice((start + drop) * 64, (start + 4) * 64)
        flat_ref[step, rows, :] = act.astype(BF)
        slope_ref[step, rows, :] = slope.astype(BF)
    start_row(flat_ref, flat_far_ref, flat_sems, step)
    start_row(slope_ref, slope_far_ref, slope_sems, step)

    @pl.when(step == 6)
    def _():
        wait_rows(two_ref, two_far_ref, two_sems)
        wait_rows(slope_two_ref, slope_two_far_ref, slope_two_sems)
        wait_rows(flat_ref, flat_far_ref, flat_sems)
        wait_rows(slope_ref, slope_far_ref, slope_sems)


def conv_three(act_two, slope_two, weight, bias):
    n = act_two.shape[-1]
    shape = (7, 448, n)
    out = pltpu.HBM(shape, BF)
    two = pltpu.HBM(act_two.shape, BF)
    return pl.pallas_call(
        conv_three_kernel,
        out_shape=(out, out, two, two),
        grid=(7,),
        in_specs=[vmem()] * 4,
        out_specs=(anywhere(),) * 4,
        scratch_shapes=[
            pltpu.VMEM((256, 1152), BF),
            pltpu.VMEM((256, n), F32),
            pltpu.VMEM(shape, BF),
            pltpu.VMEM(shape, BF),
            dma(9),
            dma(9),
            dma(7),
            dma(7),
        ],
        compiler_params=params(),
        cost_estimate=cost(5),
        name="conv_three",
    )(held(act_two), held(slope_two), weight, bias)


def head_gradient(heads, actions, adv, values, old_logp, mask, count, centre, var):
    rows, n = heads.shape
    acts = rows - 1
    norm_adv = (adv - centre) * lax.rsqrt(var + 1e-05)
    returns = adv + values
    index = lax.broadcasted_iota(jnp.int32, (rows, n), 0)
    is_logit = index < acts
    top = jnp.max(jnp.where(is_logit, heads, -jnp.inf), axis=0, keepdims=True)
    shifted = heads - top
    grown = jnp.where(is_logit, jnp.exp(jnp.where(is_logit, shifted, 0.0)), 0.0)
    total = jnp.sum(grown, axis=0, keepdims=True)
    logp_all = jnp.where(is_logit, shifted - jnp.log(total), 0.0)
    prob = jnp.where(is_logit, jnp.exp(logp_all), 0.0)
    chosen = jnp.where(index == actions, 1.0, 0.0)
    logp = jnp.sum(logp_all * chosen, axis=0, keepdims=True)
    plogp = jnp.sum(prob * logp_all, axis=0, keepdims=True)
    value = jnp.sum(jnp.where(index == acts, heads, 0.0), axis=0, keepdims=True)
    ratio = jnp.exp(logp - old_logp)
    bent = jnp.tanh((ratio - 1.0) / CLIP)
    soft = 1.0 + CLIP * bent
    plain = ratio * norm_adv
    clipped = soft * norm_adv
    share = jnp.where(plain < clipped, 1.0, jnp.where(plain > clipped, 0.0, 0.5))
    by_ratio = -norm_adv * (share + (1.0 - share) * (1.0 - bent * bent))
    scale = mask / count
    by_logp = by_ratio * ratio
    by_logit = by_logp * (chosen - prob) + ENTROPY_COEF * prob * (logp_all - plogp)
    by_value = VALUE_COEF * (value - returns)
    return jnp.where(is_logit, by_logit, by_value) * scale


def dense_kernel(*refs, places, n_dp, n_own, rows):
    place_ref, lengths_ref, flat_far_ref, slope_far_ref, two_far_ref, slope_two_far_ref = refs[:6]
    heads_ref, bias_ref, actions_ref, adv_ref, values_ref, logp_ref = refs[6:12]
    piece_refs = refs[12 : 12 + len(places)]
    (
        d_three_ref, two_ref, slope_two_ref, keep_ref, send_ref, grad_heads_ref, sums_ref, sum_heads_ref,
        blocks_ref, weight_ref, d_dense_ref, flat_rows_ref, slope_ref,
        sems, two_sems, slope_two_sems, flat_sems, slope_sems,
    ) = refs[12 + len(places) :]
    n = flat_rows_ref.shape[-1]
    cols = 128
    dp, own = place_ref[0], place_ref[1]
    stats = []
    copies = []
    for ref, spots in zip(piece_refs, places):
        for k, (i, j) in enumerate(spots):
            copies.append(
                pltpu.make_async_copy(ref.at[k], blocks_ref.at[i ^ dp, j ^ own], sems.at[len(copies)])
            )
    for copy in copies:
        copy.start()
    start_rows(flat_far_ref, flat_rows_ref, flat_sems)
    start_rows(slope_far_ref, slope_ref, slope_sems)
    start_rows(two_far_ref, two_ref, two_sems)
    start_rows(slope_two_far_ref, slope_two_ref, slope_two_sems)
    for copy in copies:
        copy.wait()
    for i in range(n_dp):
        for j in range(n_own):
            tail = blocks_ref[i, j, blocks_ref.shape[2] - 16 :].astype(F32)
            stats.append((tail[0:1] + tail[1:2]) + tail[2:3])
    stats = jnp.concatenate(stats, axis=0)
    each = stats[:, 0:1]
    count = jnp.sum(each, axis=0, keepdims=True)
    centre = jnp.sum(each * stats[:, 1:2], axis=0, keepdims=True) / count
    gap = stats[:, 1:2] - centre
    var = jnp.sum(stats[:, 2:3] + each * gap * gap, axis=0, keepdims=True) / count
    for i in range(n_dp):
        for j in range(n_own):
            weight_ref[i * rows : (i + 1) * rows, j * cols : (j + 1) * cols] = blocks_ref[i, j, 0:rows]
    hid = n_own * cols
    bias_dense = wide(bias_ref[:, 160 : 160 + hid], hid, n)
    bias_heads = wide(bias_ref[:, 160 + hid : 160 + hid + 19], 19, n)
    wait_rows(flat_far_ref, flat_rows_ref, flat_sems)
    flat = flat_rows_ref[...].reshape(n_dp * rows, n)
    pre = dot(weight_ref[...], flat, TN) + bias_dense
    hidden, slope = gelu_both(pre)
    hidden = hidden.astype(BF)
    head_weight = heads_ref[...].astype(BF)
    heads = dot(head_weight, hidden) + bias_heads
    position = lax.broadcasted_iota(jnp.int32, (1, n), 1)
    mask = jnp.where(position < lengths_ref[0], 1.0, 0.0)
    d_heads = head_gradient(
        heads, actions_ref[...], adv_ref[...], values_ref[...], logp_ref[...], mask, count, centre, var
    ).astype(BF)
    ones = jnp.ones((8, n), BF)
    grad_heads_ref[...] = dot(d_heads, hidden, NT)
    sum_heads_ref[...] = dot(ones, d_heads, NT)[0:1]
    d_dense = (dot(head_weight, d_heads, TN) * slope).astype(BF)
    sums_ref[0:1, 128 : 128 + hid] = dot(ones, d_dense, NT)[0:1]
    for j in range(n_own):
        d_dense_ref[j] = d_dense[j * cols : (j + 1) * cols]
    for half, ref in ((0, keep_ref), (1, send_ref)):
        for k in range(n_own // 4):
            both = [d_dense_ref[own ^ (4 * k + half)], d_dense_ref[own ^ (4 * k + 2 + half)]]
            block = dot(flat, jnp.concatenate(both, axis=0), NT).astype(BF)
            for i in range(n_dp):
                rel = i ^ dp
                spot = (rel % 2) * (n_dp // 2) + rel // 2
                for m in range(2):
                    ref[2 * k + m, spot] = block[i * rows : (i + 1) * rows, m * cols : (m + 1) * cols]
    wait_rows(slope_far_ref, slope_ref, slope_sems)
    total = jnp.zeros((64, n), F32)
    for part in range(7):
        span = slice(part * 448, part * 448 + 448)
        d_three = (dot(weight_ref[span, :], d_dense) * slope_ref[part].astype(F32)).astype(BF)
        d_three_ref[part] = d_three
        back = d_three.astype(F32)
        for c in range(7):
            total = total + back[c * 64 : c * 64 + 64]
    sums_ref[0:1, 0:64] = dot(jnp.ones((8, n), F32), total, NT, HIGH)[0:1]
    sums_ref[0:1, 64:128] = jnp.zeros((1, 64), F32)
    wait_rows(two_far_ref, two_ref, two_sems)
    wait_rows(slope_two_far_ref, slope_two_ref, slope_two_sems)


def dense(
    place, lengths, flat, slope_three, act_two, slope_two, heads, bias, actions, adv, values, logp,
    pieces, n_dp, n_own, rows,
):
    n = flat.shape[-1]
    hid = n_own * 128
    part = jax.ShapeDtypeStruct((n_own // 2, n_dp, rows, 128), BF)
    arrays = [p[0] for p in pieces]
    body = functools.partial(
        dense_kernel, places=[p[1] for p in pieces], n_dp=n_dp, n_own=n_own, rows=rows
    )
    return pl.pallas_call(
        body,
        out_shape=(
            near(flat.shape, BF),
            near(act_two.shape, BF),
            near(act_two.shape, BF),
            part,
            part,
            jax.ShapeDtypeStruct(heads.shape, F32),
            jax.ShapeDtypeStruct((1, 128 + hid), F32),
            jax.ShapeDtypeStruct((1, heads.shape[0]), F32),
        ),
        in_specs=[smem(), smem()] + [anywhere()] * 4 + [vmem()] * 6 + [anywhere()] * len(arrays),
        out_specs=(vmem(),) * 8,
        scratch_shapes=[
            pltpu.VMEM((n_dp, n_own) + arrays[0].shape[1:], BF),
            pltpu.VMEM((n_dp * rows, hid), BF),
            pltpu.VMEM((n_own, 128, n), BF),
            pltpu.VMEM(flat.shape, BF),
            pltpu.VMEM(flat.shape, BF),
            dma(n_dp * n_own),
            dma(9),
            dma(9),
            dma(7),
            dma(7),
        ],
        compiler_params=params(32),
        cost_estimate=cost(8),
        name="dense",
    )(
        place, lengths, far(flat), far(slope_three), far(act_two), far(slope_two), heads, bias,
        actions, adv, values, logp, *[far(a) for a in arrays],
    )


def conv_three_back_kernel(
    d_three_ref, act_ref, slope_ref, one_far_ref, slope_one_far_ref, weight_ref, heads_ref,
    d_two_ref, one_ref, slope_one_ref, pack_ref, sum_ref,
    band_ref, pad_ref, acc_ref, tot_ref, one_sems, slope_one_sems,
):
    n = d_three_ref.shape[-1]
    step = pl.program_id(0)

    @pl.when(step == 0)
    def _():
        start_rows(one_far_ref, one_ref, one_sems)
        start_rows(slope_one_far_ref, slope_one_ref, slope_one_sems)
        band_ref[...] = band_back(weight_ref[...], 3, 64, 3)
        pad_ref[...] = jnp.zeros_like(pad_ref)
        acc_ref[...] = jnp.zeros_like(acc_ref)
        tot_ref[...] = jnp.zeros_like(tot_ref)
        for r in range(7):
            pad_ref[r + 2, 128 : 128 + 448, :] = d_three_ref[r]

    total = tot_ref[...]
    for part in range(3):
        patch = jnp.concatenate(
            [pad_ref[step + a, part * 192 : part * 192 + 320, :] for a in range(3)], axis=0
        )
        rows = slice(part * 192, part * 192 + 192)
        d_two = (dot(band_ref[...], patch) * slope_ref[step, rows, :].astype(F32)).astype(BF)
        d_two_ref[step, rows, :] = d_two
        back = d_two.astype(F32)
        total = total + (back[0:64] + back[64:128]) + back[128:192]
    tot_ref[...] = total

    @pl.when(step < 7)
    def _():
        row = pad_ref[step + 2, 128 : 128 + 448, :]
        second = jnp.concatenate([jnp.zeros((64, n), BF), row[256:448]], axis=0)
        for d_rows, start in ((row[0:256], 0), (second, 3)):
            span = slice(start * 64, start * 64 + 384)
            cells = jnp.concatenate([act_ref[step + a, span, :] for a in range(3)], axis=0)
            acc_ref[...] += dot(d_rows, cells, NT)

    @pl.when(step == 8)
    def _():
        wait_rows(one_far_ref, one_ref, one_sems)
        wait_rows(slope_one_far_ref, slope_one_ref, slope_one_sems)
        for a in range(3):
            out = None
            for c in range(4):
                piece = acc_ref[c * 64 : c * 64 + 64, a * 384 + c * 64 : a * 384 + c * 64 + 192]
                out = piece if out is None else out + piece
            pack_ref[0:64, a * 192 : a * 192 + 192] = out.astype(BF)
        pack_ref[0:64, 576:640] = jnp.zeros((64, 64), BF)
        pack_ref[64:80, 0:512] = heads_ref[0:16, :].astype(BF)
        pack_ref[80:96, 0:512] = jnp.concatenate(
            [heads_ref[16:19, :], jnp.zeros((13, 512), F32)], axis=0
        ).astype(BF)
        pack_ref[64:96, 512:640] = jnp.zeros((32, 128), BF)
        sum_ref[...] = dot(jnp.ones((8, n), F32), tot_ref[...], NT, HIGH)[0:1]


def conv_three_back(d_three, act_two, slope_two, act_one, slope_one, weight, heads):
    n = act_two.shape[-1]
    return pl.pallas_call(
        conv_three_back_kernel,
        out_shape=(
            near(act_two.shape, BF),
            near(act_one.shape, BF),
            near(act_one.shape, BF),
            jax.ShapeDtypeStruct((96, 640), BF),
            jax.ShapeDtypeStruct((1, 64), F32),
        ),
        grid=(9,),
        in_specs=[vmem()] * 3 + [anywhere()] * 2 + [vmem()] * 2,
        out_specs=(vmem(),) * 5,
        scratch_shapes=[
            pltpu.VMEM((192, 960), BF),
            pltpu.VMEM((11, 704, n), BF),
            pltpu.VMEM((256, 1152), F32),
            pltpu.VMEM((64, n), F32),
            dma(10),
            dma(10),
        ],
        compiler_params=params(),
        cost_estimate=cost(9),
        name="conv_three_back",
    )(held(d_three), held(act_two), held(slope_two), far(act_one), far(slope_one), weight, heads)


def conv_two_back_kernel(
    d_two_ref, act_ref, slope_ref, weight_ref, pack_ref, d_one_ref, d_far_ref, grad_ref, sum_ref,
    band_ref, pad_ref, acc_ref, tot_ref, out_sems,
):
    n = d_one_ref.shape[-1]
    step = pl.program_id(0)

    @pl.when(step == 0)
    def _():
        band_ref[...] = band_back(weight_ref[...], 2, 128, 1)
        pad_ref[...] = jnp.zeros_like(pad_ref)
        acc_ref[...] = jnp.zeros_like(acc_ref)
        tot_ref[...] = jnp.zeros_like(tot_ref)
        for r in range(9):
            pad_ref[r + 1, 64 : 64 + 576, :] = d_two_ref[r]

    total = tot_ref[...]
    for col in range(10):
        patch = jnp.concatenate(
            [pad_ref[step + a, col * 64 : col * 64 + 128, :] for a in range(2)], axis=0
        )
        d_one = (dot(band_ref[...], patch) * slope_ref[step, col].astype(F32)).astype(BF)
        d_one_ref[step, col] = d_one
        total = total + d_one.astype(F32)
    tot_ref[...] = total
    start_row(d_one_ref, d_far_ref, out_sems, step)

    @pl.when(step < 9)
    def _():
        for part in range(3):
            span = slice(3 * part, 3 * part + 4)
            cells = jnp.concatenate(
                [act_ref[step + a, span].reshape(512, n) for a in range(2)], axis=0
            )
            rows = pad_ref[step + 1, 64 + part * 192 : 64 + part * 192 + 192, :]
            acc_ref[...] += dot(rows, cells, NT)

    @pl.when(step == 9)
    def _():
        wait_rows(d_one_ref, d_far_ref, out_sems)
        for a in range(2):
            out = None
            for c in range(3):
                piece = acc_ref[c * 64 : c * 64 + 64, a * 512 + c * 128 : a * 512 + c * 128 + 256]
                out = piece if out is None else out + piece
            grad_ref[96:160, a * 256 : a * 256 + 256] = out.astype(BF)
        grad_ref[0:96, :] = pack_ref[...]
        grad_ref[96:160, 512:640] = jnp.zeros((64, 128), BF)
        sums = dot(jnp.ones((8, n), F32), tot_ref[...], NT, HIGH)[0:1]
        sum_ref[...] = (sums[:, 0:32] + sums[:, 32:64]) + (sums[:, 64:96] + sums[:, 96:128])


def conv_two_back(d_two, act_one, slope_one, weight, pack):
    n = act_one.shape[-1]
    shape = act_one.shape
    return pl.pallas_call(
        conv_two_back_kernel,
        out_shape=(
            near(shape, BF),
            pltpu.HBM(shape, BF),
            jax.ShapeDtypeStruct((160, 640), BF),
            jax.ShapeDtypeStruct((1, 32), F32),
        ),
        grid=(10,),
        in_specs=[vmem()] * 5,
        out_specs=(vmem(), anywhere(), vmem(), vmem()),
        scratch_shapes=[
            pltpu.VMEM((128, 256), BF),
            pltpu.VMEM((11, 704, n), BF),
            pltpu.VMEM((192, 1024), F32),
            pltpu.VMEM((128, n), F32),
            dma(10),
        ],
        compiler_params=params(),
        cost_estimate=cost(11),
        name="conv_two_back",
    )(held(d_two), held(act_one), held(slope_one), weight, pack)


def conv_one_grad_kernel(
    frames_ref, d_one_ref, dense_ref, heads_ref, one_ref, two_ref, grad_ref, acc_ref, cells_ref, sems
):
    n = d_one_ref.shape[-1]
    step = pl.program_id(0)

    @pl.when(step == 0)
    def _():
        start_rows(frames_ref, cells_ref, sems)
        acc_ref[...] = jnp.zeros_like(acc_ref)
        wait_row(frames_ref, cells_ref, sems, 0)

    wait_row(frames_ref, cells_ref, sems, 2 * step + 1)
    wait_row(frames_ref, cells_ref, sems, 2 * step + 2)
    for pair in range(d_one_ref.shape[1] // 2):
        span = slice(pair * 256, pair * 256 + 320)
        cells = jnp.concatenate([cells_ref[2 * step + a, span, :] for a in range(3)], axis=0)
        rows = d_one_ref[step, 2 * pair : 2 * pair + 2].reshape(256, n)
        acc_ref[...] += dot(rows, cells, NT)

    @pl.when(step == pl.num_programs(0) - 1)
    def _():
        for a in range(2):
            out = None
            for k in range(2):
                for dy in range(2):
                    for dx in range(2):
                        row = ((k * 2 + dy) * 2 + dx) * 32
                        lane = (dy + a) * 320 + (2 * k + dx) * 64
                        piece = acc_ref[row : row + 32, lane : lane + 128]
                        out = piece if out is None else out + piece
            grad_ref[0:32, a * 128 : a * 128 + 128] = out
        grad_ref[32:40, :] = jnp.zeros((8, 256), F32)
        grad_ref[32:33, :] = dense_ref[0:1, 128:384]
        grad_ref[33:34, :] = dense_ref[0:1, 384:640]
        grad_ref[34:35, 0:64] = dense_ref[0:1, 0:64]
        grad_ref[35:36, 0:64] = two_ref[...]
        grad_ref[36:37, 0:32] = one_ref[...]
        grad_ref[37:38, 0:19] = heads_ref[...]


def conv_one_grad(frames, d_one, sums, sum_heads, sum_one, sum_two):
    return pl.pallas_call(
        conv_one_grad_kernel,
        out_shape=jax.ShapeDtypeStruct((40, 256), F32),
        grid=(d_one.shape[0],),
        in_specs=[anywhere()] + [vmem()] * 5,
        out_specs=vmem(),
        scratch_shapes=[
            pltpu.VMEM((256, 960), F32),
            pltpu.VMEM(frames.shape, BF),
            dma(frames.shape[0]),
        ],
        compiler_params=params(24),
        cost_estimate=cost(10),
        name="conv_one_grad",
    )(far(frames), held(d_one), sums, sum_heads, sum_one, sum_two)


def frames_back_kernel(*refs, begin, end, total):
    d_one_ref, weight_ref = refs[:2]
    out_ref, band_ref, here_ref, rows_ref, in_sems, out_sems = refs[-6:]
    n = rows_ref.shape[-1]
    step = pl.program_id(0)
    cells = here_ref.shape[1]
    zero = jnp.zeros((32, n), BF)
    lead = begin - 1
    kept = range(max(lead, 0), min(end, total - 1))

    def fetch(r):
        return pltpu.make_async_copy(d_one_ref.at[r], here_ref.at[r - lead], in_sems.at[r - lead])

    @pl.when(step == 0)
    def _():
        for r in kept:
            fetch(r).start()
        band_ref[...] = band_back(weight_ref[...], 2, 64, 3)
        if begin == 0:
            here_ref[0] = jnp.zeros_like(here_ref[0])
        else:
            fetch(lead).wait()
        if end == total:
            here_ref[end - 1 - lead] = jnp.zeros_like(here_ref[0])

    @pl.when(step + begin < total - 1)
    def _():
        fetch(step + begin).wait()

    def slab(at, dy, first):
        parts = []
        for c in range(first, first + 4):
            if c < 0 or c >= 2 * cells:
                parts.append(zero)
            else:
                spot = (dy * 2 + c % 2) * 32
                parts.append(here_ref[at, c // 2, spot : spot + 32, :])
        return jnp.concatenate(parts, axis=0)

    def row(up, low, at):
        for block in range(7):
            first = 3 * block - 1
            patch = jnp.concatenate([slab(*up, first), slab(*low, first)], axis=0)
            rows_ref[at, block * 192 : block * 192 + 192, :] = dot(band_ref[...], patch).astype(BF)

    def send(at):
        return pltpu.make_async_copy(rows_ref.at[at], out_ref.at[at + 2 * begin], out_sems.at[at])

    row((step, 1), (step + 1, 0), 2 * step)
    send(2 * step).start()

    @pl.when(step + begin < total - 1)
    def _():
        row((step + 1, 0), (step + 1, 1), 2 * step + 1)
        send(2 * step + 1).start()

    @pl.when(step == end - begin - 1)
    def _():
        for at in range(min(2 * end, 2 * total - 1) - 2 * begin):
            send(at).wait()


def frames_back(d_one, weight, shape, begin, end, so_far=None):
    total = d_one.shape[0] + 1
    old = [] if so_far is None else [so_far]
    count = end - begin
    return pl.pallas_call(
        functools.partial(frames_back_kernel, begin=begin, end=end, total=total),
        out_shape=pltpu.HBM(shape, BF),
        grid=(count,),
        in_specs=[anywhere(), vmem()] + [anywhere()] * len(old),
        out_specs=anywhere(),
        scratch_shapes=[
            pltpu.VMEM((192, 256), BF),
            pltpu.VMEM((count + 1,) + d_one.shape[1:], BF),
            pltpu.VMEM((2 * count,) + shape[1:], BF),
            dma(count + 1),
            dma(2 * count),
        ],
        input_output_aliases={2: 0} if old else {},
        compiler_params=params(24),
        cost_estimate=cost(count),
        name="frames_back",
    )(far(d_one), weight, *old)


def adam_terms(grad, mean, square):
    momentum = BETA * mean + (1.0 - BETA) * grad
    variance = BETA * square + (1.0 - BETA) * grad * grad
    fix = 1.0 - BETA**STEP
    direction = momentum / fix / (jnp.sqrt(variance / fix) + EPSILON)
    return (momentum, variance, direction)


def split(x):
    top = x.astype(BF)
    return top, (x - top.astype(F32)).astype(BF)


def dot3(a, b, dims=NN):
    a_top, a_low = split(a)
    b_top, b_low = split(b)
    return dot(a_top, b_top, dims) + (dot(a_top, b_low, dims) + dot(a_low, b_top, dims))


def turned_step(weight, grad, mean, square, left, right):
    rate = RATE / math.sqrt(weight.shape[1])
    turned = dot3(dot3(right, grad, TN), left)
    momentum, variance, direction = adam_terms(turned, mean, square)
    back = dot3(dot3(right, direction), left, NT)
    return momentum, variance, weight - rate * back


def steps_kernel(*refs, spots):
    count = len(spots)
    packs = 1 + max(spot[0] for spot in spots)
    ins, outs = refs[packs : packs + 5 * count], refs[packs + 5 * count :]
    for w, (pack, row, rows, cols) in enumerate(spots):
        grad = refs[pack][row : row + rows, 0:cols]
        weight, mean, square, left, right = [ref[...] for ref in ins[5 * w : 5 * w + 5]]
        results = (grad,) + turned_step(weight, grad, mean, square, left, right)
        for ref, value in zip(outs[4 * w : 4 * w + 4], results):
            ref[...] = value


def steps(packs, spots, groups):
    arrays = []
    shapes = []
    for weight, mean, square, left, right in groups:
        arrays += [weight.T, mean.T, square.T, left, right]
        shapes += [jax.ShapeDtypeStruct(weight.shape[::-1], F32)] * 4
    return pl.pallas_call(
        functools.partial(steps_kernel, spots=spots),
        out_shape=tuple(shapes),
        in_specs=[vmem()] * (len(packs) + len(arrays)),
        out_specs=(vmem(),) * len(shapes),
        compiler_params=params(24),
        cost_estimate=cost(5),
        name="steps",
    )(*packs, *arrays)


def dense_step_kernel(*refs, rate):
    weight_ref, mean_ref, square_ref, block_ref = refs[:4]
    grad_ref, mom_ref, var_ref, new_ref = refs[-4:]
    grad = None
    for ref in refs[4:-4]:
        part = ref[...].astype(F32)
        grad = part if grad is None else grad + part
    grad_ref[...] = grad
    turned = dot3(grad, block_ref[0])
    momentum, variance, direction = adam_terms(turned, mean_ref[...], square_ref[...])
    mom_ref[...] = momentum
    var_ref[...] = variance
    new_ref[...] = weight_ref[...] - rate * dot3(direction, block_ref[0], NT)


def dense_step(weight, mean, square, block, parts, rate):
    shape = jax.ShapeDtypeStruct(weight.shape, F32)
    return pl.pallas_call(
        functools.partial(dense_step_kernel, rate=rate),
        out_shape=(shape,) * 4,
        in_specs=[vmem()] * (4 + len(parts)),
        out_specs=(vmem(),) * 4,
        compiler_params=params(),
        cost_estimate=cost(3),
        name="dense_step",
    )(weight, mean, square, block, *parts)


def swap(x, axis, bit, size):
    return lax.ppermute(x, axis, [(i, i ^ bit) for i in range(size)])


def bits_of(size):
    return [1 << b for b in range(size.bit_length() - 1)]


def fence(*values):
    leaves, tree = jax.tree.flatten(values)
    return jax.tree.unflatten(tree, lax.optimization_barrier(tuple(leaves)))


def stage(x, axis, bits, size):
    if len(bits) == 1:
        return [swap(x, axis, bits[0], size)]
    one, two = bits
    return [swap(x, axis, bit, size) for bit in (one, two, one | two)]


def stage_sum(x, came):
    up = [v.astype(F32) for v in [x] + came]
    if len(up) == 2:
        return up[0] + up[1]
    return (up[0] + up[1]) + (up[2] + up[3])


def bit_pairs(bits):
    odd = len(bits) % 2
    return [tuple(bits[k : k + 2]) for k in range(odd, len(bits), 2)] + [(b,) for b in bits[:odd]]


def few_stages(n_dp, n_own):
    plan = [("own", bits, n_own) for bits in bit_pairs(bits_of(n_own))]
    return plan + [("dp", bits, n_dp) for bits in bit_pairs(bits_of(n_dp))]


def light_stages(n_dp, n_own):
    far_first = bits_of(n_dp)[::-1]
    plan = [("dp", (bit,), n_dp) for bit in far_first] + [("own", (bit,), n_own) for bit in bits_of(n_own)[::-1]]
    return plan[:1] + plan[len(far_first) : -1] + plan[1 : len(far_first)] + plan[-1:]


def add_low(*terms):
    total = terms[0].astype(F32)
    for term in terms[1:]:
        total = total + term.astype(F32)
    return total.astype(BF)


def plain_gather(piece, n_dp, n_own):
    pieces = piece[None]
    spots = [(0, 0)]
    for bit in bits_of(n_dp):
        pieces = jnp.concatenate([pieces, swap(pieces, "dp", bit, n_dp)], axis=0)
        spots = spots + [(i ^ bit, j) for i, j in spots]
    for bit in bits_of(n_own):
        pieces = jnp.concatenate([pieces, swap(pieces, "own", bit, n_own)], axis=0)
        spots = spots + [(i, j ^ bit) for i, j in spots]
    return [(pieces, spots)]


def plain_scatter(keep, send, n_dp, n_own):
    block = add_low(keep, swap(send, "own", 1, n_own))
    bit = n_own // 2
    while bit > 1:
        half = block.shape[0] // 2
        block = add_low(block[:half], swap(block[half:], "own", bit, n_own))
        bit //= 2
    block = block[0]
    for bit in [1] + bits_of(n_dp)[:0:-1]:
        half = block.shape[0] // 2
        block = add_low(block[:half], swap(block[half:], "dp", bit, n_dp))
    return [block[0]]


def shards(
    frames, actions, dones, lengths, rewards, old_values, old_logp,
    conv_first, conv_second, conv_third, dense_hidden, dense_heads, bias_all,
    mean_first, mean_second, mean_third, mean_dense, mean_heads, mean_bias,
    square_first, square_second, square_third, square_dense, square_heads, square_bias,
    left_first, right_first, left_second, right_second, left_third, right_third,
    right_dense, left_heads, right_heads, *, n_dp, n_own,
):
    tokens, grid = frames.shape[0], frames.shape[1]
    planes = frames.shape[3]
    rows = dense_hidden.shape[0]
    tuned = (n_dp, n_own) == (8, 4)
    own_swap = lambda x, bit: swap(x, "own", bit, n_own)
    dp_swap = lambda x, bit: swap(x, "dp", bit, n_dp)
    place = jnp.stack([lax.axis_index("dp"), lax.axis_index("own")]).astype(jnp.int32)
    bias_row = bias_all.reshape(1, -1)
    adv, piece = first(lengths, dones, rewards, old_values, dense_hidden)
    cells = frames.transpose(1, 2, 3, 0).reshape(grid, grid * planes, tokens)

    if tuned:
        along_z = [dp_swap(piece, 2 * k) for k in (1, 2, 3)]
    act_one, slope_one_far = conv_one(cells, conv_first.T, bias_row)
    if tuned:
        spots = [(2 * k, 0) for k in range(4)]
        act_one, piece, along_z = fence(act_one, piece, along_z)
        column = jnp.stack([piece] + along_z)
        act_one, column = fence(act_one, column)
        by_x, by_y = dp_swap(column, 1), own_swap(column, 2)
    else:
        pieces = plain_gather(piece, n_dp, n_own)
    act_two, slope_two, act_one_far = conv_two(act_one, conv_second.T, bias_row)
    if tuned:
        act_two, column, by_x, by_y = fence(act_two, column, by_x, by_y)
        halves = (by_x[0:2], by_y[2:4])
        plane = jnp.concatenate([column, by_x, by_y])
        act_two, halves, plane = fence(act_two, halves, plane)
        corner = [own_swap(halves[0], 2), dp_swap(halves[1], 1)]
        other = own_swap(plane, 1)
    flat, slope_three, act_two_far, slope_two_far = conv_three(act_two, slope_two, conv_third.T, bias_row)
    if tuned:
        flat, corner = fence(flat, corner)
        corner = jnp.concatenate(corner)
        plane_spots = [(i ^ x, j ^ y) for x, y in ((0, 0), (1, 0), (0, 2)) for i, j in spots]
        corner_spots = [(i ^ 1, j ^ 2) for i, j in spots]
        pieces = [(plane, plane_spots), (corner, corner_spots)]
        pieces += [
            (other, [(i, j ^ 1) for i, j in plane_spots]),
            (own_swap(corner, 1), [(i, j ^ 1) for i, j in corner_spots]),
        ]
    d_three, act_two, slope_two, keep, send, here_heads, sums, sum_heads = dense(
        place, lengths, flat, slope_three, act_two_far, slope_two_far, dense_heads.T, bias_row,
        actions, adv, old_values, old_logp, pieces, n_dp, n_own, rows,
    )

    many_plan, one_plan = light_stages(n_dp, n_own), few_stages(n_dp, n_own)

    def leave(x, plan, at):
        axis, bits, size = plan[at]
        return stage(x, axis, bits, size)

    def rest(x, plan, at, low):
        for k in range(at, len(plan)):
            total = stage_sum(x, leave(x, plan, k))
            x = total.astype(BF) if low and k < len(plan) - 1 else total
        return x

    d_three, act_two, slope_two, keep, send = fence(d_three, act_two, slope_two, keep, send)
    came = own_swap(send, 1) if tuned else None
    d_two, act_one, slope_one, pack, sum_two = conv_three_back(
        d_three, act_two, slope_two, act_one_far, slope_one_far, conv_third.T, here_heads
    )
    if tuned:
        d_two, keep, came = fence(d_two, keep, came)
        block = add_low(keep, came)
        ends = (block[1, 4:6], block[1, 6:8])
        d_two, block, ends = fence(d_two, block, ends)
        by_y, by_x = own_swap(ends[0], 2), dp_swap(ends[1], 1)
    d_one, d_one_far, pack, sum_one = conv_two_back(d_two, act_one, slope_one, conv_second.T, pack)
    if tuned:
        d_one, d_one_far, pack, block, by_x, by_y = fence(d_one, d_one_far, pack, block, by_x, by_y)
        side_x = jnp.concatenate([add_low(block[0, 4:6], by_y), block[0, 6:8]])
        side_y = jnp.concatenate([block[1, 0:2], add_low(block[1, 2:4], by_x)])
        d_one, d_one_far, pack, block, side_x, side_y = fence(d_one, d_one_far, pack, block[0, 0:4], side_x, side_y)
        by_x, by_y = dp_swap(side_x, 1), own_swap(side_y, 2)
    many = leave(pack, many_plan, 0)
    pack_one = conv_one_grad(cells, d_one, sums, sum_heads, sum_one, sum_two)
    if tuned:
        pack_one, block, by_x, by_y = fence(pack_one, block, by_x, by_y)
        block = add_low(block, by_x, by_y)
        parts = [block[k] for k in range(4)]
    else:
        parts = plain_scatter(keep, send, n_dp, n_own)
    pack_one, d_one_far, pack, many = fence(pack_one, d_one_far, pack, many)
    pack = stage_sum(pack, many).astype(BF)
    pack_one, d_one_far, pack, parts = fence(pack_one, d_one_far, pack, parts)
    if tuned:
        parts = [parts[0]] + [dp_swap(parts[k], 2 * k) for k in (1, 2, 3)]
    many = leave(pack, many_plan, 1)
    one = leave(pack_one, one_plan, 0)
    shape = cells.shape
    cuts = (0, 4, 8, grid // 2 + 1)
    back = None
    for k in range(3):
        back = frames_back(d_one_far, conv_first.T, shape, cuts[k], cuts[k + 1], back)
        back, d_one_far, parts, pack, many, pack_one, one = fence(
            back, d_one_far, parts, pack, many, pack_one, one
        )
        pack = stage_sum(pack, many).astype(BF)
        pack_one = stage_sum(pack_one, one)
        back, d_one_far, parts, pack, pack_one = fence(back, d_one_far, parts, pack, pack_one)
        many = leave(pack, many_plan, k + 2)
        if k < 2:
            one = leave(pack_one, one_plan, k + 1)
    frames_grad = back.reshape(grid, grid, planes, tokens).transpose(3, 0, 1, 2)
    grad_dense, *wide_step = dense_step(
        dense_hidden, mean_dense, square_dense, right_dense, parts, RATE / math.sqrt(rows * n_dp)
    )
    pack_one = rest(pack_one, one_plan, 3, False)
    first_step = steps(
        [pack_one], [(0, 0, 32, 256)], [(conv_first, mean_first, square_first, left_first, right_first)]
    )
    grad_dense, first_step, pack, many = fence(grad_dense, first_step, pack, many)
    pack = stage_sum(pack, many)
    if len(many_plan) > 5:
        pack = rest(pack.astype(BF), many_plan, 5, True)
    late = steps(
        [pack],
        [(0, 0, 64, 576), (0, 64, 19, 512), (0, 96, 64, 512)],
        [
            (conv_third, mean_third, square_third, left_third, right_third),
            (dense_heads, mean_heads, square_heads, left_heads, right_heads),
            (conv_second, mean_second, square_second, left_second, right_second),
        ],
    )
    third, top, second = late[0:4], late[4:8], late[8:12]
    grad_bias = jnp.concatenate(
        [pack_one[36, 0:32], pack_one[35, 0:64], pack_one[34, 0:64], pack_one[32], pack_one[33], pack_one[37, 0:19]]
    )
    mom_bias, var_bias, bias_dir = adam_terms(grad_bias, mean_bias, square_bias)
    new_bias = bias_all - BIAS_RATE * bias_dir
    outs = [frames_grad]
    wide_step = [grad_dense] + list(wide_step)
    for index, bias_part in enumerate((grad_bias, mom_bias, var_bias, new_bias)):
        outs += [first_step[index].T, second[index].T, third[index].T, wide_step[index], top[index].T, bias_part]
    return tuple(outs)


def solution(mesh):
    n_dp, n_own = mesh.shape["dp"], mesh.shape["own"]
    both = ("dp", "own")
    rep = P()
    in_specs = (
        (P(both, None, None, None), P(both, None), P(both, None), P(both))
        + (P(both, None),) * 3
        + (rep, rep, rep, P("dp", "own"), rep, rep) * 3
        + (rep,) * 6
        + (P("own", None, None), rep, rep)
    )
    out_specs = (P(both, None, None, None),) + (rep, rep, rep, P("dp", "own"), rep, rep) * 4
    body = functools.partial(shards, n_dp=n_dp, n_own=n_own)
    return jax.shard_map(body, mesh=mesh, in_specs=in_specs, out_specs=out_specs, check_vma=False)
```

```python
import functools
import math

import jax
import jax.numpy as jnp
from jax import lax
from jax.experimental import pallas as pl
from jax.experimental.pallas import tpu as pltpu
from jax.sharding import PartitionSpec as P

STEP = 10
GAMMA = 0.99
LAMBDA = 0.95
CLIP = 0.1
ENTROPY_COEF = 0.01
VALUE_COEF = 0.5
BETA = 0.5
EPSILON = 1e-08
RATE = 1.0
BIAS_RATE = 0.1
HIGH = lax.Precision.HIGHEST
ROOT = math.sqrt(2.0 / math.pi)
CUBE = 0.044715
BF = jnp.bfloat16
F32 = jnp.float32
MIB = 2**20

NN = (((1,), (0,)), ((), ()))
NT = (((1,), (1,)), ((), ()))
TN = (((0,), (0,)), ((), ()))


def dot(a, b, dims=NN, precision=None):
    return lax.dot_general(a, b, dims, precision=precision, preferred_element_type=F32)


def params(limit=32, **more):
    return pltpu.CompilerParams(vmem_limit_bytes=limit * MIB, **more)


def cost(us):
    return pl.CostEstimate(flops=int(us * 1e9), bytes_accessed=0, transcendentals=0)


def near(shape, dtype):
    return pltpu.VMEM(shape, dtype)


def held(x):
    return pltpu.with_memory_space_constraint(x, pltpu.VMEM)


def far(x):
    return pltpu.with_memory_space_constraint(x, pltpu.HBM)


def vmem():
    return pl.BlockSpec(memory_space=pltpu.VMEM)


def smem():
    return pl.BlockSpec(memory_space=pltpu.SMEM)


def anywhere():
    return pl.BlockSpec(memory_space=pl.ANY)


def row_copy(source, target, sems, r):
    return pltpu.make_async_copy(source.at[r], target.at[r], sems.at[r])


def start_rows(source, target, sems):
    for r in range(source.shape[0]):
        row_copy(source, target, sems, r).start()


def wait_rows(source, target, sems):
    for r in range(source.shape[0]):
        row_copy(source, target, sems, r).wait()


def call(body, ins, outs, in_specs=None, out_specs=None, scratch=(), grid=None, us=5, name=None, aliases=None, limit=24):
    more = {} if grid is None else {"grid": (grid,)}
    return pl.pallas_call(
        body,
        out_shape=tuple(outs),
        in_specs=list(in_specs or [vmem()] * len(ins)),
        out_specs=tuple(out_specs or [vmem()] * len(outs)),
        scratch_shapes=list(scratch),
        input_output_aliases=aliases or {},
        compiler_params=params(limit),
        cost_estimate=cost(us),
        name=name,
        **more,
    )(*ins)


def dma(count):
    return pltpu.SemaphoreType.DMA((count,))


def gelu_both(x):
    x2 = x * x
    up = 1.0 + jnp.tanh(x * (ROOT + (ROOT * CUBE) * x2))
    h = 0.5 * x
    bend = h * (ROOT + (3.0 * ROOT * CUBE) * x2)
    return h * up, up * (0.5 + bend * (2.0 - up))


def wide(line, rows, n):
    k = line.shape[1]
    column = jnp.broadcast_to(line, (128, k)).T
    tall = jnp.concatenate([column] * (rows // k), axis=0) if rows > k else column
    return jnp.concatenate([tall] * (n // 128), axis=1)


def lanes(parts):
    return jnp.concatenate([p for p in parts if p.shape[1] > 0], axis=1)


def band_forward(w, kernel, feats, count):
    ch = w.shape[0]
    run = kernel * feats
    rows = []
    for j in range(count):
        parts = []
        for a in range(kernel):
            parts.append(jnp.zeros((ch, j * feats), F32))
            parts.append(w[:, a * run : (a + 1) * run])
            parts.append(jnp.zeros((ch, (count - 1 - j) * feats), F32))
        rows.append(lanes(parts))
    return jnp.concatenate(rows, axis=0).astype(BF)


def band_square(w, feats):
    ch = w.shape[0]
    rows = []
    for dy in range(2):
        for dx in range(2):
            lead = (dy * 3 + dx) * feats
            rows.append(
                lanes(
                    [
                        jnp.zeros((ch, lead), F32),
                        w[:, : 2 * feats],
                        jnp.zeros((ch, feats), F32),
                        w[:, 2 * feats :],
                        jnp.zeros((ch, 4 * feats - lead), F32),
                    ]
                )
            )
    return jnp.concatenate(rows, axis=0).astype(BF)


def band_back(w, kernel, feats, count):
    ch = w.shape[0]
    turned = w.T
    zero = jnp.zeros((feats, ch), F32)
    rows = []
    for i in range(count):
        parts = []
        for a in range(kernel):
            for j in range(kernel + count - 1):
                b = j - i
                if 0 <= b < kernel:
                    spot = ((kernel - 1 - a) * kernel + (kernel - 1 - b)) * feats
                    parts.append(turned[spot : spot + feats])
                else:
                    parts.append(zero)
        rows.append(lanes(parts))
    return jnp.concatenate(rows, axis=0).astype(BF)


def first_kernel(
    lengths_ref, dones_far_ref, rewards_far_ref, values_far_ref, weight_far_ref, frames_ref,
    adv_ref, piece_ref, cells_ref, dones_ref, rewards_ref, values_ref, weight_ref, sems, small_sems,
):
    near_refs = (dones_ref, rewards_ref, values_ref, weight_ref)
    far_refs = (dones_far_ref, rewards_far_ref, values_far_ref, weight_far_ref)
    small = [pltpu.make_async_copy(a, b, small_sems.at[k]) for k, (a, b) in enumerate(zip(far_refs, near_refs))]
    for copy in small:
        copy.start()
    for r in range(5):
        ring_copy(frames_ref, cells_ref, sems, r).start()
    for copy in small:
        copy.wait()
    n = rewards_ref.shape[1]
    length = lengths_ref[0]
    position = lax.broadcasted_iota(jnp.int32, (8, n), 1)
    live = position < length
    mask = jnp.where(live, 1.0, 0.0)
    next_live = jnp.where(position + 1 < length, 1.0, 0.0)
    values = jnp.broadcast_to(values_ref[...], (8, n))
    rewards = jnp.broadcast_to(rewards_ref[...], (8, n))
    going = 1.0 - jnp.broadcast_to(dones_ref[...], (8, n)).astype(F32)

    def ahead(v, k, fill):
        return jnp.concatenate([v[:, k:], jnp.full((8, k), fill, F32)], axis=1)

    delta = rewards + GAMMA * going * ahead(values, 1, 0.0) * next_live - values
    total = mask * delta
    carry = mask * (GAMMA * LAMBDA) * going
    k = 1
    while k < n:
        total = total + carry * ahead(total, k, 0.0)
        carry = carry * ahead(carry, k, 0.0)
        k *= 2
    adv_ref[...] = total[0:1]
    count = jnp.sum(mask, axis=1, keepdims=True)
    mean = jnp.sum(mask * total, axis=1, keepdims=True) / count
    spread = jnp.sum(mask * (total - mean) ** 2, axis=1, keepdims=True)
    lane = lax.broadcasted_iota(jnp.int32, (8, 128), 1)
    stat = jnp.where(lane == 0, count, jnp.where(lane == 1, mean, jnp.where(lane == 2, spread, 0.0)))
    top = stat.astype(BF).astype(F32)
    mid = (stat - top).astype(BF).astype(F32)
    low = ((stat - top) - mid).astype(BF).astype(F32)
    line = lax.broadcasted_iota(jnp.int32, (8, 128), 0)
    terms = jnp.where(line == 0, top, jnp.where(line == 1, mid, jnp.where(line == 2, low, 0.0)))
    rows = weight_ref.shape[0]
    tail = piece_ref.shape[0] - 16
    piece_ref[...] = jnp.zeros_like(piece_ref)
    piece_ref[0:rows, :] = weight_ref[...].astype(BF)
    piece_ref[tail:, :] = jnp.concatenate([terms, jnp.zeros((8, 128), F32)], axis=0).astype(BF)
    for r in range(5):
        ring_copy(frames_ref, cells_ref, sems, r).wait()


def first(lengths, dones, rewards, old_values, weight, frames):
    n = rewards.shape[1]
    rows = -(-weight.shape[0] // 16) * 16 + 16
    small = [dones, rewards, old_values, weight]
    return pl.pallas_call(
        first_kernel,
        out_shape=(
            jax.ShapeDtypeStruct((1, n), F32),
            jax.ShapeDtypeStruct((rows, 128), BF),
            near((RING,) + frames.shape[1:], BF),
        ),
        in_specs=[smem()] + [anywhere()] * 5,
        out_specs=(vmem(),) * 3,
        scratch_shapes=[pltpu.VMEM(a.shape, a.dtype) for a in small] + [dma(5), dma(4)],
        compiler_params=params(16),
        cost_estimate=cost(3),
        name="first",
    )(lengths, *[far(a) for a in small], far(frames))


RING = 8


def ring_copy(frames_ref, cells_ref, sems, r):
    slot = r % RING if isinstance(r, int) else lax.rem(r, RING)
    return pltpu.make_async_copy(frames_ref.at[r], cells_ref.at[slot], sems.at[slot])


def fetch_rows(frames_ref, cells_ref, sems, step, last):
    @pl.when(step < last - 1)
    def _():
        ring_copy(frames_ref, cells_ref, sems, 2 * step + 5).start()
        ring_copy(frames_ref, cells_ref, sems, 2 * step + 6).start()

    @pl.when(step >= 2)
    def _():
        ring_copy(frames_ref, cells_ref, sems, 2 * step + 1).wait()
        ring_copy(frames_ref, cells_ref, sems, 2 * step + 2).wait()

    return [lax.rem(2 * step + a, RING) for a in range(3)]


def conv_one_kernel(
    frames_ref, weight_ref, bias_ref, cells_in_ref, act_ref, slope_ref, cells_ref, band_ref, wide_ref, sems
):
    n = act_ref.shape[-1]
    half = act_ref.shape[0]
    step = pl.program_id(0)

    slots = fetch_rows(frames_ref, cells_ref, sems, step, half - 1)

    @pl.when(step == 0)
    def _():
        band_ref[...] = band_square(weight_ref[...], 64)
        wide_ref[...] = wide(bias_ref[:, 0:32], 128, n)

    for col in range(half):
        span = slice(col * 128, col * 128 + 192)
        patch = jnp.concatenate([cells_ref[slot, span, :] for slot in slots], axis=0)
        act, slope = gelu_both(dot(band_ref[...], patch) + wide_ref[...])
        act_ref[step, col] = act.astype(BF)
        slope_ref[step, col] = slope.astype(BF)


def conv_one(frames, weight, bias, cells):
    grid, _, n = frames.shape
    half = grid // 2
    shape = (half, half, 128, n)
    return call(
        conv_one_kernel,
        [far(frames), weight, bias, held(cells)],
        [near(shape, BF), near(shape, BF), near(cells.shape, BF)],
        in_specs=[anywhere()] + [vmem()] * 3,
        scratch=[pltpu.VMEM((128, 576), BF), pltpu.VMEM((128, n), F32), dma(RING)],
        grid=half,
        us=12,
        name="conv_one",
        aliases={3: 2},
        limit=16,
    )


def conv_two_kernel(
    one_ref, slope_one_ref, weight_ref, bias_ref, act_ref, slope_ref, one_far_ref, slope_one_far_ref,
    band_ref, wide_ref, sems, slope_sems,
):
    n = act_ref.shape[-1]
    step = pl.program_id(0)

    @pl.when(step == 0)
    def _():
        start_rows(one_ref, one_far_ref, sems)
        start_rows(slope_one_ref, slope_one_far_ref, slope_sems)
        band_ref[...] = band_forward(weight_ref[...], 2, 128, 3)
        wide_ref[...] = wide(bias_ref[:, 32:96], 192, n)

    for part in range(3):
        span = slice(3 * part, 3 * part + 4)
        patch = jnp.concatenate(
            [one_ref[step + a, span].reshape(512, n) for a in range(2)], axis=0
        )
        act, slope = gelu_both(dot(band_ref[...], patch) + wide_ref[...])
        rows = slice(part * 192, part * 192 + 192)
        act_ref[step, rows, :] = act.astype(BF)
        slope_ref[step, rows, :] = slope.astype(BF)

    @pl.when(step == 8)
    def _():
        wait_rows(one_ref, one_far_ref, sems)
        wait_rows(slope_one_ref, slope_one_far_ref, slope_sems)


def conv_two(act_one, slope_one, weight, bias):
    n = act_one.shape[-1]
    shape = (9, 576, n)
    return call(
        conv_two_kernel,
        [held(act_one), held(slope_one), weight, bias],
        [near(shape, BF)] * 2 + [pltpu.HBM(act_one.shape, BF)] * 2,
        out_specs=[vmem(), vmem(), anywhere(), anywhere()],
        scratch=[pltpu.VMEM((192, 1024), BF), pltpu.VMEM((192, n), F32), dma(10), dma(10)],
        grid=9,
        us=7,
        name="conv_two",
        limit=16,
    )


def conv_three_kernel(
    two_ref, slope_two_ref, weight_ref, bias_ref,
    flat_far_ref, slope_far_ref, two_far_ref, slope_two_far_ref,
    band_ref, wide_ref, flat_ref, slope_ref, two_sems, slope_two_sems, flat_sems, slope_sems,
):
    n = two_ref.shape[-1]
    step = pl.program_id(0)

    @pl.when(step == 0)
    def _():
        start_rows(two_ref, two_far_ref, two_sems)
        start_rows(slope_two_ref, slope_two_far_ref, slope_two_sems)
        band_ref[...] = band_forward(weight_ref[...], 3, 64, 4)
        wide_ref[...] = wide(bias_ref[:, 96:160], 256, n)

    for drop, start in ((0, 0), (1, 3)):
        patch = jnp.concatenate(
            [two_ref[step + a, start * 64 : start * 64 + 384, :] for a in range(3)], axis=0
        )
        pre = dot(band_ref[drop * 64 :, :], patch) + wide_ref[drop * 64 :, :]
        act, slope = gelu_both(pre)
        rows = slice((start + drop) * 64, (start + 4) * 64)
        flat_ref[step, rows, :] = act.astype(BF)
        slope_ref[step, rows, :] = slope.astype(BF)
    row_copy(flat_ref, flat_far_ref, flat_sems, step).start()
    row_copy(slope_ref, slope_far_ref, slope_sems, step).start()

    @pl.when(step == 6)
    def _():
        wait_rows(two_ref, two_far_ref, two_sems)
        wait_rows(slope_two_ref, slope_two_far_ref, slope_two_sems)
        wait_rows(flat_ref, flat_far_ref, flat_sems)
        wait_rows(slope_ref, slope_far_ref, slope_sems)


def conv_three(act_two, slope_two, weight, bias):
    n = act_two.shape[-1]
    shape = (7, 448, n)
    out, two = pltpu.HBM(shape, BF), pltpu.HBM(act_two.shape, BF)
    return call(
        conv_three_kernel,
        [held(act_two), held(slope_two), weight, bias],
        [out, out, two, two],
        out_specs=[anywhere()] * 4,
        scratch=[
            pltpu.VMEM((256, 1152), BF),
            pltpu.VMEM((256, n), F32),
            pltpu.VMEM(shape, BF),
            pltpu.VMEM(shape, BF),
            dma(9),
            dma(9),
            dma(7),
            dma(7),
        ],
        grid=7,
        us=6,
        name="conv_three",
        limit=16,
    )


def head_gradient(heads, actions, adv, values, old_logp, mask, count, centre, var):
    rows, n = heads.shape
    acts = rows - 1
    norm_adv = (adv - centre) * lax.rsqrt(var + 1e-05)
    returns = adv + values
    index = lax.broadcasted_iota(jnp.int32, (rows, n), 0)
    is_logit = index < acts
    top = jnp.max(jnp.where(is_logit, heads, -jnp.inf), axis=0, keepdims=True)
    shifted = heads - top
    grown = jnp.where(is_logit, jnp.exp(jnp.where(is_logit, shifted, 0.0)), 0.0)
    total = jnp.sum(grown, axis=0, keepdims=True)
    logp_all = jnp.where(is_logit, shifted - jnp.log(total), 0.0)
    prob = jnp.where(is_logit, jnp.exp(logp_all), 0.0)
    chosen = jnp.where(index == actions, 1.0, 0.0)
    logp = jnp.sum(logp_all * chosen, axis=0, keepdims=True)
    plogp = jnp.sum(prob * logp_all, axis=0, keepdims=True)
    value = jnp.sum(jnp.where(index == acts, heads, 0.0), axis=0, keepdims=True)
    ratio = jnp.exp(logp - old_logp)
    bent = jnp.tanh((ratio - 1.0) / CLIP)
    soft = 1.0 + CLIP * bent
    plain = ratio * norm_adv
    clipped = soft * norm_adv
    share = jnp.where(plain < clipped, 1.0, jnp.where(plain > clipped, 0.0, 0.5))
    by_ratio = -norm_adv * (share + (1.0 - share) * (1.0 - bent * bent))
    scale = mask / count
    by_logp = by_ratio * ratio
    by_logit = by_logp * (chosen - prob) + ENTROPY_COEF * prob * (logp_all - plogp)
    by_value = VALUE_COEF * (value - returns)
    return jnp.where(is_logit, by_logit, by_value) * scale


def dense_kernel(*refs, places, n_dp, n_own, rows):
    place_ref, lengths_ref = refs[:2]
    small_far_refs, (flat_far_ref, slope_far_ref, two_far_ref) = refs[2:8], refs[8:11]
    piece_refs = refs[11 : 11 + len(places)]
    (
        d_three_far_ref, two_ref, keep_ref, send_ref, grad_heads_ref, sums_ref, sum_heads_ref,
        blocks_ref, weight_ref, d_dense_ref, flat_ref, slope_ref, *small_refs,
        sems, two_sems, flat_sems, slope_sems, small_sems,
    ) = refs[11 + len(places) :]
    heads_ref, bias_ref, actions_ref, adv_ref, values_ref, logp_ref = small_refs
    n = flat_ref.shape[-1]
    cols = 128
    dp, own = place_ref[0], place_ref[1]
    stats = []
    copies = []
    for ref, spots in zip(piece_refs, places):
        for k, (i, j) in enumerate(spots):
            copies.append(
                pltpu.make_async_copy(ref.at[k], blocks_ref.at[i ^ dp, j ^ own], sems.at[len(copies)])
            )
    for k in range(6):
        copies.append(pltpu.make_async_copy(small_far_refs[k], small_refs[k], small_sems.at[k]))
    for copy in copies:
        copy.start()
    start_rows(flat_far_ref, flat_ref, flat_sems)
    for copy in copies:
        copy.wait()
    start_rows(slope_far_ref, slope_ref, slope_sems)
    start_rows(two_far_ref, two_ref, two_sems)
    for i in range(n_dp):
        for j in range(n_own):
            tail = blocks_ref[i, j, blocks_ref.shape[2] - 16 :].astype(F32)
            stats.append((tail[0:1] + tail[1:2]) + tail[2:3])
    stats = jnp.concatenate(stats, axis=0)
    each = stats[:, 0:1]
    count = jnp.sum(each, axis=0, keepdims=True)
    centre = jnp.sum(each * stats[:, 1:2], axis=0, keepdims=True) / count
    gap = stats[:, 1:2] - centre
    var = jnp.sum(stats[:, 2:3] + each * gap * gap, axis=0, keepdims=True) / count
    for i in range(n_dp):
        for j in range(n_own):
            weight_ref[i * rows : (i + 1) * rows, j * cols : (j + 1) * cols] = blocks_ref[i, j, 0:rows]
    hid = n_own * cols
    bias_dense = wide(bias_ref[:, 160 : 160 + hid], hid, n)
    bias_heads = wide(bias_ref[:, 160 + hid : 160 + hid + 19], 19, n)
    wait_rows(flat_far_ref, flat_ref, flat_sems)
    flat = flat_ref[...].reshape(n_dp * rows, n)
    pre = dot(weight_ref[...], flat, TN) + bias_dense
    hidden, slope = gelu_both(pre)
    hidden = hidden.astype(BF)
    head_weight = heads_ref[...].astype(BF)
    heads = dot(head_weight, hidden) + bias_heads
    position = lax.broadcasted_iota(jnp.int32, (1, n), 1)
    mask = jnp.where(position < lengths_ref[0], 1.0, 0.0)
    d_heads = head_gradient(
        heads, actions_ref[...], adv_ref[...], values_ref[...], logp_ref[...], mask, count, centre, var
    ).astype(BF)
    ones = jnp.ones((8, n), BF)
    grad_heads_ref[...] = dot(d_heads, hidden, NT)
    sum_heads_ref[...] = dot(ones, d_heads, NT)[0:1]
    d_dense = (dot(head_weight, d_heads, TN) * slope).astype(BF)
    sums_ref[0:1, 128 : 128 + hid] = dot(ones, d_dense, NT)[0:1]
    for j in range(n_own):
        d_dense_ref[j] = d_dense[j * cols : (j + 1) * cols]
    for half, ref in ((0, keep_ref), (1, send_ref)):
        for k in range(n_own // 4):
            both = [d_dense_ref[own ^ (4 * k + half)], d_dense_ref[own ^ (4 * k + 2 + half)]]
            block = dot(flat, jnp.concatenate(both, axis=0), NT).astype(BF)
            for i in range(n_dp):
                rel = i ^ dp
                spot = (rel % 2) * (n_dp // 2) + rel // 2
                for m in range(2):
                    ref[2 * k + m, spot] = block[i * rows : (i + 1) * rows, m * cols : (m + 1) * cols]
    wait_rows(slope_far_ref, slope_ref, slope_sems)
    total = jnp.zeros((64, n), F32)
    for part in range(7):
        span = slice(part * 448, part * 448 + 448)
        d_three = (dot(weight_ref[span, :], d_dense) * slope_ref[part].astype(F32)).astype(BF)
        slope_ref[part] = d_three
        row_copy(slope_ref, d_three_far_ref, slope_sems, part).start()
        back = d_three.astype(F32)
        for c in range(7):
            total = total + back[c * 64 : c * 64 + 64]
    sums_ref[0:1, 0:64] = dot(jnp.ones((8, n), F32), total, NT, HIGH)[0:1]
    sums_ref[0:1, 64:128] = jnp.zeros((1, 64), F32)
    wait_rows(two_far_ref, two_ref, two_sems)
    wait_rows(slope_ref, d_three_far_ref, slope_sems)


def dense(
    place, lengths, heads, bias, actions, adv, values, logp, flat, slope_three, act_two,
    pieces, n_dp, n_own, rows,
):
    n = flat.shape[-1]
    hid = n_own * 128
    part = pltpu.HBM((n_own // 2, n_dp, rows, 128), BF)
    arrays = [far(p[0]) for p in pieces]
    small = [heads, bias, actions, adv, values, logp]
    body = functools.partial(
        dense_kernel, places=[p[1] for p in pieces], n_dp=n_dp, n_own=n_own, rows=rows
    )
    return call(
        body,
        [place, lengths] + [far(a) for a in small + [flat, slope_three, act_two]] + arrays,
        [
            pltpu.HBM(flat.shape, BF),
            near(act_two.shape, BF),
            part,
            part,
            jax.ShapeDtypeStruct(heads.shape, F32),
            jax.ShapeDtypeStruct((1, 128 + hid), F32),
            jax.ShapeDtypeStruct((1, heads.shape[0]), F32),
        ],
        in_specs=[smem(), smem()] + [anywhere()] * (9 + len(arrays)),
        out_specs=[anywhere()] + [vmem()] * 6,
        scratch=[
            pltpu.VMEM((n_dp, n_own) + arrays[0].shape[1:], BF),
            pltpu.VMEM((n_dp * rows, hid), BF),
            pltpu.VMEM((n_own, 128, n), BF),
            pltpu.VMEM(flat.shape, BF),
            pltpu.VMEM(flat.shape, BF),
        ]
        + [pltpu.VMEM(a.shape, a.dtype) for a in small]
        + [dma(n_dp * n_own), dma(9), dma(7), dma(7), dma(6)],
        us=10,
        name="dense",
        limit=32,
    )


def conv_three_back_kernel(
    act_ref, d_three_ref, slope_far_ref, one_far_ref, slope_one_far_ref, weight_ref, heads_ref,
    d_two_ref, one_ref, slope_one_ref, pack_ref, sum_ref,
    band_ref, pad_ref, acc_ref, tot_ref, slope_ref, one_sems, slope_one_sems, slope_sems, d_sems,
):
    n = act_ref.shape[-1]
    step = pl.program_id(0)

    def three_row(r):
        inner = pad_ref.at[r + 2, pl.ds(128, 448), :]
        return pltpu.make_async_copy(d_three_ref.at[r], inner, d_sems.at[r])

    @pl.when(step == 0)
    def _():
        for r in range(7):
            three_row(r).start()
        for r in range(11):
            if 2 <= r < 9:
                pad_ref[r, 0:128, :] = jnp.zeros((128, n), BF)
                pad_ref[r, 576:704, :] = jnp.zeros((128, n), BF)
            else:
                pad_ref[r] = jnp.zeros((704, n), BF)
        start_rows(slope_far_ref, slope_ref, slope_sems)
        band_ref[...] = band_back(weight_ref[...], 3, 64, 3)
        acc_ref[...] = jnp.zeros_like(acc_ref)
        tot_ref[...] = jnp.zeros_like(tot_ref)
        for r in range(7):
            three_row(r).wait()
        start_rows(one_far_ref, one_ref, one_sems)
        start_rows(slope_one_far_ref, slope_one_ref, slope_one_sems)

    row_copy(slope_far_ref, slope_ref, slope_sems, step).wait()
    total = tot_ref[...]
    for part in range(3):
        patch = jnp.concatenate(
            [pad_ref[step + a, part * 192 : part * 192 + 320, :] for a in range(3)], axis=0
        )
        rows = slice(part * 192, part * 192 + 192)
        d_two = (dot(band_ref[...], patch) * slope_ref[step, rows, :].astype(F32)).astype(BF)
        d_two_ref[step, rows, :] = d_two
        back = d_two.astype(F32)
        total = total + (back[0:64] + back[64:128]) + back[128:192]
    tot_ref[...] = total

    @pl.when(step < 7)
    def _():
        row = pad_ref[step + 2, 128 : 128 + 448, :]
        second = jnp.concatenate([jnp.zeros((64, n), BF), row[256:448]], axis=0)
        for d_rows, start in ((row[0:256], 0), (second, 3)):
            span = slice(start * 64, start * 64 + 384)
            cells = jnp.concatenate([act_ref[step + a, span, :] for a in range(3)], axis=0)
            acc_ref[...] += dot(d_rows, cells, NT)

    @pl.when(step == 8)
    def _():
        wait_rows(one_far_ref, one_ref, one_sems)
        wait_rows(slope_one_far_ref, slope_one_ref, slope_one_sems)
        for a in range(3):
            out = None
            for c in range(4):
                piece = acc_ref[c * 64 : c * 64 + 64, a * 384 + c * 64 : a * 384 + c * 64 + 192]
                out = piece if out is None else out + piece
            pack_ref[0:64, a * 192 : a * 192 + 192] = out.astype(BF)
        pack_ref[0:64, 576:640] = jnp.zeros((64, 64), BF)
        pack_ref[64:80, 0:512] = heads_ref[0:16, :].astype(BF)
        pack_ref[80:96, 0:512] = jnp.concatenate(
            [heads_ref[16:19, :], jnp.zeros((13, 512), F32)], axis=0
        ).astype(BF)
        pack_ref[64:96, 512:640] = jnp.zeros((32, 128), BF)
        sum_ref[...] = dot(jnp.ones((8, n), F32), tot_ref[...], NT, HIGH)[0:1]


def conv_three_back(d_three, act_two, slope_two, act_one, slope_one, weight, heads):
    n = act_two.shape[-1]
    return call(
        conv_three_back_kernel,
        [held(act_two)] + [far(a) for a in (d_three, slope_two, act_one, slope_one)] + [weight, heads],
        [
            near(act_two.shape, BF),
            near(act_one.shape, BF),
            near(act_one.shape, BF),
            jax.ShapeDtypeStruct((96, 640), BF),
            jax.ShapeDtypeStruct((1, 64), F32),
        ],
        in_specs=[vmem()] + [anywhere()] * 4 + [vmem()] * 2,
        scratch=[
            pltpu.VMEM((192, 960), BF),
            pltpu.VMEM((11, 704, n), BF),
            pltpu.VMEM((256, 1152), F32),
            pltpu.VMEM((64, n), F32),
            pltpu.VMEM(act_two.shape, BF),
            dma(10),
            dma(10),
            dma(9),
            dma(7),
        ],
        grid=9,
        us=9,
        name="conv_three_back",
        limit=16,
    )


def conv_two_back_kernel(
    d_two_ref, act_ref, slope_ref, weight_ref, pack_ref, d_one_ref, grad_ref, sum_ref,
    band_ref, pad_ref, acc_ref, tot_ref,
):
    n = d_one_ref.shape[-1]
    step = pl.program_id(0)

    @pl.when(step == 0)
    def _():
        band_ref[...] = band_back(weight_ref[...], 2, 128, 1)
        pad_ref[...] = jnp.zeros_like(pad_ref)
        acc_ref[...] = jnp.zeros_like(acc_ref)
        tot_ref[...] = jnp.zeros_like(tot_ref)
        for r in range(9):
            pad_ref[r + 1, 64 : 64 + 576, :] = d_two_ref[r]

    total = tot_ref[...]
    for col in range(10):
        patch = jnp.concatenate(
            [pad_ref[step + a, col * 64 : col * 64 + 128, :] for a in range(2)], axis=0
        )
        d_one = (dot(band_ref[...], patch) * slope_ref[step, col].astype(F32)).astype(BF)
        d_one_ref[step, col] = d_one
        total = total + d_one.astype(F32)
    tot_ref[...] = total

    @pl.when(step < 9)
    def _():
        for part in range(3):
            span = slice(3 * part, 3 * part + 4)
            cells = jnp.concatenate(
                [act_ref[step + a, span].reshape(512, n) for a in range(2)], axis=0
            )
            rows = pad_ref[step + 1, 64 + part * 192 : 64 + part * 192 + 192, :]
            acc_ref[...] += dot(rows, cells, NT)

    @pl.when(step == 9)
    def _():
        for a in range(2):
            out = None
            for c in range(3):
                piece = acc_ref[c * 64 : c * 64 + 64, a * 512 + c * 128 : a * 512 + c * 128 + 256]
                out = piece if out is None else out + piece
            grad_ref[96:160, a * 256 : a * 256 + 256] = out.astype(BF)
        grad_ref[0:96, :] = pack_ref[...]
        grad_ref[96:160, 512:640] = jnp.zeros((64, 128), BF)
        sums = dot(jnp.ones((8, n), F32), tot_ref[...], NT, HIGH)[0:1]
        sum_ref[...] = (sums[:, 0:32] + sums[:, 32:64]) + (sums[:, 64:96] + sums[:, 96:128])


def conv_two_back(d_two, act_one, slope_one, weight, pack):
    n = act_one.shape[-1]
    return call(
        conv_two_back_kernel,
        [held(d_two), held(act_one), held(slope_one), weight, pack],
        [
            near(act_one.shape, BF),
            jax.ShapeDtypeStruct((160, 640), BF),
            jax.ShapeDtypeStruct((1, 32), F32),
        ],
        scratch=[
            pltpu.VMEM((128, 256), BF),
            pltpu.VMEM((11, 704, n), BF),
            pltpu.VMEM((192, 1024), F32),
            pltpu.VMEM((128, n), F32),
        ],
        grid=10,
        us=11,
        name="conv_two_back",
        limit=16,
    )


def conv_one_grad_kernel(
    frames_ref, d_one_ref, cells_in_ref, dense_ref, heads_ref, one_ref, two_ref,
    grad_ref, d_out_ref, cells_ref, acc_ref, sems,
):
    n = d_one_ref.shape[-1]
    step = pl.program_id(0)
    half = pl.num_programs(0)

    slots = fetch_rows(frames_ref, cells_ref, sems, step, half - 1)

    @pl.when(step == 0)
    def _():
        acc_ref[...] = jnp.zeros_like(acc_ref)

    for pair in range(d_one_ref.shape[1] // 2):
        span = slice(pair * 256, pair * 256 + 320)
        cells = jnp.concatenate([cells_ref[slot, span, :] for slot in slots], axis=0)
        rows = d_one_ref[step, 2 * pair : 2 * pair + 2].reshape(256, n)
        acc_ref[...] += dot(rows, cells, NT)

    @pl.when(step == half - 1)
    def _():
        for a in range(2):
            out = None
            for k in range(2):
                for dy in range(2):
                    for dx in range(2):
                        row = ((k * 2 + dy) * 2 + dx) * 32
                        lane = (dy + a) * 320 + (2 * k + dx) * 64
                        piece = acc_ref[row : row + 32, lane : lane + 128]
                        out = piece if out is None else out + piece
            grad_ref[:, a * 128 : a * 128 + 128] = out[0:16]
            grad_ref[:, 256 + a * 128 : 384 + a * 128] = out[16:32]
        grad_ref[:, 512:640] = jnp.zeros((16, 128), F32)
        for k in range(4):
            grad_ref[k : k + 1, 512:640] = dense_ref[0:1, 128 + k * 128 : 256 + k * 128]
        grad_ref[4:5, 512:576] = dense_ref[0:1, 0:64]
        grad_ref[5:6, 512:576] = two_ref[...]
        grad_ref[6:7, 512:544] = one_ref[...]
        grad_ref[7:8, 512:531] = heads_ref[...]


def conv_one_grad(frames, d_one, cells, sums, sum_heads, sum_one, sum_two):
    return pl.pallas_call(
        conv_one_grad_kernel,
        out_shape=(
            jax.ShapeDtypeStruct((16, 640), F32),
            near(d_one.shape, BF),
            near(cells.shape, BF),
        ),
        grid=(d_one.shape[0],),
        in_specs=[anywhere()] + [vmem()] * 6,
        out_specs=(vmem(),) * 3,
        scratch_shapes=[pltpu.VMEM((256, 960), F32), dma(RING)],
        input_output_aliases={1: 1, 2: 2},
        compiler_params=params(16),
        cost_estimate=cost(10),
        name="conv_one_grad",
    )(far(frames), held(d_one), held(cells), sums, sum_heads, sum_one, sum_two)


def frames_back_kernel(*refs, begin, end, total, ahead):
    d_one_ref, weight_ref = refs[:2]
    if ahead:
        frames_ref = refs[2]
        out_ref, d_out_ref, cells_ref, band_ref, rows_ref, sems, cell_sems = refs[-7:]
    else:
        out_ref, d_out_ref, band_ref, rows_ref, sems = refs[-5:]
    n = rows_ref.shape[-1]
    step = pl.program_id(0)
    row = step + begin
    cells = d_one_ref.shape[1]
    zero = jnp.zeros((32, n), BF)

    @pl.when(step == 0)
    def _():
        if ahead:
            for r in range(5):
                ring_copy(frames_ref, cells_ref, cell_sems, r).start()
        band_ref[...] = band_back(weight_ref[...], 2, 64, 3)

    def slab(at, dy, first, alive):
        parts = []
        for c in range(first, first + 4):
            if c < 0 or c >= 2 * cells:
                parts.append(zero)
            else:
                spot = (dy * 2 + c % 2) * 32
                parts.append(d_one_ref[at, c // 2, spot : spot + 32, :])
        whole = jnp.concatenate(parts, axis=0)
        return whole if alive is None else jnp.where(alive, whole, jnp.zeros_like(whole))

    def make(up, low, at):
        for block in range(7):
            first = 3 * block - 1
            patch = jnp.concatenate([slab(*up[:2], first, up[2]), slab(*low[:2], first, low[2])], axis=0)
            rows_ref[at, block * 192 : block * 192 + 192, :] = dot(band_ref[...], patch).astype(BF)

    def send(at):
        return pltpu.make_async_copy(rows_ref.at[at], out_ref.at[at + 2 * begin], sems.at[at])

    here = row if end < total else jnp.minimum(row, total - 2)
    above = row - 1 if begin > 0 else jnp.maximum(row - 1, 0)
    make(
        (above, 1, None if begin > 0 else row > 0),
        (here, 0, None if end < total else row < total - 1),
        2 * step,
    )
    send(2 * step).start()

    @pl.when(row < total - 1)
    def _():
        make((here, 0, None), (here, 1, None), 2 * step + 1)
        send(2 * step + 1).start()

    @pl.when(step == end - begin - 1)
    def _():
        for at in range(min(2 * end, 2 * total - 1) - 2 * begin):
            send(at).wait()
        if ahead:
            for r in range(5):
                ring_copy(frames_ref, cells_ref, cell_sems, r).wait()


def frames_back(d_one, weight, shape, begin, end, so_far=None, frames=None):
    total = d_one.shape[0] + 1
    ahead = frames is not None
    more = [far(frames)] if ahead else [] if so_far is None else [so_far]
    count = end - begin
    cells = [near((RING,) + shape[1:], BF)] if ahead else []
    return call(
        functools.partial(frames_back_kernel, begin=begin, end=end, total=total, ahead=ahead),
        [held(d_one), weight] + more,
        [pltpu.HBM(shape, BF), near(d_one.shape, BF)] + cells,
        in_specs=[vmem(), vmem()] + [anywhere()] * len(more),
        out_specs=[anywhere(), vmem()] + [vmem()] * len(cells),
        scratch=[
            pltpu.VMEM((192, 256), BF),
            pltpu.VMEM((2 * count,) + shape[1:], BF),
            dma(2 * count),
        ]
        + [dma(5)] * len(cells),
        grid=count,
        us=count,
        name="frames_back",
        aliases={0: 1, 2: 0} if so_far is not None else {0: 1},
        limit=16,
    )


def adam_terms(grad, mean, square):
    momentum = BETA * mean + (1.0 - BETA) * grad
    variance = BETA * square + (1.0 - BETA) * grad * grad
    fix = 1.0 - BETA**STEP
    direction = momentum / fix / (jnp.sqrt(variance / fix) + EPSILON)
    return (momentum, variance, direction)


def split(x):
    top = x.astype(BF)
    return top, (x - top.astype(F32)).astype(BF)


def dot3(a, b, dims=NN):
    a_top, a_low = split(a)
    b_top, b_low = split(b)
    if dims == TN:
        return dot(a_top, b_top, dims) + (dot(a_top, b_low, dims) + dot(a_low, b_top, dims))
    rows = a.shape[0]
    both = dot(jnp.concatenate([a_top, a_low], axis=0), b_top, dims)
    return both[:rows] + (both[rows:] + dot(a_top, b_low, dims))


def turned_step(weight, grad, mean, square, left, right):
    rate = RATE / math.sqrt(weight.shape[1])
    turned = dot3(dot3(right, grad, TN), left)
    momentum, variance, direction = adam_terms(turned, mean, square)
    back = dot3(dot3(right, direction), left, NT)
    return momentum, variance, weight - rate * back


def steps_kernel(*refs, spots):
    count = len(spots)
    packs = 1 + max(spot[0] for spot in spots)
    ins, outs = refs[packs : packs + 5 * count], refs[packs + 5 * count :]
    for w, (pack, row, rows, cols) in enumerate(spots):
        grad = refs[pack][row : row + rows, 0:cols].astype(F32)
        if rows == 16:
            grad = jnp.concatenate([grad, refs[pack][row : row + rows, cols : 2 * cols]], axis=0)
        weight, mean, square, left, right = [ref[...] for ref in ins[5 * w : 5 * w + 5]]
        results = (grad,) + turned_step(weight, grad, mean, square, left, right)
        for ref, value in zip(outs[4 * w : 4 * w + 4], results):
            ref[...] = value


def steps(packs, spots, groups):
    arrays = []
    shapes = []
    for weight, mean, square, left, right in groups:
        arrays += [weight.T, mean.T, square.T, left, right]
        shapes += [jax.ShapeDtypeStruct(weight.shape[::-1], F32)] * 4
    return pl.pallas_call(
        functools.partial(steps_kernel, spots=spots),
        out_shape=tuple(shapes),
        in_specs=[vmem()] * (len(packs) + len(arrays)),
        out_specs=(vmem(),) * len(shapes),
        compiler_params=params(32),
        cost_estimate=cost(5),
        name="steps",
    )(*packs, *arrays)


def dense_step_kernel(*refs, rate):
    weight_ref, mean_ref, square_ref, block_ref = refs[:4]
    grad_ref, mom_ref, var_ref, new_ref = refs[-4:]
    grad = None
    for ref in refs[4:-4]:
        part = ref[...].astype(F32)
        grad = part if grad is None else grad + part
    grad_ref[...] = grad
    turned = dot3(grad, block_ref[0])
    momentum, variance, direction = adam_terms(turned, mean_ref[...], square_ref[...])
    mom_ref[...] = momentum
    var_ref[...] = variance
    new_ref[...] = weight_ref[...] - rate * dot3(direction, block_ref[0], NT)


def dense_step(weight, mean, square, block, parts, rate):
    shape = jax.ShapeDtypeStruct(weight.shape, F32)
    return pl.pallas_call(
        functools.partial(dense_step_kernel, rate=rate),
        out_shape=(shape,) * 4,
        in_specs=[vmem()] * (4 + len(parts)),
        out_specs=(vmem(),) * 4,
        compiler_params=params(),
        cost_estimate=cost(3),
        name="dense_step",
    )(weight, mean, square, block, *parts)


def swap(x, axis, bit, size):
    return lax.ppermute(x, axis, [(i, i ^ bit) for i in range(size)])


def bits_of(size):
    return [1 << b for b in range(size.bit_length() - 1)]


def fence(*values):
    leaves, tree = jax.tree.flatten(values)
    return jax.tree.unflatten(tree, lax.optimization_barrier(tuple(leaves)))


def add_low(*terms):
    total = terms[0].astype(F32)
    for term in terms[1:]:
        total = total + term.astype(F32)
    return total.astype(BF)


def plain_gather(piece, n_dp, n_own):
    pieces = piece[None]
    spots = [(0, 0)]
    for bit in bits_of(n_dp):
        pieces = jnp.concatenate([pieces, swap(pieces, "dp", bit, n_dp)], axis=0)
        spots = spots + [(i ^ bit, j) for i, j in spots]
    for bit in bits_of(n_own):
        pieces = jnp.concatenate([pieces, swap(pieces, "own", bit, n_own)], axis=0)
        spots = spots + [(i, j ^ bit) for i, j in spots]
    return [(pieces, spots)]


def plain_scatter(keep, send, n_dp, n_own):
    block = add_low(keep, swap(send, "own", 1, n_own))
    bit = n_own // 2
    while bit > 1:
        half = block.shape[0] // 2
        block = add_low(block[:half], swap(block[half:], "own", bit, n_own))
        bit //= 2
    block = block[0]
    for bit in [1] + bits_of(n_dp)[:0:-1]:
        half = block.shape[0] // 2
        block = add_low(block[:half], swap(block[half:], "dp", bit, n_dp))
    return [block[0]]


def shards(
    frames, actions, dones, lengths, rewards, old_values, old_logp,
    conv_first, conv_second, conv_third, dense_hidden, dense_heads, bias_all,
    mean_first, mean_second, mean_third, mean_dense, mean_heads, mean_bias,
    square_first, square_second, square_third, square_dense, square_heads, square_bias,
    left_first, right_first, left_second, right_second, left_third, right_third,
    right_dense, left_heads, right_heads, *, n_dp, n_own,
):
    tokens, grid = frames.shape[0], frames.shape[1]
    planes = frames.shape[3]
    rows = dense_hidden.shape[0]
    tuned = (n_dp, n_own) == (8, 4)
    own_swap = lambda x, bit: swap(x, "own", bit, n_own)
    dp_swap = lambda x, bit: swap(x, "dp", bit, n_dp)
    place = jnp.stack([lax.axis_index("dp"), lax.axis_index("own")]).astype(jnp.int32)
    bias_row = bias_all.reshape(1, -1)
    cells = frames.transpose(1, 2, 3, 0).reshape(grid, grid * planes, tokens)
    adv, piece, ring = first(lengths, dones, rewards, old_values, dense_hidden, cells)

    if tuned:
        along_z = [dp_swap(piece, 2 * k) for k in (1, 2, 3)]
    act_one, slope_one, _ = conv_one(cells, conv_first.T, bias_row, ring)
    if tuned:
        spots = [(2 * k, 0) for k in range(4)]
        act_one, slope_one, piece, along_z = fence(act_one, slope_one, piece, along_z)
        column = jnp.stack([piece] + along_z)
        act_one, slope_one, column = fence(act_one, slope_one, column)
        by_x, by_y = dp_swap(column, 1), own_swap(column, 2)
    else:
        pieces = plain_gather(piece, n_dp, n_own)
    act_two, slope_two, act_one_far, slope_one_far = conv_two(act_one, slope_one, conv_second.T, bias_row)
    if tuned:
        act_two, slope_two, column, by_x, by_y = fence(act_two, slope_two, column, by_x, by_y)
        halves = (by_x[0:2], by_y[2:4])
        plane = jnp.concatenate([column, by_x, by_y])
        act_two, slope_two, halves, plane = fence(act_two, slope_two, halves, plane)
        corner = [own_swap(halves[0], 2), dp_swap(halves[1], 1)]
        other = own_swap(plane, 1)
    flat, slope_three, act_two_far, slope_two_far = conv_three(act_two, slope_two, conv_third.T, bias_row)
    if tuned:
        flat, corner = fence(flat, corner)
        corner = jnp.concatenate(corner)
        plane_spots = [(i ^ x, j ^ y) for x, y in ((0, 0), (1, 0), (0, 2)) for i, j in spots]
        corner_spots = [(i ^ 1, j ^ 2) for i, j in spots]
        pieces = [(plane, plane_spots), (corner, corner_spots)]
        pieces += [
            (other, [(i, j ^ 1) for i, j in plane_spots]),
            (own_swap(corner, 1), [(i, j ^ 1) for i, j in corner_spots]),
        ]
    d_three, act_two, keep, send, here_heads, sums, sum_heads = dense(
        place, lengths, dense_heads.T, bias_row, actions, adv, old_values, old_logp,
        flat, slope_three, act_two_far, pieces, n_dp, n_own, rows,
    )

    came = own_swap(send, 1) if tuned else None
    d_two, act_one, slope_one, pack, sum_two = conv_three_back(
        d_three, act_two, slope_two_far, act_one_far, slope_one_far, conv_third.T, here_heads
    )
    if tuned:
        d_two, act_one, slope_one, keep, came = fence(d_two, act_one, slope_one, keep, came)
        block = add_low(keep, came)
        ends = (block[1, 4:6], block[1, 6:8])
        d_two, act_one, slope_one, block, ends = fence(d_two, act_one, slope_one, block, ends)
        by_y, by_x = own_swap(ends[0], 2), dp_swap(ends[1], 1)
    d_one, pack, sum_one = conv_two_back(d_two, act_one, slope_one, conv_second.T, pack)

    shape = cells.shape
    side = lax.axis_index("own") % 2
    rows_half = pack.shape[0] // 2
    if tuned:
        d_one, pack, block, by_x, by_y = fence(d_one, pack, block, by_x, by_y)
        side_x = jnp.concatenate([add_low(block[0, 4:6], by_y), block[0, 6:8]])
        side_y = jnp.concatenate([block[1, 0:2], add_low(block[1, 2:4], by_x)])
        block = block[0, 0:4]
    else:
        side_x = side_y = block = jnp.zeros((8, 128), BF)
    half = lax.dynamic_slice_in_dim(pack, side * rows_half, rows_half)
    gone = lax.dynamic_slice_in_dim(pack, (1 - side) * rows_half, rows_half)
    d_one, half, gone, block, side_x, side_y = fence(d_one, half, gone, block, side_x, side_y)
    if tuned:
        by_x, by_y = dp_swap(side_x, 1), own_swap(side_y, 2)
    came = own_swap(gone, 1)
    cuts = (0, 2, 5, 8, grid // 2 + 1)
    back, d_one, ring = frames_back(d_one, conv_first.T, shape, cuts[0], cuts[1], frames=cells)
    back, d_one, ring, half, came = fence(back, d_one, ring, half, came)
    half = add_low(half, came)
    back, d_one, ring, half = fence(back, d_one, ring, half)
    far_bits = bits_of(n_dp)[:0:-1]
    came = dp_swap(half, far_bits[0])
    pack_one, d_one, _ = conv_one_grad(cells, d_one, ring, sums, sum_heads, sum_one, sum_two)
    if tuned:
        pack_one, d_one, block, by_x, by_y = fence(pack_one, d_one, block, by_x, by_y)
        block = add_low(block, by_x, by_y)
    pack_one, d_one, half, came = fence(pack_one, d_one, half, came)

    half = add_low(half, came)
    pack_one, d_one, half, block = fence(pack_one, d_one, half, block)
    came_one = dp_swap(pack_one, far_bits[0])
    came = own_swap(half, 2)
    if tuned:
        parts = [block[0]] + [dp_swap(block[k], 2 * k) for k in (1, 2, 3)]
    else:
        parts = plain_scatter(keep, send, n_dp, n_own)
    back, d_one = frames_back(d_one, conv_first.T, shape, cuts[1], cuts[2], back)
    back, d_one, half, came, pack_one, came_one = fence(back, d_one, half, came, pack_one, came_one)

    def join(pack, pack_one):
        return jnp.concatenate([pack.astype(BF), *split(pack_one)])

    def part(both):
        count = pack_one.shape[0]
        low = both[rows_half:].astype(F32)
        return both[:rows_half].astype(F32), low[:count] + low[count:]

    def add_up(both, came):
        a, b = part(both), part(came)
        return a[0] + b[0], a[1] + b[1]

    both = join(add_low(half, came), pack_one + came_one)
    back, d_one, both = fence(back, d_one, both)
    more = [1] + far_bits[1:]
    came = dp_swap(both, more[0])
    back, d_one = frames_back(d_one, conv_first.T, shape, cuts[2], cuts[3], back)
    back, d_one, both, came = fence(back, d_one, both, came)
    both = join(*add_up(both, came))
    back, d_one, both = fence(back, d_one, both)
    came = dp_swap(both, more[1])
    back, d_one = frames_back(d_one, conv_first.T, shape, cuts[3], cuts[4], back)
    for bit in more[2:]:
        both = join(*add_up(both, came))
        came = dp_swap(both, bit)
    back, parts, both, came = fence(back, parts, both, came)
    both = join(*add_up(both, came))
    parts, both = fence(parts, both)
    came = own_swap(both, 1)
    frames_grad = back.reshape(grid, grid, planes, tokens).transpose(3, 0, 1, 2)
    grad_dense, *wide_step = dense_step(
        dense_hidden, mean_dense, square_dense, right_dense, parts, RATE / math.sqrt(rows * n_dp)
    )
    grad_dense, both, came = fence(grad_dense, both, came)
    pack_one = add_up(both, came)[1]
    halves = (both[:rows_half], came[:rows_half])
    pack = jnp.concatenate([jnp.where(side == 0, *halves), jnp.where(side == 0, *halves[::-1])])
    pack_one, pack = fence(pack_one, pack)
    one = own_swap(pack_one, 2)
    late = steps(
        [pack],
        [(0, 0, 64, 576), (0, 64, 19, 512), (0, 96, 64, 512)],
        [
            (conv_third, mean_third, square_third, left_third, right_third),
            (dense_heads, mean_heads, square_heads, left_heads, right_heads),
            (conv_second, mean_second, square_second, left_second, right_second),
        ],
    )
    late, pack_one, one = fence(late, pack_one, one)
    pack_one = pack_one + one
    third, top, second = late[0:4], late[4:8], late[8:12]
    first_step = steps(
        [pack_one],
        [(0, 0, 16, 256)],
        [(conv_first, mean_first, square_first, left_first, right_first)],
    )
    line = pack_one[:, 512:]
    grad_bias = jnp.concatenate(
        [line[6, 0:32], line[5, 0:64], line[4, 0:64], line[0], line[1], line[2], line[3], line[7, 0:19]]
    )
    mom_bias, var_bias, bias_dir = adam_terms(grad_bias, mean_bias, square_bias)
    new_bias = bias_all - BIAS_RATE * bias_dir
    outs = [frames_grad]
    wide_step = [grad_dense] + list(wide_step)
    for index, bias_part in enumerate((grad_bias, mom_bias, var_bias, new_bias)):
        outs += [first_step[index].T, second[index].T, third[index].T, wide_step[index], top[index].T, bias_part]
    return tuple(outs)


def solution(mesh):
    n_dp, n_own = mesh.shape["dp"], mesh.shape["own"]
    both = ("dp", "own")
    rep = P()
    in_specs = (
        (P(both, None, None, None), P(both, None), P(both, None), P(both))
        + (P(both, None),) * 3
        + (rep, rep, rep, P("dp", "own"), rep, rep) * 3
        + (rep,) * 6
        + (P("own", None, None), rep, rep)
    )
    out_specs = (P(both, None, None, None),) + (rep, rep, rep, P("dp", "own"), rep, rep) * 4
    body = functools.partial(shards, n_dp=n_dp, n_own=n_own)
    return jax.shard_map(body, mesh=mesh, in_specs=in_specs, out_specs=out_specs, check_vma=False)
```

```python
import functools
import math

import jax
import jax.numpy as jnp
from jax import lax
from jax.experimental import pallas as pl
from jax.experimental.pallas import tpu as pltpu
from jax.sharding import PartitionSpec as P

STEP = 10
GAMMA = 0.99
LAMBDA = 0.95
CLIP = 0.1
ENTROPY_COEF = 0.01
VALUE_COEF = 0.5
BETA = 0.5
EPSILON = 1e-08
RATE = 1.0
BIAS_RATE = 0.1
HIGH = lax.Precision.HIGHEST
ROOT = math.sqrt(2.0 / math.pi)
CUBE = 0.044715
BF = jnp.bfloat16
F32 = jnp.float32
MIB = 2**20

NN = (((1,), (0,)), ((), ()))
NT = (((1,), (1,)), ((), ()))
TN = (((0,), (0,)), ((), ()))


def dot(a, b, dims=NN, precision=None):
    return lax.dot_general(a, b, dims, precision=precision, preferred_element_type=F32)


def params(limit=32, **more):
    return pltpu.CompilerParams(vmem_limit_bytes=limit * MIB, **more)


def cost(us):
    return pl.CostEstimate(flops=int(us * 1e9), bytes_accessed=0, transcendentals=0)


def near(shape, dtype):
    return pltpu.VMEM(shape, dtype)


def held(x):
    return pltpu.with_memory_space_constraint(x, pltpu.VMEM)


def far(x):
    return pltpu.with_memory_space_constraint(x, pltpu.HBM)


def vmem():
    return pl.BlockSpec(memory_space=pltpu.VMEM)


def smem():
    return pl.BlockSpec(memory_space=pltpu.SMEM)


def anywhere():
    return pl.BlockSpec(memory_space=pl.ANY)


def row_copy(source, target, sems, r):
    return pltpu.make_async_copy(source.at[r], target.at[r], sems.at[r])


def start_rows(source, target, sems):
    for r in range(source.shape[0]):
        row_copy(source, target, sems, r).start()


def wait_rows(source, target, sems):
    for r in range(source.shape[0]):
        row_copy(source, target, sems, r).wait()


def call(body, ins, outs, in_specs=None, out_specs=None, scratch=(), grid=None, us=5, name=None, aliases=None, limit=24):
    more = {} if grid is None else {"grid": (grid,)}
    return pl.pallas_call(
        body,
        out_shape=tuple(outs),
        in_specs=list(in_specs or [vmem()] * len(ins)),
        out_specs=tuple(out_specs or [vmem()] * len(outs)),
        scratch_shapes=list(scratch),
        input_output_aliases=aliases or {},
        compiler_params=params(limit),
        cost_estimate=cost(us),
        name=name,
        **more,
    )(*ins)


def dma(count):
    return pltpu.SemaphoreType.DMA((count,))


def gelu_both(x):
    x2 = x * x
    up = 1.0 + jnp.tanh(x * (ROOT + (ROOT * CUBE) * x2))
    h = 0.5 * x
    bend = h * (ROOT + (3.0 * ROOT * CUBE) * x2)
    return h * up, up * (0.5 + bend * (2.0 - up))


def wide(line, rows, n):
    k = line.shape[1]
    column = jnp.broadcast_to(line, (128, k)).T
    tall = jnp.concatenate([column] * (rows // k), axis=0) if rows > k else column
    return jnp.concatenate([tall] * (n // 128), axis=1)


def lanes(parts):
    return jnp.concatenate([p for p in parts if p.shape[1] > 0], axis=1)


def band_forward(w, kernel, feats, count):
    ch = w.shape[0]
    run = kernel * feats
    rows = []
    for j in range(count):
        parts = []
        for a in range(kernel):
            parts.append(jnp.zeros((ch, j * feats), F32))
            parts.append(w[:, a * run : (a + 1) * run])
            parts.append(jnp.zeros((ch, (count - 1 - j) * feats), F32))
        rows.append(lanes(parts))
    return jnp.concatenate(rows, axis=0).astype(BF)


def band_square(w, feats):
    ch = w.shape[0]
    rows = []
    for dy in range(2):
        for dx in range(2):
            lead = (dy * 3 + dx) * feats
            rows.append(
                lanes(
                    [
                        jnp.zeros((ch, lead), F32),
                        w[:, : 2 * feats],
                        jnp.zeros((ch, feats), F32),
                        w[:, 2 * feats :],
                        jnp.zeros((ch, 4 * feats - lead), F32),
                    ]
                )
            )
    return jnp.concatenate(rows, axis=0).astype(BF)


def band_back(w, kernel, feats, count):
    ch = w.shape[0]
    turned = w.T
    zero = jnp.zeros((feats, ch), F32)
    rows = []
    for i in range(count):
        parts = []
        for a in range(kernel):
            for j in range(kernel + count - 1):
                b = j - i
                if 0 <= b < kernel:
                    spot = ((kernel - 1 - a) * kernel + (kernel - 1 - b)) * feats
                    parts.append(turned[spot : spot + feats])
                else:
                    parts.append(zero)
        rows.append(lanes(parts))
    return jnp.concatenate(rows, axis=0).astype(BF)


def first_kernel(
    lengths_ref, dones_far_ref, rewards_far_ref, values_far_ref, weight_far_ref, frames_ref,
    adv_ref, piece_ref, cells_ref, dones_ref, rewards_ref, values_ref, weight_ref, sems, small_sems,
):
    near_refs = (dones_ref, rewards_ref, values_ref, weight_ref)
    far_refs = (dones_far_ref, rewards_far_ref, values_far_ref, weight_far_ref)
    small = [pltpu.make_async_copy(a, b, small_sems.at[k]) for k, (a, b) in enumerate(zip(far_refs, near_refs))]
    for copy in small:
        copy.start()
    for r in range(5):
        ring_copy(frames_ref, cells_ref, sems, r).start()
    for copy in small:
        copy.wait()
    n = rewards_ref.shape[1]
    length = lengths_ref[0]
    position = lax.broadcasted_iota(jnp.int32, (8, n), 1)
    live = position < length
    mask = jnp.where(live, 1.0, 0.0)
    next_live = jnp.where(position + 1 < length, 1.0, 0.0)
    values = jnp.broadcast_to(values_ref[...], (8, n))
    rewards = jnp.broadcast_to(rewards_ref[...], (8, n))
    going = 1.0 - jnp.broadcast_to(dones_ref[...], (8, n)).astype(F32)

    def ahead(v, k, fill):
        return jnp.concatenate([v[:, k:], jnp.full((8, k), fill, F32)], axis=1)

    delta = rewards + GAMMA * going * ahead(values, 1, 0.0) * next_live - values
    total = mask * delta
    carry = mask * (GAMMA * LAMBDA) * going
    k = 1
    while k < n:
        total = total + carry * ahead(total, k, 0.0)
        carry = carry * ahead(carry, k, 0.0)
        k *= 2
    adv_ref[...] = total[0:1]
    count = jnp.sum(mask, axis=1, keepdims=True)
    mean = jnp.sum(mask * total, axis=1, keepdims=True) / count
    spread = jnp.sum(mask * (total - mean) ** 2, axis=1, keepdims=True)
    lane = lax.broadcasted_iota(jnp.int32, (8, 128), 1)
    stat = jnp.where(lane == 0, count, jnp.where(lane == 1, mean, jnp.where(lane == 2, spread, 0.0)))
    top = stat.astype(BF).astype(F32)
    mid = (stat - top).astype(BF).astype(F32)
    low = ((stat - top) - mid).astype(BF).astype(F32)
    line = lax.broadcasted_iota(jnp.int32, (8, 128), 0)
    terms = jnp.where(line == 0, top, jnp.where(line == 1, mid, jnp.where(line == 2, low, 0.0)))
    rows = weight_ref.shape[0]
    tail = piece_ref.shape[0] - 16
    piece_ref[...] = jnp.zeros_like(piece_ref)
    piece_ref[0:rows, :] = weight_ref[...].astype(BF)
    piece_ref[tail:, :] = jnp.concatenate([terms, jnp.zeros((8, 128), F32)], axis=0).astype(BF)
    for r in range(5):
        ring_copy(frames_ref, cells_ref, sems, r).wait()


def first(lengths, dones, rewards, old_values, weight, frames):
    n = rewards.shape[1]
    rows = -(-weight.shape[0] // 16) * 16 + 16
    small = [dones, rewards, old_values, weight]
    return pl.pallas_call(
        first_kernel,
        out_shape=(
            jax.ShapeDtypeStruct((1, n), F32),
            jax.ShapeDtypeStruct((rows, 128), BF),
            near((RING,) + frames.shape[1:], BF),
        ),
        in_specs=[smem()] + [anywhere()] * 5,
        out_specs=(vmem(),) * 3,
        scratch_shapes=[pltpu.VMEM(a.shape, a.dtype) for a in small] + [dma(5), dma(4)],
        compiler_params=params(16),
        cost_estimate=cost(3),
        name="first",
    )(lengths, *[far(a) for a in small], far(frames))


RING = 8


def ring_copy(frames_ref, cells_ref, sems, r):
    slot = r % RING if isinstance(r, int) else lax.rem(r, RING)
    return pltpu.make_async_copy(frames_ref.at[r], cells_ref.at[slot], sems.at[slot])


def fetch_rows(frames_ref, cells_ref, sems, step, last):
    @pl.when(step < last - 1)
    def _():
        ring_copy(frames_ref, cells_ref, sems, 2 * step + 5).start()
        ring_copy(frames_ref, cells_ref, sems, 2 * step + 6).start()

    @pl.when(step >= 2)
    def _():
        ring_copy(frames_ref, cells_ref, sems, 2 * step + 1).wait()
        ring_copy(frames_ref, cells_ref, sems, 2 * step + 2).wait()

    return [lax.rem(2 * step + a, RING) for a in range(3)]


def conv_one_kernel(
    frames_ref, weight_ref, bias_ref, cells_in_ref, act_ref, slope_ref, cells_ref, band_ref, wide_ref, sems
):
    n = act_ref.shape[-1]
    half = act_ref.shape[0]
    step = pl.program_id(0)

    slots = fetch_rows(frames_ref, cells_ref, sems, step, half - 1)

    @pl.when(step == 0)
    def _():
        band_ref[...] = band_square(weight_ref[...], 64)
        wide_ref[...] = wide(bias_ref[:, 0:32], 128, n)

    for col in range(half):
        span = slice(col * 128, col * 128 + 192)
        patch = jnp.concatenate([cells_ref[slot, span, :] for slot in slots], axis=0)
        act, slope = gelu_both(dot(band_ref[...], patch) + wide_ref[...])
        act_ref[step, col] = act.astype(BF)
        slope_ref[step, col] = slope.astype(BF)


def conv_one(frames, weight, bias, cells):
    grid, _, n = frames.shape
    half = grid // 2
    shape = (half, half, 128, n)
    return call(
        conv_one_kernel,
        [far(frames), weight, bias, held(cells)],
        [near(shape, BF), near(shape, BF), near(cells.shape, BF)],
        in_specs=[anywhere()] + [vmem()] * 3,
        scratch=[pltpu.VMEM((128, 576), BF), pltpu.VMEM((128, n), F32), dma(RING)],
        grid=half,
        us=12,
        name="conv_one",
        aliases={3: 2},
        limit=16,
    )


def conv_two_kernel(
    one_ref, slope_one_ref, weight_ref, bias_ref, act_ref, slope_ref, one_far_ref, slope_one_far_ref,
    band_ref, wide_ref, sems, slope_sems,
):
    n = act_ref.shape[-1]
    step = pl.program_id(0)

    @pl.when(step == 0)
    def _():
        start_rows(one_ref, one_far_ref, sems)
        start_rows(slope_one_ref, slope_one_far_ref, slope_sems)
        band_ref[...] = band_forward(weight_ref[...], 2, 128, 3)
        wide_ref[...] = wide(bias_ref[:, 32:96], 192, n)

    for part in range(3):
        span = slice(3 * part, 3 * part + 4)
        patch = jnp.concatenate(
            [one_ref[step + a, span].reshape(512, n) for a in range(2)], axis=0
        )
        act, slope = gelu_both(dot(band_ref[...], patch) + wide_ref[...])
        rows = slice(part * 192, part * 192 + 192)
        act_ref[step, rows, :] = act.astype(BF)
        slope_ref[step, rows, :] = slope.astype(BF)

    @pl.when(step == 8)
    def _():
        wait_rows(one_ref, one_far_ref, sems)
        wait_rows(slope_one_ref, slope_one_far_ref, slope_sems)


def conv_two(act_one, slope_one, weight, bias):
    n = act_one.shape[-1]
    shape = (9, 576, n)
    return call(
        conv_two_kernel,
        [held(act_one), held(slope_one), weight, bias],
        [near(shape, BF)] * 2 + [pltpu.HBM(act_one.shape, BF)] * 2,
        out_specs=[vmem(), vmem(), anywhere(), anywhere()],
        scratch=[pltpu.VMEM((192, 1024), BF), pltpu.VMEM((192, n), F32), dma(10), dma(10)],
        grid=9,
        us=7,
        name="conv_two",
        limit=16,
    )


def conv_three_kernel(
    two_ref, slope_two_ref, weight_ref, bias_ref,
    flat_far_ref, slope_far_ref, two_far_ref, slope_two_far_ref,
    band_ref, wide_ref, flat_ref, slope_ref, two_sems, slope_two_sems, flat_sems, slope_sems,
):
    n = two_ref.shape[-1]
    step = pl.program_id(0)

    @pl.when(step == 0)
    def _():
        start_rows(two_ref, two_far_ref, two_sems)
        start_rows(slope_two_ref, slope_two_far_ref, slope_two_sems)
        band_ref[...] = band_forward(weight_ref[...], 3, 64, 4)
        wide_ref[...] = wide(bias_ref[:, 96:160], 256, n)

    for drop, start in ((0, 0), (1, 3)):
        patch = jnp.concatenate(
            [two_ref[step + a, start * 64 : start * 64 + 384, :] for a in range(3)], axis=0
        )
        pre = dot(band_ref[drop * 64 :, :], patch) + wide_ref[drop * 64 :, :]
        act, slope = gelu_both(pre)
        rows = slice((start + drop) * 64, (start + 4) * 64)
        flat_ref[step, rows, :] = act.astype(BF)
        slope_ref[step, rows, :] = slope.astype(BF)
    row_copy(flat_ref, flat_far_ref, flat_sems, step).start()
    row_copy(slope_ref, slope_far_ref, slope_sems, step).start()

    @pl.when(step == 6)
    def _():
        wait_rows(two_ref, two_far_ref, two_sems)
        wait_rows(slope_two_ref, slope_two_far_ref, slope_two_sems)
        wait_rows(flat_ref, flat_far_ref, flat_sems)
        wait_rows(slope_ref, slope_far_ref, slope_sems)


def conv_three(act_two, slope_two, weight, bias):
    n = act_two.shape[-1]
    shape = (7, 448, n)
    out, two = pltpu.HBM(shape, BF), pltpu.HBM(act_two.shape, BF)
    return call(
        conv_three_kernel,
        [held(act_two), held(slope_two), weight, bias],
        [out, out, two, two],
        out_specs=[anywhere()] * 4,
        scratch=[
            pltpu.VMEM((256, 1152), BF),
            pltpu.VMEM((256, n), F32),
            pltpu.VMEM(shape, BF),
            pltpu.VMEM(shape, BF),
            dma(9),
            dma(9),
            dma(7),
            dma(7),
        ],
        grid=7,
        us=6,
        name="conv_three",
        limit=16,
    )


def head_gradient(heads, actions, adv, values, old_logp, mask, count, centre, var):
    rows, n = heads.shape
    acts = rows - 1
    norm_adv = (adv - centre) * lax.rsqrt(var + 1e-05)
    returns = adv + values
    index = lax.broadcasted_iota(jnp.int32, (rows, n), 0)
    is_logit = index < acts
    top = jnp.max(jnp.where(is_logit, heads, -jnp.inf), axis=0, keepdims=True)
    shifted = heads - top
    grown = jnp.where(is_logit, jnp.exp(jnp.where(is_logit, shifted, 0.0)), 0.0)
    total = jnp.sum(grown, axis=0, keepdims=True)
    logp_all = jnp.where(is_logit, shifted - jnp.log(total), 0.0)
    prob = jnp.where(is_logit, jnp.exp(logp_all), 0.0)
    chosen = jnp.where(index == actions, 1.0, 0.0)
    logp = jnp.sum(logp_all * chosen, axis=0, keepdims=True)
    plogp = jnp.sum(prob * logp_all, axis=0, keepdims=True)
    value = jnp.sum(jnp.where(index == acts, heads, 0.0), axis=0, keepdims=True)
    ratio = jnp.exp(logp - old_logp)
    bent = jnp.tanh((ratio - 1.0) / CLIP)
    soft = 1.0 + CLIP * bent
    plain = ratio * norm_adv
    clipped = soft * norm_adv
    share = jnp.where(plain < clipped, 1.0, jnp.where(plain > clipped, 0.0, 0.5))
    by_ratio = -norm_adv * (share + (1.0 - share) * (1.0 - bent * bent))
    scale = mask / count
    by_logp = by_ratio * ratio
    by_logit = by_logp * (chosen - prob) + ENTROPY_COEF * prob * (logp_all - plogp)
    by_value = VALUE_COEF * (value - returns)
    return jnp.where(is_logit, by_logit, by_value) * scale


def dense_kernel(*refs, places, n_dp, n_own, rows):
    place_ref, lengths_ref = refs[:2]
    small_far_refs, (flat_far_ref, slope_far_ref, two_far_ref) = refs[2:8], refs[8:11]
    piece_refs = refs[11 : 11 + len(places)]
    (
        d_three_far_ref, two_ref, keep_far_ref, send_far_ref, grad_heads_ref, sums_ref, sum_heads_ref,
        blocks_ref, weight_ref, d_dense_ref, flat_ref, slope_ref, keep_ref, send_ref, *small_refs,
        sems, two_sems, flat_sems, slope_sems, small_sems, out_sems,
    ) = refs[11 + len(places) :]
    heads_ref, bias_ref, actions_ref, adv_ref, values_ref, logp_ref = small_refs
    n = flat_ref.shape[-1]
    cols = 128
    dp, own = place_ref[0], place_ref[1]
    stats = []
    copies = []
    for ref, spots in zip(piece_refs, places):
        for k, (i, j) in enumerate(spots):
            copies.append(
                pltpu.make_async_copy(ref.at[k], blocks_ref.at[i ^ dp, j ^ own], sems.at[len(copies)])
            )
    for k in range(6):
        copies.append(pltpu.make_async_copy(small_far_refs[k], small_refs[k], small_sems.at[k]))
    for copy in copies:
        copy.start()
    start_rows(flat_far_ref, flat_ref, flat_sems)
    for copy in copies:
        copy.wait()
    start_rows(slope_far_ref, slope_ref, slope_sems)
    start_rows(two_far_ref, two_ref, two_sems)
    for i in range(n_dp):
        for j in range(n_own):
            tail = blocks_ref[i, j, blocks_ref.shape[2] - 16 :].astype(F32)
            stats.append((tail[0:1] + tail[1:2]) + tail[2:3])
    stats = jnp.concatenate(stats, axis=0)
    each = stats[:, 0:1]
    count = jnp.sum(each, axis=0, keepdims=True)
    centre = jnp.sum(each * stats[:, 1:2], axis=0, keepdims=True) / count
    gap = stats[:, 1:2] - centre
    var = jnp.sum(stats[:, 2:3] + each * gap * gap, axis=0, keepdims=True) / count
    for i in range(n_dp):
        for j in range(n_own):
            weight_ref[i * rows : (i + 1) * rows, j * cols : (j + 1) * cols] = blocks_ref[i, j, 0:rows]
    hid = n_own * cols
    bias_dense = wide(bias_ref[:, 160 : 160 + hid], hid, n)
    bias_heads = wide(bias_ref[:, 160 + hid : 160 + hid + 19], 19, n)
    wait_rows(flat_far_ref, flat_ref, flat_sems)
    flat = flat_ref[...].reshape(n_dp * rows, n)
    pre = dot(flat, weight_ref[...], TN).T + bias_dense
    hidden, slope = gelu_both(pre)
    hidden = hidden.astype(BF)
    head_weight = heads_ref[...].astype(BF)
    heads = dot(head_weight, hidden) + bias_heads
    position = lax.broadcasted_iota(jnp.int32, (1, n), 1)
    mask = jnp.where(position < lengths_ref[0], 1.0, 0.0)
    d_heads = head_gradient(
        heads, actions_ref[...], adv_ref[...], values_ref[...], logp_ref[...], mask, count, centre, var
    ).astype(BF)
    ones = jnp.ones((8, n), BF)
    grad_heads_ref[...] = dot(d_heads, hidden, NT)
    sum_heads_ref[...] = dot(ones, d_heads, NT)[0:1]
    d_dense = (dot(head_weight, d_heads, TN) * slope).astype(BF)
    sums_ref[0:1, 128 : 128 + hid] = dot(ones, d_dense, NT)[0:1]
    for j in range(n_own):
        d_dense_ref[j] = d_dense[j * cols : (j + 1) * cols]
    outs = []
    for half, ref, far_ref in ((1, send_ref, send_far_ref), (0, keep_ref, keep_far_ref)):
        for k in range(n_own // 4):
            both = [d_dense_ref[own ^ (4 * k + half)], d_dense_ref[own ^ (4 * k + 2 + half)]]
            block = dot(flat, jnp.concatenate(both, axis=0), NT).astype(BF)
            for i in range(n_dp):
                rel = i ^ dp
                spot = (rel % 2) * (n_dp // 2) + rel // 2
                for m in range(2):
                    ref[2 * k + m, spot] = block[i * rows : (i + 1) * rows, m * cols : (m + 1) * cols]
            for m in range(2 * k, 2 * k + 2):
                outs.append(pltpu.make_async_copy(ref.at[m], far_ref.at[m], out_sems.at[len(outs)]))
                outs[-1].start()
    wait_rows(slope_far_ref, slope_ref, slope_sems)
    total = jnp.zeros((64, n), F32)
    for part in range(7):
        span = slice(part * 448, part * 448 + 448)
        d_three = (dot(weight_ref[span, :], d_dense) * slope_ref[part].astype(F32)).astype(BF)
        slope_ref[part] = d_three
        row_copy(slope_ref, d_three_far_ref, slope_sems, part).start()
        back = d_three.astype(F32)
        for c in range(7):
            total = total + back[c * 64 : c * 64 + 64]
    sums_ref[0:1, 0:64] = dot(jnp.ones((8, n), F32), total, NT, HIGH)[0:1]
    sums_ref[0:1, 64:128] = jnp.zeros((1, 64), F32)
    wait_rows(two_far_ref, two_ref, two_sems)
    wait_rows(slope_ref, d_three_far_ref, slope_sems)
    for copy in outs:
        copy.wait()


def dense(
    place, lengths, heads, bias, actions, adv, values, logp, flat, slope_three, act_two,
    pieces, n_dp, n_own, rows,
):
    n = flat.shape[-1]
    hid = n_own * 128
    part = pltpu.HBM((n_own // 2, n_dp, rows, 128), BF)
    arrays = [far(p[0]) for p in pieces]
    small = [heads, bias, actions, adv, values, logp]
    body = functools.partial(
        dense_kernel, places=[p[1] for p in pieces], n_dp=n_dp, n_own=n_own, rows=rows
    )
    return call(
        body,
        [place, lengths] + [far(a) for a in small + [flat, slope_three, act_two]] + arrays,
        [
            pltpu.HBM(flat.shape, BF),
            near(act_two.shape, BF),
            part,
            part,
            jax.ShapeDtypeStruct(heads.shape, F32),
            jax.ShapeDtypeStruct((1, 128 + hid), F32),
            jax.ShapeDtypeStruct((1, heads.shape[0]), F32),
        ],
        in_specs=[smem(), smem()] + [anywhere()] * (9 + len(arrays)),
        out_specs=[anywhere(), vmem(), anywhere(), anywhere()] + [vmem()] * 3,
        scratch=[
            pltpu.VMEM((n_dp, n_own) + arrays[0].shape[1:], BF),
            pltpu.VMEM((n_dp * rows, hid), BF),
            pltpu.VMEM((n_own, 128, n), BF),
            pltpu.VMEM(flat.shape, BF),
            pltpu.VMEM(flat.shape, BF),
            pltpu.VMEM((n_own // 2, n_dp, rows, 128), BF),
            pltpu.VMEM((n_own // 2, n_dp, rows, 128), BF),
        ]
        + [pltpu.VMEM(a.shape, a.dtype) for a in small]
        + [dma(n_dp * n_own), dma(9), dma(7), dma(7), dma(6), dma(n_own)],
        us=10,
        name="dense",
        limit=32,
    )


def conv_three_back_kernel(
    act_ref, d_three_ref, slope_far_ref, one_far_ref, slope_one_far_ref, weight_ref, heads_ref,
    d_two_ref, one_ref, slope_one_ref, pack_ref, sum_ref,
    band_ref, pad_ref, acc_ref, tot_ref, slope_ref, one_sems, slope_one_sems, slope_sems, d_sems,
):
    n = act_ref.shape[-1]
    step = pl.program_id(0)

    def three_row(r):
        inner = pad_ref.at[r + 2, pl.ds(128, 448), :]
        return pltpu.make_async_copy(d_three_ref.at[r], inner, d_sems.at[r])

    @pl.when(step == 0)
    def _():
        for r in range(7):
            three_row(r).start()
        for r in range(11):
            if 2 <= r < 9:
                pad_ref[r, 0:128, :] = jnp.zeros((128, n), BF)
                pad_ref[r, 576:704, :] = jnp.zeros((128, n), BF)
            else:
                pad_ref[r] = jnp.zeros((704, n), BF)
        start_rows(slope_far_ref, slope_ref, slope_sems)
        band_ref[...] = band_back(weight_ref[...], 3, 64, 3)
        acc_ref[...] = jnp.zeros_like(acc_ref)
        tot_ref[...] = jnp.zeros_like(tot_ref)

    @pl.when(step < 7)
    def _():
        three_row(step).wait()

    row_copy(slope_far_ref, slope_ref, slope_sems, step).wait()

    @pl.when(step == 1)
    def _():
        start_rows(one_far_ref, one_ref, one_sems)
        start_rows(slope_one_far_ref, slope_one_ref, slope_one_sems)

    total = tot_ref[...]
    for part in range(3):
        patch = jnp.concatenate(
            [pad_ref[step + a, part * 192 : part * 192 + 320, :] for a in range(3)], axis=0
        )
        rows = slice(part * 192, part * 192 + 192)
        d_two = (dot(band_ref[...], patch) * slope_ref[step, rows, :].astype(F32)).astype(BF)
        d_two_ref[step, rows, :] = d_two
        back = d_two.astype(F32)
        total = total + (back[0:64] + back[64:128]) + back[128:192]
    tot_ref[...] = total

    @pl.when(step < 7)
    def _():
        row = pad_ref[step + 2, 128 : 128 + 448, :]
        second = jnp.concatenate([jnp.zeros((64, n), BF), row[256:448]], axis=0)
        for d_rows, start in ((row[0:256], 0), (second, 3)):
            span = slice(start * 64, start * 64 + 384)
            cells = jnp.concatenate([act_ref[step + a, span, :] for a in range(3)], axis=0)
            acc_ref[...] += dot(d_rows, cells, NT)

    @pl.when(step == 8)
    def _():
        wait_rows(one_far_ref, one_ref, one_sems)
        wait_rows(slope_one_far_ref, slope_one_ref, slope_one_sems)
        for a in range(3):
            out = None
            for c in range(4):
                piece = acc_ref[c * 64 : c * 64 + 64, a * 384 + c * 64 : a * 384 + c * 64 + 192]
                out = piece if out is None else out + piece
            pack_ref[0:64, a * 192 : a * 192 + 192] = out.astype(BF)
        pack_ref[0:64, 576:640] = jnp.zeros((64, 64), BF)
        pack_ref[64:80, 0:512] = heads_ref[0:16, :].astype(BF)
        pack_ref[80:96, 0:512] = jnp.concatenate(
            [heads_ref[16:19, :], jnp.zeros((13, 512), F32)], axis=0
        ).astype(BF)
        pack_ref[64:96, 512:640] = jnp.zeros((32, 128), BF)
        sum_ref[...] = dot(jnp.ones((8, n), F32), tot_ref[...], NT, HIGH)[0:1]


def conv_three_back(d_three, act_two, slope_two, act_one, slope_one, weight, heads):
    n = act_two.shape[-1]
    return call(
        conv_three_back_kernel,
        [held(act_two)] + [far(a) for a in (d_three, slope_two, act_one, slope_one)] + [weight, heads],
        [
            near(act_two.shape, BF),
            near(act_one.shape, BF),
            near(act_one.shape, BF),
            jax.ShapeDtypeStruct((96, 640), BF),
            jax.ShapeDtypeStruct((1, 64), F32),
        ],
        in_specs=[vmem()] + [anywhere()] * 4 + [vmem()] * 2,
        scratch=[
            pltpu.VMEM((192, 960), BF),
            pltpu.VMEM((11, 704, n), BF),
            pltpu.VMEM((256, 1152), F32),
            pltpu.VMEM((64, n), F32),
            pltpu.VMEM(act_two.shape, BF),
            dma(10),
            dma(10),
            dma(9),
            dma(7),
        ],
        grid=9,
        us=9,
        name="conv_three_back",
        limit=16,
    )


def conv_two_back_kernel(
    d_two_ref, act_ref, slope_ref, weight_ref, pack_ref, d_one_ref, grad_ref, sum_ref,
    band_ref, pad_ref, acc_ref, tot_ref,
):
    n = d_one_ref.shape[-1]
    step = pl.program_id(0)

    @pl.when(step == 0)
    def _():
        band_ref[...] = band_back(weight_ref[...], 2, 128, 1)
        pad_ref[0] = jnp.zeros((704, n), BF)
        pad_ref[10] = jnp.zeros((704, n), BF)
        for r in range(1, 10):
            pad_ref[r, 0:64, :] = jnp.zeros((64, n), BF)
            pad_ref[r, 640:704, :] = jnp.zeros((64, n), BF)
        acc_ref[...] = jnp.zeros_like(acc_ref)
        tot_ref[...] = jnp.zeros_like(tot_ref)

    @pl.when(step < 9)
    def _():
        pad_ref[step + 1, 64 : 64 + 576, :] = d_two_ref[step]

    total = tot_ref[...]
    for col in range(10):
        patch = jnp.concatenate(
            [pad_ref[step + a, col * 64 : col * 64 + 128, :] for a in range(2)], axis=0
        )
        d_one = (dot(band_ref[...], patch) * slope_ref[step, col].astype(F32)).astype(BF)
        d_one_ref[step, col] = d_one
        total = total + d_one.astype(F32)
    tot_ref[...] = total

    @pl.when(step < 9)
    def _():
        for part in range(3):
            span = slice(3 * part, 3 * part + 4)
            cells = jnp.concatenate(
                [act_ref[step + a, span].reshape(512, n) for a in range(2)], axis=0
            )
            rows = pad_ref[step + 1, 64 + part * 192 : 64 + part * 192 + 192, :]
            acc_ref[...] += dot(rows, cells, NT)

    @pl.when(step == 9)
    def _():
        for a in range(2):
            out = None
            for c in range(3):
                piece = acc_ref[c * 64 : c * 64 + 64, a * 512 + c * 128 : a * 512 + c * 128 + 256]
                out = piece if out is None else out + piece
            grad_ref[96:160, a * 256 : a * 256 + 256] = out.astype(BF)
        grad_ref[0:96, :] = pack_ref[...]
        grad_ref[96:160, 512:640] = jnp.zeros((64, 128), BF)
        sums = dot(jnp.ones((8, n), F32), tot_ref[...], NT, HIGH)[0:1]
        sum_ref[...] = (sums[:, 0:32] + sums[:, 32:64]) + (sums[:, 64:96] + sums[:, 96:128])


def conv_two_back(d_two, act_one, slope_one, weight, pack):
    n = act_one.shape[-1]
    return call(
        conv_two_back_kernel,
        [held(d_two), held(act_one), held(slope_one), weight, pack],
        [
            near(act_one.shape, BF),
            jax.ShapeDtypeStruct((160, 640), BF),
            jax.ShapeDtypeStruct((1, 32), F32),
        ],
        scratch=[
            pltpu.VMEM((128, 256), BF),
            pltpu.VMEM((11, 704, n), BF),
            pltpu.VMEM((192, 1024), F32),
            pltpu.VMEM((128, n), F32),
        ],
        grid=10,
        us=11,
        name="conv_two_back",
        limit=16,
    )


def conv_one_grad_kernel(
    frames_ref, d_one_ref, cells_in_ref, dense_ref, heads_ref, one_ref, two_ref,
    grad_ref, d_out_ref, cells_ref, acc_ref, sems,
):
    n = d_one_ref.shape[-1]
    step = pl.program_id(0)
    half = pl.num_programs(0)

    slots = fetch_rows(frames_ref, cells_ref, sems, step, half - 1)

    @pl.when(step == 0)
    def _():
        acc_ref[...] = jnp.zeros_like(acc_ref)

    for pair in range(d_one_ref.shape[1] // 2):
        span = slice(pair * 256, pair * 256 + 320)
        cells = jnp.concatenate([cells_ref[slot, span, :] for slot in slots], axis=0)
        rows = d_one_ref[step, 2 * pair : 2 * pair + 2].reshape(256, n)
        acc_ref[...] += dot(rows, cells, NT)

    @pl.when(step == half - 1)
    def _():
        for a in range(2):
            out = None
            for k in range(2):
                for dy in range(2):
                    for dx in range(2):
                        row = ((k * 2 + dy) * 2 + dx) * 32
                        lane = (dy + a) * 320 + (2 * k + dx) * 64
                        piece = acc_ref[row : row + 32, lane : lane + 128]
                        out = piece if out is None else out + piece
            grad_ref[:, a * 128 : a * 128 + 128] = out[0:16]
            grad_ref[:, 256 + a * 128 : 384 + a * 128] = out[16:32]
        grad_ref[:, 512:640] = jnp.zeros((16, 128), F32)
        for k in range(4):
            grad_ref[k : k + 1, 512:640] = dense_ref[0:1, 128 + k * 128 : 256 + k * 128]
        grad_ref[4:5, 512:576] = dense_ref[0:1, 0:64]
        grad_ref[5:6, 512:576] = two_ref[...]
        grad_ref[6:7, 512:544] = one_ref[...]
        grad_ref[7:8, 512:531] = heads_ref[...]


def conv_one_grad(frames, d_one, cells, sums, sum_heads, sum_one, sum_two):
    return pl.pallas_call(
        conv_one_grad_kernel,
        out_shape=(
            jax.ShapeDtypeStruct((16, 640), F32),
            near(d_one.shape, BF),
            near(cells.shape, BF),
        ),
        grid=(d_one.shape[0],),
        in_specs=[anywhere()] + [vmem()] * 6,
        out_specs=(vmem(),) * 3,
        scratch_shapes=[pltpu.VMEM((256, 960), F32), dma(RING)],
        input_output_aliases={1: 1, 2: 2},
        compiler_params=params(16),
        cost_estimate=cost(10),
        name="conv_one_grad",
    )(far(frames), held(d_one), held(cells), sums, sum_heads, sum_one, sum_two)


def frames_back_kernel(*refs, begin, end, total, ahead):
    d_one_ref, weight_ref = refs[:2]
    if ahead:
        frames_ref = refs[2]
        out_ref, d_out_ref, cells_ref, band_ref, rows_ref, sems, cell_sems = refs[-7:]
    else:
        band_ref = weight_ref
        out_ref, d_out_ref, rows_ref, sems = refs[-4:]
    n = rows_ref.shape[-1]
    step = pl.program_id(0)
    row = step + begin
    cells = d_one_ref.shape[1]
    zero = jnp.zeros((32, n), BF)

    if ahead:

        @pl.when(step == 0)
        def _():
            for r in range(5):
                ring_copy(frames_ref, cells_ref, cell_sems, r).start()
            band_ref[...] = band_back(weight_ref[...], 2, 64, 3)

    def slab(at, dy, first, alive):
        parts = []
        for c in range(first, first + 4):
            if c < 0 or c >= 2 * cells:
                parts.append(zero)
            else:
                spot = (dy * 2 + c % 2) * 32
                parts.append(d_one_ref[at, c // 2, spot : spot + 32, :])
        whole = jnp.concatenate(parts, axis=0)
        return whole if alive is None else jnp.where(alive, whole, jnp.zeros_like(whole))

    def make(up, low, at):
        for block in range(7):
            first = 3 * block - 1
            patch = jnp.concatenate([slab(*up[:2], first, up[2]), slab(*low[:2], first, low[2])], axis=0)
            rows_ref[at, block * 192 : block * 192 + 192, :] = dot(band_ref[...], patch).astype(BF)

    def send(at):
        return pltpu.make_async_copy(rows_ref.at[at], out_ref.at[at + 2 * begin], sems.at[at])

    here = row if end < total else jnp.minimum(row, total - 2)
    above = row - 1 if begin > 0 else jnp.maximum(row - 1, 0)
    make(
        (above, 1, None if begin > 0 else row > 0),
        (here, 0, None if end < total else row < total - 1),
        2 * step,
    )
    send(2 * step).start()

    @pl.when(row < total - 1)
    def _():
        make((here, 0, None), (here, 1, None), 2 * step + 1)
        send(2 * step + 1).start()

    @pl.when(step == end - begin - 1)
    def _():
        for at in range(min(2 * end, 2 * total - 1) - 2 * begin):
            send(at).wait()
        if ahead:
            for r in range(5):
                ring_copy(frames_ref, cells_ref, cell_sems, r).wait()


def frames_back(d_one, weight, shape, begin, end, so_far=None, frames=None):
    total = d_one.shape[0] + 1
    ahead = frames is not None
    more = [far(frames)] if ahead else [] if so_far is None else [so_far]
    count = end - begin
    cells = [near((RING,) + shape[1:], BF), jax.ShapeDtypeStruct((192, 256), BF)] if ahead else []
    return call(
        functools.partial(frames_back_kernel, begin=begin, end=end, total=total, ahead=ahead),
        [held(d_one), weight] + more,
        [pltpu.HBM(shape, BF), near(d_one.shape, BF)] + cells,
        in_specs=[vmem(), vmem()] + [anywhere()] * len(more),
        out_specs=[anywhere(), vmem()] + [vmem()] * len(cells),
        scratch=[pltpu.VMEM((2 * count,) + shape[1:], BF), dma(2 * count)] + [dma(5)] * ahead,
        grid=count,
        us=count,
        name="frames_back",
        aliases={0: 1, 2: 0} if so_far is not None else {0: 1},
        limit=16,
    )


def adam_terms(grad, mean, square):
    momentum = BETA * mean + (1.0 - BETA) * grad
    variance = BETA * square + (1.0 - BETA) * grad * grad
    fix = 1.0 - BETA**STEP
    direction = momentum / fix / (jnp.sqrt(variance / fix) + EPSILON)
    return (momentum, variance, direction)


def split(x):
    top = x.astype(BF)
    return top, (x - top.astype(F32)).astype(BF)


def dot3(a, b, dims=NN):
    a_top, a_low = split(a)
    b_top, b_low = split(b)
    if dims == TN:
        return dot(a_top, b_top, dims) + (dot(a_top, b_low, dims) + dot(a_low, b_top, dims))
    rows = a.shape[0]
    both = dot(jnp.concatenate([a_top, a_low], axis=0), b_top, dims)
    return both[:rows] + (both[rows:] + dot(a_top, b_low, dims))


def dot2(a, b, dims=NN):
    rows = a.shape[0]
    both = dot(jnp.concatenate(split(a), axis=0), b, dims)
    return both[:rows] + both[rows:]


def turned_step(weight, grad, mean, square, left, right):
    rate = RATE / math.sqrt(weight.shape[1])
    left = left.astype(BF)
    turned = dot2(dot3(right, grad, TN), left)
    momentum, variance, direction = adam_terms(turned, mean, square)
    back = dot2(dot3(right, direction), left, NT)
    return momentum, variance, weight - rate * back


def steps_kernel(*refs, spots):
    count = len(spots)
    packs = 1 + max(spot[0] for spot in spots)
    ins, outs = refs[packs : packs + 5 * count], refs[packs + 5 * count :]
    for w, (pack, row, rows, cols) in enumerate(spots):
        grad = refs[pack][row : row + rows, 0:cols].astype(F32)
        if rows == 16:
            grad = jnp.concatenate([grad, refs[pack][row : row + rows, cols : 2 * cols]], axis=0)
        weight, mean, square, left, right = [ref[...] for ref in ins[5 * w : 5 * w + 5]]
        results = (grad,) + turned_step(weight, grad, mean, square, left, right)
        for ref, value in zip(outs[4 * w : 4 * w + 4], results):
            ref[...] = value


def steps(packs, spots, groups):
    arrays = []
    shapes = []
    for weight, mean, square, left, right in groups:
        arrays += [weight.T, mean.T, square.T, left, right]
        shapes += [jax.ShapeDtypeStruct(weight.shape[::-1], F32)] * 4
    return pl.pallas_call(
        functools.partial(steps_kernel, spots=spots),
        out_shape=tuple(shapes),
        in_specs=[vmem()] * (len(packs) + len(arrays)),
        out_specs=(vmem(),) * len(shapes),
        compiler_params=params(32),
        cost_estimate=cost(5),
        name="steps",
    )(*packs, *arrays)


def dense_step_kernel(*refs, rate):
    weight_ref, mean_ref, square_ref, block_ref = refs[:4]
    grad_ref, mom_ref, var_ref, new_ref = refs[-4:]
    grad = None
    for ref in refs[4:-4]:
        part = ref[...].astype(F32)
        grad = part if grad is None else grad + part
    grad_ref[...] = grad
    turned = dot3(grad, block_ref[0])
    momentum, variance, direction = adam_terms(turned, mean_ref[...], square_ref[...])
    mom_ref[...] = momentum
    var_ref[...] = variance
    new_ref[...] = weight_ref[...] - rate * dot3(direction, block_ref[0], NT)


def dense_step(weight, mean, square, block, parts, rate):
    shape = jax.ShapeDtypeStruct(weight.shape, F32)
    return pl.pallas_call(
        functools.partial(dense_step_kernel, rate=rate),
        out_shape=(shape,) * 4,
        in_specs=[vmem()] * (4 + len(parts)),
        out_specs=(vmem(),) * 4,
        compiler_params=params(),
        cost_estimate=cost(3),
        name="dense_step",
    )(weight, mean, square, block, *parts)


def swap(x, axis, bit, size):
    return lax.ppermute(x, axis, [(i, i ^ bit) for i in range(size)])


def bits_of(size):
    return [1 << b for b in range(size.bit_length() - 1)]


def fence(*values):
    leaves, tree = jax.tree.flatten(values)
    return jax.tree.unflatten(tree, lax.optimization_barrier(tuple(leaves)))


def add_low(*terms):
    total = terms[0].astype(F32)
    for term in terms[1:]:
        total = total + term.astype(F32)
    return total.astype(BF)


def plain_gather(piece, n_dp, n_own):
    pieces = piece[None]
    spots = [(0, 0)]
    for bit in bits_of(n_dp):
        pieces = jnp.concatenate([pieces, swap(pieces, "dp", bit, n_dp)], axis=0)
        spots = spots + [(i ^ bit, j) for i, j in spots]
    for bit in bits_of(n_own):
        pieces = jnp.concatenate([pieces, swap(pieces, "own", bit, n_own)], axis=0)
        spots = spots + [(i, j ^ bit) for i, j in spots]
    return [(pieces, spots)]


def plain_scatter(keep, send, n_dp, n_own):
    block = add_low(keep, swap(send, "own", 1, n_own))
    bit = n_own // 2
    while bit > 1:
        half = block.shape[0] // 2
        block = add_low(block[:half], swap(block[half:], "own", bit, n_own))
        bit //= 2
    block = block[0]
    for bit in [1] + bits_of(n_dp)[:0:-1]:
        half = block.shape[0] // 2
        block = add_low(block[:half], swap(block[half:], "dp", bit, n_dp))
    return [block[0]]


def shards(
    frames, actions, dones, lengths, rewards, old_values, old_logp,
    conv_first, conv_second, conv_third, dense_hidden, dense_heads, bias_all,
    mean_first, mean_second, mean_third, mean_dense, mean_heads, mean_bias,
    square_first, square_second, square_third, square_dense, square_heads, square_bias,
    left_first, right_first, left_second, right_second, left_third, right_third,
    right_dense, left_heads, right_heads, *, n_dp, n_own,
):
    tokens, grid = frames.shape[0], frames.shape[1]
    planes = frames.shape[3]
    rows = dense_hidden.shape[0]
    tuned = (n_dp, n_own) == (8, 4)
    own_swap = lambda x, bit: swap(x, "own", bit, n_own)
    dp_swap = lambda x, bit: swap(x, "dp", bit, n_dp)
    place = jnp.stack([lax.axis_index("dp"), lax.axis_index("own")]).astype(jnp.int32)
    bias_row = bias_all.reshape(1, -1)
    cells = frames.transpose(1, 2, 3, 0).reshape(grid, grid * planes, tokens)
    adv, piece, ring = first(lengths, dones, rewards, old_values, dense_hidden, cells)

    if tuned:
        along_z = [dp_swap(piece, 2 * k) for k in (1, 2, 3)]
    act_one, slope_one, _ = conv_one(cells, conv_first.T, bias_row, ring)
    if tuned:
        spots = [(2 * k, 0) for k in range(4)]
        act_one, slope_one, piece, along_z = fence(act_one, slope_one, piece, along_z)
        column = jnp.stack([piece] + along_z)
        act_one, slope_one, column = fence(act_one, slope_one, column)
        by_x, by_y = dp_swap(column, 1), own_swap(column, 2)
    else:
        pieces = plain_gather(piece, n_dp, n_own)
    act_two, slope_two, act_one_far, slope_one_far = conv_two(act_one, slope_one, conv_second.T, bias_row)
    if tuned:
        act_two, slope_two, column, by_x, by_y = fence(act_two, slope_two, column, by_x, by_y)
        halves = (by_x[0:2], by_y[2:4])
        plane = jnp.concatenate([column, by_x, by_y])
        act_two, slope_two, halves, plane = fence(act_two, slope_two, halves, plane)
        corner = [own_swap(halves[0], 2), dp_swap(halves[1], 1)]
        other = own_swap(plane, 1)
    flat, slope_three, act_two_far, slope_two_far = conv_three(act_two, slope_two, conv_third.T, bias_row)
    if tuned:
        flat, corner = fence(flat, corner)
        corner = jnp.concatenate(corner)
        plane_spots = [(i ^ x, j ^ y) for x, y in ((0, 0), (1, 0), (0, 2)) for i, j in spots]
        corner_spots = [(i ^ 1, j ^ 2) for i, j in spots]
        pieces = [(plane, plane_spots), (corner, corner_spots)]
        pieces += [
            (other, [(i, j ^ 1) for i, j in plane_spots]),
            (own_swap(corner, 1), [(i, j ^ 1) for i, j in corner_spots]),
        ]
    d_three, act_two, keep, send, here_heads, sums, sum_heads = dense(
        place, lengths, dense_heads.T, bias_row, actions, adv, old_values, old_logp,
        flat, slope_three, act_two_far, pieces, n_dp, n_own, rows,
    )

    came = own_swap(send, 1) if tuned else None
    d_two, act_one, slope_one, pack, sum_two = conv_three_back(
        d_three, act_two, slope_two_far, act_one_far, slope_one_far, conv_third.T, here_heads
    )
    if tuned:
        d_two, act_one, slope_one, keep, came = fence(d_two, act_one, slope_one, keep, came)
        block = add_low(keep, came)
        ends = (block[1, 4:6], block[1, 6:8])
        d_two, act_one, slope_one, block, ends = fence(d_two, act_one, slope_one, block, ends)
        by_y, by_x = own_swap(ends[0], 2), dp_swap(ends[1], 1)
    d_one, pack, sum_one = conv_two_back(d_two, act_one, slope_one, conv_second.T, pack)

    shape = cells.shape
    side = lax.axis_index("own") % 2
    rows_half = pack.shape[0] // 2
    if tuned:
        d_one, pack, block, by_x, by_y = fence(d_one, pack, block, by_x, by_y)
        side_x = jnp.concatenate([add_low(block[0, 4:6], by_y), block[0, 6:8]])
        side_y = jnp.concatenate([block[1, 0:2], add_low(block[1, 2:4], by_x)])
        block = block[0, 0:4]
    else:
        side_x = side_y = block = jnp.zeros((8, 128), BF)
    half = lax.dynamic_slice_in_dim(pack, side * rows_half, rows_half)
    gone = lax.dynamic_slice_in_dim(pack, (1 - side) * rows_half, rows_half)
    d_one, half, gone, block, side_x, side_y = fence(d_one, half, gone, block, side_x, side_y)
    if tuned:
        by_x, by_y = dp_swap(side_x, 1), own_swap(side_y, 2)
    came = own_swap(gone, 1)
    cuts = (0, 2, 5, 8, grid // 2 + 1)
    back, d_one, ring, band = frames_back(d_one, conv_first.T, shape, cuts[0], cuts[1], frames=cells)
    back, d_one, ring, half, came = fence(back, d_one, ring, half, came)
    half = add_low(half, came)
    back, d_one, ring, half = fence(back, d_one, ring, half)
    far_bits = bits_of(n_dp)[:0:-1]
    came = dp_swap(half, far_bits[0])
    pack_one, d_one, _ = conv_one_grad(cells, d_one, ring, sums, sum_heads, sum_one, sum_two)
    if tuned:
        pack_one, d_one, block, by_x, by_y = fence(pack_one, d_one, block, by_x, by_y)
        block = add_low(block, by_x, by_y)
    pack_one, d_one, half, came = fence(pack_one, d_one, half, came)

    half = add_low(half, came)
    pack_one, d_one, half, block = fence(pack_one, d_one, half, block)
    came_one = dp_swap(pack_one, far_bits[0])
    came = own_swap(half, 2)
    if tuned:
        parts = [block[0]] + [dp_swap(block[k], 2 * k) for k in (1, 2, 3)]
    else:
        parts = plain_scatter(keep, send, n_dp, n_own)
    back, d_one = frames_back(d_one, band, shape, cuts[1], cuts[2], back)
    back, d_one, half, came, pack_one, came_one = fence(back, d_one, half, came, pack_one, came_one)

    def join(pack, pack_one):
        return jnp.concatenate([pack.astype(BF), *split(pack_one)])

    def part(both):
        count = pack_one.shape[0]
        low = both[rows_half:].astype(F32)
        return both[:rows_half].astype(F32), low[:count] + low[count:]

    def add_up(both, came):
        a, b = part(both), part(came)
        return a[0] + b[0], a[1] + b[1]

    both = join(add_low(half, came), pack_one + came_one)
    back, d_one, both = fence(back, d_one, both)
    more = [1] + far_bits[1:]
    came = dp_swap(both, more[0])
    back, d_one = frames_back(d_one, band, shape, cuts[2], cuts[3], back)
    back, d_one, both, came = fence(back, d_one, both, came)
    both = join(*add_up(both, came))
    back, d_one, both = fence(back, d_one, both)
    came = dp_swap(both, more[1])
    back, d_one = frames_back(d_one, band, shape, cuts[3], cuts[4], back)
    for bit in more[2:]:
        both = join(*add_up(both, came))
        came = dp_swap(both, bit)
    back, parts, both, came = fence(back, parts, both, came)
    both = join(*add_up(both, came))
    parts, both = fence(parts, both)
    came = own_swap(both, 1)
    frames_grad = back.reshape(grid, grid, planes, tokens).transpose(3, 0, 1, 2)
    grad_dense, *wide_step = dense_step(
        dense_hidden, mean_dense, square_dense, right_dense, parts, RATE / math.sqrt(rows * n_dp)
    )
    grad_dense, both, came = fence(grad_dense, both, came)
    pack_one = add_up(both, came)[1]
    halves = (both[:rows_half], came[:rows_half])
    pack = jnp.concatenate([jnp.where(side == 0, *halves), jnp.where(side == 0, *halves[::-1])])
    pack_one, pack = fence(pack_one, pack)
    one = own_swap(pack_one, 2)
    late = steps(
        [pack],
        [(0, 0, 64, 576), (0, 64, 19, 512), (0, 96, 64, 512)],
        [
            (conv_third, mean_third, square_third, left_third, right_third),
            (dense_heads, mean_heads, square_heads, left_heads, right_heads),
            (conv_second, mean_second, square_second, left_second, right_second),
        ],
    )
    late, pack_one, one = fence(late, pack_one, one)
    pack_one = pack_one + one
    third, top, second = late[0:4], late[4:8], late[8:12]
    first_step = steps(
        [pack_one],
        [(0, 0, 16, 256)],
        [(conv_first, mean_first, square_first, left_first, right_first)],
    )
    line = pack_one[:, 512:]
    grad_bias = jnp.concatenate(
        [line[6, 0:32], line[5, 0:64], line[4, 0:64], line[0], line[1], line[2], line[3], line[7, 0:19]]
    )
    mom_bias, var_bias, bias_dir = adam_terms(grad_bias, mean_bias, square_bias)
    new_bias = bias_all - BIAS_RATE * bias_dir
    outs = [frames_grad]
    wide_step = [grad_dense] + list(wide_step)
    for index, bias_part in enumerate((grad_bias, mom_bias, var_bias, new_bias)):
        outs += [first_step[index].T, second[index].T, third[index].T, wide_step[index], top[index].T, bias_part]
    return tuple(outs)


def solution(mesh):
    n_dp, n_own = mesh.shape["dp"], mesh.shape["own"]
    both = ("dp", "own")
    rep = P()
    in_specs = (
        (P(both, None, None, None), P(both, None), P(both, None), P(both))
        + (P(both, None),) * 3
        + (rep, rep, rep, P("dp", "own"), rep, rep) * 3
        + (rep,) * 6
        + (P("own", None, None), rep, rep)
    )
    out_specs = (P(both, None, None, None),) + (rep, rep, rep, P("dp", "own"), rep, rep) * 4
    body = functools.partial(shards, n_dp=n_dp, n_own=n_own)
    return jax.shard_map(body, mesh=mesh, in_specs=in_specs, out_specs=out_specs, check_vma=False)
```

```python
import functools
import math

import jax
import jax.numpy as jnp
from jax import lax
from jax.experimental import pallas as pl
from jax.experimental.pallas import tpu as pltpu
from jax.sharding import PartitionSpec as P

STEP = 10
GAMMA = 0.99
LAMBDA = 0.95
CLIP = 0.1
ENTROPY_COEF = 0.01
VALUE_COEF = 0.5
BETA = 0.5
EPSILON = 1e-08
RATE = 1.0
BIAS_RATE = 0.1
HIGH = lax.Precision.HIGHEST
ROOT = math.sqrt(2.0 / math.pi)
CUBE = 0.044715
BF = jnp.bfloat16
F32 = jnp.float32
MIB = 2**20

NN = (((1,), (0,)), ((), ()))
NT = (((1,), (1,)), ((), ()))
TN = (((0,), (0,)), ((), ()))


def dot(a, b, dims=NN, precision=None):
    return lax.dot_general(a, b, dims, precision=precision, preferred_element_type=F32)


def params(limit=32, **more):
    return pltpu.CompilerParams(vmem_limit_bytes=limit * MIB, **more)


def cost(us):
    return pl.CostEstimate(flops=int(us * 1e9), bytes_accessed=0, transcendentals=0)


def near(shape, dtype):
    return pltpu.VMEM(shape, dtype)


def held(x):
    return pltpu.with_memory_space_constraint(x, pltpu.VMEM)


def far(x):
    return pltpu.with_memory_space_constraint(x, pltpu.HBM)


def vmem():
    return pl.BlockSpec(memory_space=pltpu.VMEM)


def smem():
    return pl.BlockSpec(memory_space=pltpu.SMEM)


def anywhere():
    return pl.BlockSpec(memory_space=pl.ANY)


def row_copy(source, target, sems, r):
    return pltpu.make_async_copy(source.at[r], target.at[r], sems.at[r])


def start_rows(source, target, sems):
    for r in range(source.shape[0]):
        row_copy(source, target, sems, r).start()


def wait_rows(source, target, sems):
    for r in range(source.shape[0]):
        row_copy(source, target, sems, r).wait()


def call(body, ins, outs, in_specs=None, out_specs=None, scratch=(), grid=None, us=5, name=None, aliases=None, limit=24):
    more = {} if grid is None else {"grid": (grid,)}
    return pl.pallas_call(
        body,
        out_shape=tuple(outs),
        in_specs=list(in_specs or [vmem()] * len(ins)),
        out_specs=tuple(out_specs or [vmem()] * len(outs)),
        scratch_shapes=list(scratch),
        input_output_aliases=aliases or {},
        compiler_params=params(limit),
        cost_estimate=cost(us),
        name=name,
        **more,
    )(*ins)


def dma(count):
    return pltpu.SemaphoreType.DMA((count,))


def gelu_both(x):
    x2 = x * x
    up = 1.0 + jnp.tanh(x * (ROOT + (ROOT * CUBE) * x2))
    h = 0.5 * x
    bend = h * (ROOT + (3.0 * ROOT * CUBE) * x2)
    return h * up, up * (0.5 + bend * (2.0 - up))


def wide(line, rows, n):
    k = line.shape[1]
    column = jnp.broadcast_to(line, (128, k)).T
    tall = jnp.concatenate([column] * (rows // k), axis=0) if rows > k else column
    return jnp.concatenate([tall] * (n // 128), axis=1)


def lanes(parts):
    return jnp.concatenate([p for p in parts if p.shape[1] > 0], axis=1)


def band_forward(w, kernel, feats, count):
    ch = w.shape[0]
    run = kernel * feats
    rows = []
    for j in range(count):
        parts = []
        for a in range(kernel):
            parts.append(jnp.zeros((ch, j * feats), F32))
            parts.append(w[:, a * run : (a + 1) * run])
            parts.append(jnp.zeros((ch, (count - 1 - j) * feats), F32))
        rows.append(lanes(parts))
    return jnp.concatenate(rows, axis=0).astype(BF)


def band_square(w, feats):
    ch = w.shape[0]
    rows = []
    for dy in range(2):
        for dx in range(2):
            lead = (dy * 3 + dx) * feats
            rows.append(
                lanes(
                    [
                        jnp.zeros((ch, lead), F32),
                        w[:, : 2 * feats],
                        jnp.zeros((ch, feats), F32),
                        w[:, 2 * feats :],
                        jnp.zeros((ch, 4 * feats - lead), F32),
                    ]
                )
            )
    return jnp.concatenate(rows, axis=0).astype(BF)


def band_back(w, kernel, feats, count):
    ch = w.shape[0]
    turned = w.T
    zero = jnp.zeros((feats, ch), F32)
    rows = []
    for i in range(count):
        parts = []
        for a in range(kernel):
            for j in range(kernel + count - 1):
                b = j - i
                if 0 <= b < kernel:
                    spot = ((kernel - 1 - a) * kernel + (kernel - 1 - b)) * feats
                    parts.append(turned[spot : spot + feats])
                else:
                    parts.append(zero)
        rows.append(lanes(parts))
    return jnp.concatenate(rows, axis=0).astype(BF)


def first_kernel(
    lengths_ref, dones_far_ref, rewards_far_ref, values_far_ref, weight_far_ref, frames_ref,
    adv_ref, piece_ref, cells_ref, dones_ref, rewards_ref, values_ref, weight_ref, sems, small_sems,
):
    near_refs = (dones_ref, rewards_ref, values_ref, weight_ref)
    far_refs = (dones_far_ref, rewards_far_ref, values_far_ref, weight_far_ref)
    small = [pltpu.make_async_copy(a, b, small_sems.at[k]) for k, (a, b) in enumerate(zip(far_refs, near_refs))]
    for copy in small:
        copy.start()
    for r in range(5):
        ring_copy(frames_ref, cells_ref, sems, r).start()
    for copy in small:
        copy.wait()
    n = rewards_ref.shape[1]
    length = lengths_ref[0]
    position = lax.broadcasted_iota(jnp.int32, (8, n), 1)
    live = position < length
    mask = jnp.where(live, 1.0, 0.0)
    next_live = jnp.where(position + 1 < length, 1.0, 0.0)
    values = jnp.broadcast_to(values_ref[...], (8, n))
    rewards = jnp.broadcast_to(rewards_ref[...], (8, n))
    going = 1.0 - jnp.broadcast_to(dones_ref[...], (8, n)).astype(F32)

    def ahead(v, k, fill):
        return jnp.concatenate([v[:, k:], jnp.full((8, k), fill, F32)], axis=1)

    delta = rewards + GAMMA * going * ahead(values, 1, 0.0) * next_live - values
    total = mask * delta
    carry = mask * (GAMMA * LAMBDA) * going
    k = 1
    while k < n:
        total = total + carry * ahead(total, k, 0.0)
        carry = carry * ahead(carry, k, 0.0)
        k *= 2
    adv_ref[...] = total[0:1]
    count = jnp.sum(mask, axis=1, keepdims=True)
    mean = jnp.sum(mask * total, axis=1, keepdims=True) / count
    spread = jnp.sum(mask * (total - mean) ** 2, axis=1, keepdims=True)
    lane = lax.broadcasted_iota(jnp.int32, (8, 128), 1)
    stat = jnp.where(lane == 0, count, jnp.where(lane == 1, mean, jnp.where(lane == 2, spread, 0.0)))
    top = stat.astype(BF).astype(F32)
    mid = (stat - top).astype(BF).astype(F32)
    low = ((stat - top) - mid).astype(BF).astype(F32)
    line = lax.broadcasted_iota(jnp.int32, (8, 128), 0)
    terms = jnp.where(line == 0, top, jnp.where(line == 1, mid, jnp.where(line == 2, low, 0.0)))
    rows = weight_ref.shape[0]
    tail = piece_ref.shape[0] - 16
    lead = max(rows - tail, 0)
    if tail > rows:
        piece_ref[rows // 16 * 16 : tail, :] = jnp.zeros((tail - rows // 16 * 16, 128), BF)
    piece_ref[0 : min(rows, tail), :] = weight_ref[0 : min(rows, tail), :].astype(BF)
    last = [weight_ref[rows - lead :, :]] if lead else []
    last += [jnp.zeros((8 - lead, 128), F32)] if lead < 8 else []
    piece_ref[tail:, :] = jnp.concatenate(last + [terms], axis=0).astype(BF)
    for r in range(5):
        ring_copy(frames_ref, cells_ref, sems, r).wait()


def first(lengths, dones, rewards, old_values, weight, frames):
    n = rewards.shape[1]
    rows = -(-weight.shape[0] // 16) * 16
    rows += 16 if weight.shape[0] - (rows - 16) > 8 else 0
    small = [dones, rewards, old_values, weight]
    return pl.pallas_call(
        first_kernel,
        out_shape=(
            jax.ShapeDtypeStruct((1, n), F32),
            jax.ShapeDtypeStruct((rows, 128), BF),
            near((RING,) + frames.shape[1:], BF),
        ),
        in_specs=[smem()] + [anywhere()] * 5,
        out_specs=(vmem(),) * 3,
        scratch_shapes=[pltpu.VMEM(a.shape, a.dtype) for a in small] + [dma(5), dma(4)],
        compiler_params=params(16),
        cost_estimate=cost(3),
        name="first",
    )(lengths, *[far(a) for a in small], far(frames))


RING = 10


def ring_copy(frames_ref, cells_ref, sems, r):
    slot = r % RING if isinstance(r, int) else lax.rem(r, RING)
    return pltpu.make_async_copy(frames_ref.at[r], cells_ref.at[slot], sems.at[slot])


def fetch_rows(frames_ref, cells_ref, sems, step, last):
    @pl.when(step < last)
    def _():
        for a in range(5, 9):
            ring_copy(frames_ref, cells_ref, sems, 4 * step + a).start()

    @pl.when(step >= 1)
    def _():
        for a in range(1, 5):
            ring_copy(frames_ref, cells_ref, sems, 4 * step + a).wait()

    return [lax.rem(4 * step + a, RING) for a in range(5)]


def conv_one_kernel(
    frames_ref, weight_ref, bias_ref, cells_in_ref, act_ref, slope_ref, cells_ref, band_ref, wide_ref, sems
):
    n = act_ref.shape[-1]
    half = act_ref.shape[0]
    step = pl.program_id(0)

    slots = fetch_rows(frames_ref, cells_ref, sems, step, half // 2 - 1)

    @pl.when(step == 0)
    def _():
        band_ref[...] = band_square(weight_ref[...], 64)
        wide_ref[...] = wide(bias_ref[:, 0:32], 128, n)

    for q in range(2):
        for col in range(half):
            span = slice(col * 128, col * 128 + 192)
            patch = jnp.concatenate([cells_ref[slot, span, :] for slot in slots[2 * q : 2 * q + 3]], axis=0)
            act, slope = gelu_both(dot(band_ref[...], patch) + wide_ref[...])
            act_ref[2 * step + q, col] = act.astype(BF)
            slope_ref[2 * step + q, col] = slope.astype(BF)


def conv_one(frames, weight, bias, cells):
    grid, _, n = frames.shape
    half = grid // 2
    shape = (half, half, 128, n)
    return call(
        conv_one_kernel,
        [far(frames), weight, bias, held(cells)],
        [near(shape, BF), near(shape, BF), near(cells.shape, BF)],
        in_specs=[anywhere()] + [vmem()] * 3,
        scratch=[pltpu.VMEM((128, 576), BF), pltpu.VMEM((128, n), F32), dma(RING)],
        grid=half // 2,
        us=12,
        name="conv_one",
        aliases={3: 2},
        limit=16,
    )


def conv_two_kernel(
    one_ref, slope_one_ref, weight_ref, bias_ref, act_ref, slope_ref, one_far_ref, slope_one_far_ref,
    band_ref, wide_ref, sems, slope_sems,
):
    n = act_ref.shape[-1]
    step = pl.program_id(0)

    @pl.when(step == 0)
    def _():
        start_rows(one_ref, one_far_ref, sems)
        start_rows(slope_one_ref, slope_one_far_ref, slope_sems)
        band_ref[...] = band_forward(weight_ref[...], 2, 128, 3)
        wide_ref[...] = wide(bias_ref[:, 32:96], 192, n)

    for row in range(9):
        for part in range(3):
            span = slice(3 * part, 3 * part + 4)
            patch = jnp.concatenate(
                [one_ref[row + a, span].reshape(512, n) for a in range(2)], axis=0
            )
            act, slope = gelu_both(dot(band_ref[...], patch) + wide_ref[...])
            rows = slice(part * 192, part * 192 + 192)
            act_ref[row, rows, :] = act.astype(BF)
            slope_ref[row, rows, :] = slope.astype(BF)

    @pl.when(step == 0)
    def _():
        wait_rows(one_ref, one_far_ref, sems)
        wait_rows(slope_one_ref, slope_one_far_ref, slope_sems)


def conv_two(act_one, slope_one, weight, bias):
    n = act_one.shape[-1]
    shape = (9, 576, n)
    return call(
        conv_two_kernel,
        [held(act_one), held(slope_one), weight, bias],
        [near(shape, BF)] * 2 + [pltpu.HBM(act_one.shape, BF)] * 2,
        out_specs=[vmem(), vmem(), anywhere(), anywhere()],
        scratch=[pltpu.VMEM((192, 1024), BF), pltpu.VMEM((192, n), F32), dma(10), dma(10)],
        grid=1,
        us=7,
        name="conv_two",
        limit=16,
    )


def conv_three_kernel(
    two_ref, slope_two_ref, weight_ref, bias_ref,
    flat_far_ref, slope_far_ref, two_far_ref, slope_two_far_ref,
    band_ref, wide_ref, flat_ref, slope_ref, two_sems, slope_two_sems, flat_sems, slope_sems,
):
    n = two_ref.shape[-1]
    start_rows(two_ref, two_far_ref, two_sems)
    start_rows(slope_two_ref, slope_two_far_ref, slope_two_sems)
    band_ref[...] = band_forward(weight_ref[...], 3, 64, 4)
    wide_ref[...] = wide(bias_ref[:, 96:160], 256, n)
    for row in range(7):
        for drop, start in ((0, 0), (1, 3)):
            patch = jnp.concatenate(
                [two_ref[row + a, start * 64 : start * 64 + 384, :] for a in range(3)], axis=0
            )
            pre = dot(band_ref[drop * 64 :, :], patch) + wide_ref[drop * 64 :, :]
            act, slope = gelu_both(pre)
            rows = slice((start + drop) * 64, (start + 4) * 64)
            flat_ref[row, rows, :] = act.astype(BF)
            slope_ref[row, rows, :] = slope.astype(BF)
        row_copy(flat_ref, flat_far_ref, flat_sems, row).start()
        row_copy(slope_ref, slope_far_ref, slope_sems, row).start()
    wait_rows(two_ref, two_far_ref, two_sems)
    wait_rows(slope_two_ref, slope_two_far_ref, slope_two_sems)
    wait_rows(flat_ref, flat_far_ref, flat_sems)
    wait_rows(slope_ref, slope_far_ref, slope_sems)


def conv_three(act_two, slope_two, weight, bias):
    n = act_two.shape[-1]
    shape = (7, 448, n)
    out, two = pltpu.HBM(shape, BF), pltpu.HBM(act_two.shape, BF)
    return call(
        conv_three_kernel,
        [held(act_two), held(slope_two), weight, bias],
        [out, out, two, two],
        out_specs=[anywhere()] * 4,
        scratch=[
            pltpu.VMEM((256, 1152), BF),
            pltpu.VMEM((256, n), F32),
            pltpu.VMEM(shape, BF),
            pltpu.VMEM(shape, BF),
            dma(9),
            dma(9),
            dma(7),
            dma(7),
        ],
        us=6,
        name="conv_three",
        limit=16,
    )


def head_gradient(heads, actions, adv, values, old_logp, mask, count, centre, var):
    rows, n = heads.shape
    acts = rows - 1
    norm_adv = (adv - centre) * lax.rsqrt(var + 1e-05)
    returns = adv + values
    index = lax.broadcasted_iota(jnp.int32, (rows, n), 0)
    is_logit = index < acts
    top = jnp.max(jnp.where(is_logit, heads, -jnp.inf), axis=0, keepdims=True)
    shifted = heads - top
    grown = jnp.where(is_logit, jnp.exp(jnp.where(is_logit, shifted, 0.0)), 0.0)
    total = jnp.sum(grown, axis=0, keepdims=True)
    logp_all = jnp.where(is_logit, shifted - jnp.log(total), 0.0)
    prob = jnp.where(is_logit, jnp.exp(logp_all), 0.0)
    chosen = jnp.where(index == actions, 1.0, 0.0)
    logp = jnp.sum(logp_all * chosen, axis=0, keepdims=True)
    plogp = jnp.sum(prob * logp_all, axis=0, keepdims=True)
    value = jnp.sum(jnp.where(index == acts, heads, 0.0), axis=0, keepdims=True)
    ratio = jnp.exp(logp - old_logp)
    bent = jnp.tanh((ratio - 1.0) / CLIP)
    soft = 1.0 + CLIP * bent
    plain = ratio * norm_adv
    clipped = soft * norm_adv
    share = jnp.where(plain < clipped, 1.0, jnp.where(plain > clipped, 0.0, 0.5))
    by_ratio = -norm_adv * (share + (1.0 - share) * (1.0 - bent * bent))
    scale = mask / count
    by_logp = by_ratio * ratio
    by_logit = by_logp * (chosen - prob) + ENTROPY_COEF * prob * (logp_all - plogp)
    by_value = VALUE_COEF * (value - returns)
    return jnp.where(is_logit, by_logit, by_value) * scale


def dense_kernel(*refs, places, n_dp, n_own, rows):
    place_ref, lengths_ref = refs[:2]
    small_far_refs, (flat_far_ref, slope_far_ref, two_far_ref) = refs[2:8], refs[8:11]
    piece_refs = refs[11 : 11 + len(places)]
    (
        d_three_far_ref, two_ref, keep_far_ref, send_far_ref, grad_heads_ref, sums_ref, sum_heads_ref,
        blocks_ref, weight_ref, d_dense_ref, flat_ref, slope_ref, keep_ref, send_ref, *small_refs,
        sems, two_sems, flat_sems, slope_sems, small_sems, out_sems,
    ) = refs[11 + len(places) :]
    heads_ref, bias_ref, actions_ref, adv_ref, values_ref, logp_ref = small_refs
    n = flat_ref.shape[-1]
    cols = 128
    dp, own = place_ref[0], place_ref[1]
    stats = []
    copies = []
    for ref, spots in zip(piece_refs, places):
        for k, (i, j) in enumerate(spots):
            copies.append(
                pltpu.make_async_copy(ref.at[k], blocks_ref.at[i ^ dp, j ^ own], sems.at[len(copies)])
            )
    for k in range(6):
        copies.append(pltpu.make_async_copy(small_far_refs[k], small_refs[k], small_sems.at[k]))
    for copy in copies:
        copy.start()
    start_rows(flat_far_ref, flat_ref, flat_sems)
    for copy in copies:
        copy.wait()
    start_rows(slope_far_ref, slope_ref, slope_sems)
    start_rows(two_far_ref, two_ref, two_sems)
    for i in range(n_dp):
        for j in range(n_own):
            tail = blocks_ref[i, j, blocks_ref.shape[2] - 16 :].astype(F32)
            stats.append((tail[8:9] + tail[9:10]) + tail[10:11])
    stats = jnp.concatenate(stats, axis=0)
    each = stats[:, 0:1]
    count = jnp.sum(each, axis=0, keepdims=True)
    centre = jnp.sum(each * stats[:, 1:2], axis=0, keepdims=True) / count
    gap = stats[:, 1:2] - centre
    var = jnp.sum(stats[:, 2:3] + each * gap * gap, axis=0, keepdims=True) / count
    for i in range(n_dp):
        for j in range(n_own):
            weight_ref[i * rows : (i + 1) * rows, j * cols : (j + 1) * cols] = blocks_ref[i, j, 0:rows]
    hid = n_own * cols
    bias_dense = wide(bias_ref[:, 160 : 160 + hid], hid, n)
    bias_heads = wide(bias_ref[:, 160 + hid : 160 + hid + 19], 19, n)
    wait_rows(flat_far_ref, flat_ref, flat_sems)
    flat = flat_ref[...].reshape(n_dp * rows, n)
    pre = dot(flat, weight_ref[...], TN).T + bias_dense
    hidden, slope = gelu_both(pre)
    hidden = hidden.astype(BF)
    head_weight = heads_ref[...].astype(BF)
    heads = dot(head_weight, hidden) + bias_heads
    position = lax.broadcasted_iota(jnp.int32, (1, n), 1)
    mask = jnp.where(position < lengths_ref[0], 1.0, 0.0)
    d_heads = head_gradient(
        heads, actions_ref[...], adv_ref[...], values_ref[...], logp_ref[...], mask, count, centre, var
    ).astype(BF)
    ones = jnp.ones((8, n), BF)
    grad_heads_ref[...] = dot(d_heads, hidden, NT)
    sum_heads_ref[...] = dot(ones, d_heads, NT)[0:1]
    d_dense = (dot(head_weight, d_heads, TN) * slope).astype(BF)
    sums_ref[0:1, 128 : 128 + hid] = dot(ones, d_dense, NT)[0:1]
    for j in range(n_own):
        d_dense_ref[j] = d_dense[j * cols : (j + 1) * cols]
    outs = []
    for half, ref, far_ref in ((1, send_ref, send_far_ref), (0, keep_ref, keep_far_ref)):
        for k in range(n_own // 4):
            both = [d_dense_ref[own ^ (4 * k + half)], d_dense_ref[own ^ (4 * k + 2 + half)]]
            block = dot(flat, jnp.concatenate(both, axis=0), NT).astype(BF)
            for i in range(n_dp):
                rel = i ^ dp
                spot = (rel % 2) * (n_dp // 2) + rel // 2
                for m in range(2):
                    ref[2 * k + m, spot] = block[i * rows : (i + 1) * rows, m * cols : (m + 1) * cols]
            for m in range(2 * k, 2 * k + 2):
                outs.append(pltpu.make_async_copy(ref.at[m], far_ref.at[m], out_sems.at[len(outs)]))
                outs[-1].start()
    wait_rows(slope_far_ref, slope_ref, slope_sems)
    total = jnp.zeros((64, n), F32)
    for part in range(7):
        span = slice(part * 448, part * 448 + 448)
        d_three = (dot(weight_ref[span, :], d_dense) * slope_ref[part].astype(F32)).astype(BF)
        slope_ref[part] = d_three
        row_copy(slope_ref, d_three_far_ref, slope_sems, part).start()
        back = d_three.astype(F32)
        for c in range(7):
            total = total + back[c * 64 : c * 64 + 64]
    sums_ref[0:1, 0:64] = dot(jnp.ones((8, n), F32), total, NT, HIGH)[0:1]
    sums_ref[0:1, 64:128] = jnp.zeros((1, 64), F32)
    wait_rows(two_far_ref, two_ref, two_sems)
    wait_rows(slope_ref, d_three_far_ref, slope_sems)
    for copy in outs:
        copy.wait()


def dense(
    place, lengths, heads, bias, actions, adv, values, logp, flat, slope_three, act_two,
    pieces, n_dp, n_own, rows,
):
    n = flat.shape[-1]
    hid = n_own * 128
    part = pltpu.HBM((n_own // 2, n_dp, rows, 128), BF)
    arrays = [far(p[0]) for p in pieces]
    small = [heads, bias, actions, adv, values, logp]
    body = functools.partial(
        dense_kernel, places=[p[1] for p in pieces], n_dp=n_dp, n_own=n_own, rows=rows
    )
    return call(
        body,
        [place, lengths] + [far(a) for a in small + [flat, slope_three, act_two]] + arrays,
        [
            pltpu.HBM(flat.shape, BF),
            near(act_two.shape, BF),
            part,
            part,
            jax.ShapeDtypeStruct(heads.shape, F32),
            jax.ShapeDtypeStruct((1, 128 + hid), F32),
            jax.ShapeDtypeStruct((1, heads.shape[0]), F32),
        ],
        in_specs=[smem(), smem()] + [anywhere()] * (9 + len(arrays)),
        out_specs=[anywhere(), vmem(), anywhere(), anywhere()] + [vmem()] * 3,
        scratch=[
            pltpu.VMEM((n_dp, n_own) + arrays[0].shape[1:], BF),
            pltpu.VMEM((n_dp * rows, hid), BF),
            pltpu.VMEM((n_own, 128, n), BF),
            pltpu.VMEM(flat.shape, BF),
            pltpu.VMEM(flat.shape, BF),
            pltpu.VMEM((n_own // 2, n_dp, rows, 128), BF),
            pltpu.VMEM((n_own // 2, n_dp, rows, 128), BF),
        ]
        + [pltpu.VMEM(a.shape, a.dtype) for a in small]
        + [dma(n_dp * n_own), dma(9), dma(7), dma(7), dma(6), dma(n_own)],
        us=10,
        name="dense",
        limit=32,
    )


def conv_three_back_kernel(
    act_ref, d_three_ref, slope_far_ref, one_far_ref, slope_one_far_ref, weight_ref, heads_ref,
    d_two_ref, one_ref, slope_one_ref, pack_ref, sum_ref,
    band_ref, pad_ref, acc_ref, tot_ref, slope_ref, one_sems, slope_one_sems, slope_sems, d_sems,
):
    n = act_ref.shape[-1]
    step = pl.program_id(0)

    def three_row(r):
        inner = pad_ref.at[r + 2, pl.ds(128, 448), :]
        return pltpu.make_async_copy(d_three_ref.at[r], inner, d_sems.at[r])

    @pl.when(step == 0)
    def _():
        for r in range(7):
            three_row(r).start()
        for r in range(11):
            if 2 <= r < 9:
                pad_ref[r, 0:128, :] = jnp.zeros((128, n), BF)
                pad_ref[r, 576:704, :] = jnp.zeros((128, n), BF)
            else:
                pad_ref[r] = jnp.zeros((704, n), BF)
        start_rows(slope_far_ref, slope_ref, slope_sems)
        band_ref[...] = band_back(weight_ref[...], 3, 64, 3)
        acc_ref[...] = jnp.zeros_like(acc_ref)
        tot_ref[...] = jnp.zeros_like(tot_ref)

    lines = [3 * step + q for q in range(3)]
    for line in lines:

        @pl.when(line < 7)
        def _(line=line):
            three_row(line).wait()

        row_copy(slope_far_ref, slope_ref, slope_sems, line).wait()

    @pl.when(step == 0)
    def _():
        start_rows(one_far_ref, one_ref, one_sems)
        start_rows(slope_one_far_ref, slope_one_ref, slope_one_sems)

    total = tot_ref[...]
    for line in lines:
        for part in range(3):
            patch = jnp.concatenate(
                [pad_ref[line + a, part * 192 : part * 192 + 320, :] for a in range(3)], axis=0
            )
            rows = slice(part * 192, part * 192 + 192)
            d_two = (dot(band_ref[...], patch) * slope_ref[line, rows, :].astype(F32)).astype(BF)
            d_two_ref[line, rows, :] = d_two
            back = d_two.astype(F32)
            total = total + (back[0:64] + back[64:128]) + back[128:192]
    tot_ref[...] = total

    def grads(line):
        row = pad_ref[line + 2, 128 : 128 + 448, :]
        second = jnp.concatenate([jnp.zeros((64, n), BF), row[256:448]], axis=0)
        for d_rows, start in ((row[0:256], 0), (second, 3)):
            span = slice(start * 64, start * 64 + 384)
            cells = jnp.concatenate([act_ref[line + a, span, :] for a in range(3)], axis=0)
            acc_ref[...] += dot(d_rows, cells, NT)

    grads(lines[0])

    @pl.when(step < 2)
    def _():
        grads(lines[1])
        grads(lines[2])

    @pl.when(step == 2)
    def _():
        wait_rows(one_far_ref, one_ref, one_sems)
        wait_rows(slope_one_far_ref, slope_one_ref, slope_one_sems)
        for a in range(3):
            out = None
            for c in range(4):
                piece = acc_ref[c * 64 : c * 64 + 64, a * 384 + c * 64 : a * 384 + c * 64 + 192]
                out = piece if out is None else out + piece
            pack_ref[0:64, a * 192 : a * 192 + 192] = out.astype(BF)
        pack_ref[0:64, 576:640] = jnp.zeros((64, 64), BF)
        pack_ref[64:80, 0:512] = heads_ref[0:16, :].astype(BF)
        pack_ref[80:96, 0:512] = jnp.concatenate(
            [heads_ref[16:19, :], jnp.zeros((13, 512), F32)], axis=0
        ).astype(BF)
        pack_ref[64:96, 512:640] = jnp.zeros((32, 128), BF)
        sum_ref[...] = dot(jnp.ones((8, n), F32), tot_ref[...], NT, HIGH)[0:1]


def conv_three_back(d_three, act_two, slope_two, act_one, slope_one, weight, heads):
    n = act_two.shape[-1]
    return call(
        conv_three_back_kernel,
        [held(act_two)] + [far(a) for a in (d_three, slope_two, act_one, slope_one)] + [weight, heads],
        [
            near(act_two.shape, BF),
            near(act_one.shape, BF),
            near(act_one.shape, BF),
            jax.ShapeDtypeStruct((96, 640), BF),
            jax.ShapeDtypeStruct((1, 64), F32),
        ],
        in_specs=[vmem()] + [anywhere()] * 4 + [vmem()] * 2,
        scratch=[
            pltpu.VMEM((192, 960), BF),
            pltpu.VMEM((11, 704, n), BF),
            pltpu.VMEM((256, 1152), F32),
            pltpu.VMEM((64, n), F32),
            pltpu.VMEM(act_two.shape, BF),
            dma(10),
            dma(10),
            dma(9),
            dma(7),
        ],
        grid=3,
        us=9,
        name="conv_three_back",
        limit=16,
    )


def conv_two_back_kernel(
    d_two_ref, act_ref, slope_ref, weight_ref, pack_ref, d_one_ref, grad_ref, sum_ref,
    band_ref, pad_ref, acc_ref, tot_ref,
):
    n = d_one_ref.shape[-1]
    step = pl.program_id(0)

    @pl.when(step == 0)
    def _():
        band_ref[...] = band_back(weight_ref[...], 2, 128, 1)
        pad_ref[0] = jnp.zeros((704, n), BF)
        pad_ref[10] = jnp.zeros((704, n), BF)
        for r in range(1, 10):
            pad_ref[r, 0:64, :] = jnp.zeros((64, n), BF)
            pad_ref[r, 640:704, :] = jnp.zeros((64, n), BF)
        acc_ref[...] = jnp.zeros_like(acc_ref)
        tot_ref[...] = jnp.zeros_like(tot_ref)

    lines = [5 * step + q for q in range(5)]
    for line in lines[:4]:
        pad_ref[line + 1, 64 : 64 + 576, :] = d_two_ref[line]

    @pl.when(step < 1)
    def _():
        pad_ref[lines[4] + 1, 64 : 64 + 576, :] = d_two_ref[lines[4]]

    total = tot_ref[...]
    for line in lines:
        for col in range(10):
            patch = jnp.concatenate(
                [pad_ref[line + a, col * 64 : col * 64 + 128, :] for a in range(2)], axis=0
            )
            d_one = (dot(band_ref[...], patch) * slope_ref[line, col].astype(F32)).astype(BF)
            d_one_ref[line, col] = d_one
            total = total + d_one.astype(F32)
    tot_ref[...] = total

    def grads(line):
        for part in range(3):
            span = slice(3 * part, 3 * part + 4)
            cells = jnp.concatenate(
                [act_ref[line + a, span].reshape(512, n) for a in range(2)], axis=0
            )
            rows = pad_ref[line + 1, 64 + part * 192 : 64 + part * 192 + 192, :]
            acc_ref[...] += dot(rows, cells, NT)

    for line in lines[:4]:
        grads(line)

    @pl.when(step < 1)
    def _():
        grads(lines[4])

    @pl.when(step == 1)
    def _():
        for a in range(2):
            out = None
            for c in range(3):
                piece = acc_ref[c * 64 : c * 64 + 64, a * 512 + c * 128 : a * 512 + c * 128 + 256]
                out = piece if out is None else out + piece
            grad_ref[96:160, a * 256 : a * 256 + 256] = out.astype(BF)
        grad_ref[0:96, :] = pack_ref[...]
        grad_ref[96:160, 512:640] = jnp.zeros((64, 128), BF)
        sums = dot(jnp.ones((8, n), F32), tot_ref[...], NT, HIGH)[0:1]
        sum_ref[...] = (sums[:, 0:32] + sums[:, 32:64]) + (sums[:, 64:96] + sums[:, 96:128])


def conv_two_back(d_two, act_one, slope_one, weight, pack):
    n = act_one.shape[-1]
    return call(
        conv_two_back_kernel,
        [held(d_two), held(act_one), held(slope_one), weight, pack],
        [
            near(act_one.shape, BF),
            jax.ShapeDtypeStruct((160, 640), BF),
            jax.ShapeDtypeStruct((1, 32), F32),
        ],
        scratch=[
            pltpu.VMEM((128, 256), BF),
            pltpu.VMEM((11, 704, n), BF),
            pltpu.VMEM((192, 1024), F32),
            pltpu.VMEM((128, n), F32),
        ],
        grid=2,
        us=11,
        name="conv_two_back",
        limit=16,
    )


def conv_one_grad_kernel(
    frames_ref, d_one_ref, cells_in_ref, dense_ref, heads_ref, one_ref, two_ref,
    grad_ref, d_out_ref, cells_ref, acc_ref, sems,
):
    n = d_one_ref.shape[-1]
    step = pl.program_id(0)
    half = pl.num_programs(0)

    slots = fetch_rows(frames_ref, cells_ref, sems, step, half - 1)

    @pl.when(step == 0)
    def _():
        acc_ref[...] = jnp.zeros_like(acc_ref)

    for q in range(2):
        for pair in range(5):
            span = slice(pair * 256, pair * 256 + 320)
            cells = jnp.concatenate([cells_ref[slot, span, :] for slot in slots[2 * q : 2 * q + 3]], axis=0)
            rows = d_one_ref[2 * step + q, 2 * pair : 2 * pair + 2].reshape(256, n)
            acc_ref[...] += dot(rows, cells, NT)

    @pl.when(step == half - 1)
    def _():
        for a in range(2):
            out = None
            for k in range(2):
                for dy in range(2):
                    for dx in range(2):
                        row = ((k * 2 + dy) * 2 + dx) * 32
                        lane = (dy + a) * 320 + (2 * k + dx) * 64
                        piece = acc_ref[row : row + 32, lane : lane + 128]
                        out = piece if out is None else out + piece
            grad_ref[:, a * 128 : a * 128 + 128] = out[0:16]
            grad_ref[:, 256 + a * 128 : 384 + a * 128] = out[16:32]
        grad_ref[:, 512:640] = jnp.zeros((16, 128), F32)
        for k in range(4):
            grad_ref[k : k + 1, 512:640] = dense_ref[0:1, 128 + k * 128 : 256 + k * 128]
        grad_ref[4:5, 512:576] = dense_ref[0:1, 0:64]
        grad_ref[5:6, 512:576] = two_ref[...]
        grad_ref[6:7, 512:544] = one_ref[...]
        grad_ref[7:8, 512:531] = heads_ref[...]


def conv_one_grad(frames, d_one, cells, sums, sum_heads, sum_one, sum_two):
    return pl.pallas_call(
        conv_one_grad_kernel,
        out_shape=(
            jax.ShapeDtypeStruct((16, 640), F32),
            near(d_one.shape, BF),
            near(cells.shape, BF),
        ),
        grid=(d_one.shape[0] // 2,),
        in_specs=[anywhere()] + [vmem()] * 6,
        out_specs=(vmem(),) * 3,
        scratch_shapes=[pltpu.VMEM((256, 960), F32), dma(RING)],
        input_output_aliases={1: 1, 2: 2},
        compiler_params=params(16),
        cost_estimate=cost(10),
        name="conv_one_grad",
    )(far(frames), held(d_one), held(cells), sums, sum_heads, sum_one, sum_two)


def frames_back_kernel(*refs, begin, end, total, ahead):
    d_one_ref, weight_ref = refs[:2]
    if ahead:
        frames_ref = refs[2]
        out_ref, d_out_ref, cells_ref, band_ref, rows_ref, sems, cell_sems = refs[-7:]
    else:
        band_ref = weight_ref
        out_ref, d_out_ref, rows_ref, sems = refs[-4:]
    n = rows_ref.shape[-1]
    cells = d_one_ref.shape[1]
    zero = jnp.zeros((32, n), BF)
    if ahead:
        for r in range(5):
            ring_copy(frames_ref, cells_ref, cell_sems, r).start()
        band_ref[...] = band_back(weight_ref[...], 2, 64, 3)

    def slab(line, first):
        parts = []
        for c in range(first, first + 4):
            if c < 0 or c >= 2 * cells or line < 0 or line >= 2 * cells:
                parts.append(zero)
            else:
                spot = (line % 2 * 2 + c % 2) * 32
                parts.append(d_one_ref[line // 2, c // 2, spot : spot + 32, :])
        return jnp.concatenate(parts, axis=0)

    def send(line):
        spot = line - 2 * begin
        return pltpu.make_async_copy(rows_ref.at[spot], out_ref.at[line], sems.at[spot])

    lines = range(2 * begin, min(2 * end, 2 * total - 1))
    for line in lines:
        for block in range(7):
            first = 3 * block - 1
            patch = jnp.concatenate([slab(line - 1, first), slab(line, first)], axis=0)
            rows = slice(block * 192, block * 192 + 192)
            rows_ref[line - 2 * begin, rows, :] = dot(band_ref[...], patch).astype(BF)
        send(line).start()
    for line in lines:
        send(line).wait()
    if ahead:
        for r in range(5):
            ring_copy(frames_ref, cells_ref, cell_sems, r).wait()


def frames_back(d_one, weight, shape, begin, end, so_far=None, frames=None):
    total = d_one.shape[0] + 1
    ahead = frames is not None
    more = [far(frames)] if ahead else [] if so_far is None else [so_far]
    count = end - begin
    cells = [near((RING,) + shape[1:], BF), jax.ShapeDtypeStruct((192, 256), BF)] if ahead else []
    return call(
        functools.partial(frames_back_kernel, begin=begin, end=end, total=total, ahead=ahead),
        [held(d_one), weight] + more,
        [pltpu.HBM(shape, BF), near(d_one.shape, BF)] + cells,
        in_specs=[vmem(), vmem()] + [anywhere()] * len(more),
        out_specs=[anywhere(), vmem()] + [vmem()] * len(cells),
        scratch=[pltpu.VMEM((2 * count,) + shape[1:], BF), dma(2 * count)] + [dma(5)] * ahead,
        us=count,
        name="frames_back",
        aliases={0: 1, 2: 0} if so_far is not None else {0: 1},
        limit=16,
    )


def adam_terms(grad, mean, square):
    momentum = BETA * mean + (1.0 - BETA) * grad
    variance = BETA * square + (1.0 - BETA) * grad * grad
    fix = 1.0 - BETA**STEP
    direction = momentum / fix / (jnp.sqrt(variance / fix) + EPSILON)
    return (momentum, variance, direction)


def split(x):
    top = x.astype(BF)
    return top, (x - top.astype(F32)).astype(BF)


def dot3(a, b, dims=NN):
    a_top, a_low = split(a)
    b_top, b_low = split(b)
    if dims == TN:
        return dot(a_top, b_top, dims) + (dot(a_top, b_low, dims) + dot(a_low, b_top, dims))
    rows = a.shape[0]
    both = dot(jnp.concatenate([a_top, a_low], axis=0), b_top, dims)
    return both[:rows] + (both[rows:] + dot(a_top, b_low, dims))


def dot2(a, b, dims=NN):
    rows = a.shape[0]
    both = dot(jnp.concatenate(split(a), axis=0), b, dims)
    return both[:rows] + both[rows:]


def turned_step(weight, grad, mean, square, left, right):
    rate = RATE / math.sqrt(weight.shape[1])
    left = left.astype(BF)
    turned = dot2(dot3(right, grad, TN), left)
    momentum, variance, direction = adam_terms(turned, mean, square)
    back = dot2(dot3(right, direction), left, NT)
    return momentum, variance, weight - rate * back


def steps_kernel(*refs, spots):
    count = len(spots)
    packs = 1 + max(spot[0] for spot in spots)
    ins, outs = refs[packs : packs + 5 * count], refs[packs + 5 * count :]
    for w, (pack, row, rows, cols) in enumerate(spots):
        grad = refs[pack][row : row + rows, 0:cols].astype(F32)
        if rows == 16:
            grad = jnp.concatenate([grad, refs[pack][row : row + rows, cols : 2 * cols]], axis=0)
        weight, mean, square, left, right = [ref[...] for ref in ins[5 * w : 5 * w + 5]]
        results = (grad,) + turned_step(weight, grad, mean, square, left, right)
        for ref, value in zip(outs[4 * w : 4 * w + 4], results):
            ref[...] = value


def steps(packs, spots, groups):
    arrays = []
    shapes = []
    for weight, mean, square, left, right in groups:
        arrays += [weight.T, mean.T, square.T, left, right]
        shapes += [jax.ShapeDtypeStruct(weight.shape[::-1], F32)] * 4
    return pl.pallas_call(
        functools.partial(steps_kernel, spots=spots),
        out_shape=tuple(shapes),
        in_specs=[vmem()] * (len(packs) + len(arrays)),
        out_specs=(vmem(),) * len(shapes),
        compiler_params=params(32),
        cost_estimate=cost(5),
        name="steps",
    )(*packs, *arrays)


def dense_step_kernel(*refs, rate):
    weight_ref, mean_ref, square_ref, block_ref = refs[:4]
    grad_ref, mom_ref, var_ref, new_ref = refs[-4:]
    grad = None
    for ref in refs[4:-4]:
        part = ref[...].astype(F32)
        grad = part if grad is None else grad + part
    grad_ref[...] = grad
    turned = dot3(grad, block_ref[0])
    momentum, variance, direction = adam_terms(turned, mean_ref[...], square_ref[...])
    mom_ref[...] = momentum
    var_ref[...] = variance
    new_ref[...] = weight_ref[...] - rate * dot3(direction, block_ref[0], NT)


def dense_step(weight, mean, square, block, parts, rate):
    shape = jax.ShapeDtypeStruct(weight.shape, F32)
    return pl.pallas_call(
        functools.partial(dense_step_kernel, rate=rate),
        out_shape=(shape,) * 4,
        in_specs=[vmem()] * (4 + len(parts)),
        out_specs=(vmem(),) * 4,
        compiler_params=params(),
        cost_estimate=cost(3),
        name="dense_step",
    )(weight, mean, square, block, *parts)


def swap(x, axis, bit, size):
    return lax.ppermute(x, axis, [(i, i ^ bit) for i in range(size)])


def bits_of(size):
    return [1 << b for b in range(size.bit_length() - 1)]


def fence(*values):
    leaves, tree = jax.tree.flatten(values)
    return jax.tree.unflatten(tree, lax.optimization_barrier(tuple(leaves)))


def add_low(*terms):
    total = terms[0].astype(F32)
    for term in terms[1:]:
        total = total + term.astype(F32)
    return total.astype(BF)


def plain_gather(piece, n_dp, n_own):
    pieces = piece[None]
    spots = [(0, 0)]
    for bit in bits_of(n_dp):
        pieces = jnp.concatenate([pieces, swap(pieces, "dp", bit, n_dp)], axis=0)
        spots = spots + [(i ^ bit, j) for i, j in spots]
    for bit in bits_of(n_own):
        pieces = jnp.concatenate([pieces, swap(pieces, "own", bit, n_own)], axis=0)
        spots = spots + [(i, j ^ bit) for i, j in spots]
    return [(pieces, spots)]


def plain_scatter(keep, send, n_dp, n_own):
    block = add_low(keep, swap(send, "own", 1, n_own))
    bit = n_own // 2
    while bit > 1:
        half = block.shape[0] // 2
        block = add_low(block[:half], swap(block[half:], "own", bit, n_own))
        bit //= 2
    block = block[0]
    for bit in [1] + bits_of(n_dp)[:0:-1]:
        half = block.shape[0] // 2
        block = add_low(block[:half], swap(block[half:], "dp", bit, n_dp))
    return [block[0]]


def shards(
    frames, actions, dones, lengths, rewards, old_values, old_logp,
    conv_first, conv_second, conv_third, dense_hidden, dense_heads, bias_all,
    mean_first, mean_second, mean_third, mean_dense, mean_heads, mean_bias,
    square_first, square_second, square_third, square_dense, square_heads, square_bias,
    left_first, right_first, left_second, right_second, left_third, right_third,
    right_dense, left_heads, right_heads, *, n_dp, n_own,
):
    tokens, grid = frames.shape[0], frames.shape[1]
    planes = frames.shape[3]
    rows = dense_hidden.shape[0]
    tuned = (n_dp, n_own) == (8, 4)
    own_swap = lambda x, bit: swap(x, "own", bit, n_own)
    dp_swap = lambda x, bit: swap(x, "dp", bit, n_dp)
    place = jnp.stack([lax.axis_index("dp"), lax.axis_index("own")]).astype(jnp.int32)
    bias_row = bias_all.reshape(1, -1)
    cells = frames.transpose(1, 2, 3, 0).reshape(grid, grid * planes, tokens)
    adv, piece, ring = first(lengths, dones, rewards, old_values, dense_hidden, cells)

    if tuned:
        along_z = [dp_swap(piece, 2 * k) for k in (1, 2, 3)]
    act_one, slope_one, _ = conv_one(cells, conv_first.T, bias_row, ring)
    if tuned:
        spots = [(2 * k, 0) for k in range(4)]
        act_one, slope_one, piece, along_z = fence(act_one, slope_one, piece, along_z)
        column = jnp.stack([piece] + along_z)
        act_one, slope_one, column = fence(act_one, slope_one, column)
        by_x, by_y = dp_swap(column, 1), own_swap(column, 2)
    else:
        pieces = plain_gather(piece, n_dp, n_own)
    act_two, slope_two, act_one_far, slope_one_far = conv_two(act_one, slope_one, conv_second.T, bias_row)
    if tuned:
        act_two, slope_two, column, by_x, by_y = fence(act_two, slope_two, column, by_x, by_y)
        halves = (by_x[0:2], by_y[2:4])
        plane = jnp.concatenate([column, by_x, by_y])
        act_two, slope_two, halves, plane = fence(act_two, slope_two, halves, plane)
        corner = [own_swap(halves[0], 2), dp_swap(halves[1], 1)]
        other = own_swap(plane, 1)
    flat, slope_three, act_two_far, slope_two_far = conv_three(act_two, slope_two, conv_third.T, bias_row)
    if tuned:
        flat, corner = fence(flat, corner)
        corner = jnp.concatenate(corner)
        plane_spots = [(i ^ x, j ^ y) for x, y in ((0, 0), (1, 0), (0, 2)) for i, j in spots]
        corner_spots = [(i ^ 1, j ^ 2) for i, j in spots]
        pieces = [(plane, plane_spots), (corner, corner_spots)]
        pieces += [
            (other, [(i, j ^ 1) for i, j in plane_spots]),
            (own_swap(corner, 1), [(i, j ^ 1) for i, j in corner_spots]),
        ]
    d_three, act_two, keep, send, here_heads, sums, sum_heads = dense(
        place, lengths, dense_heads.T, bias_row, actions, adv, old_values, old_logp,
        flat, slope_three, act_two_far, pieces, n_dp, n_own, rows,
    )

    came = own_swap(send, 1) if tuned else None
    d_two, act_one, slope_one, pack, sum_two = conv_three_back(
        d_three, act_two, slope_two_far, act_one_far, slope_one_far, conv_third.T, here_heads
    )
    if tuned:
        d_two, act_one, slope_one, keep, came = fence(d_two, act_one, slope_one, keep, came)
        block = add_low(keep, came)
        ends = (block[1, 4:6], block[1, 6:8])
        d_two, act_one, slope_one, block, ends = fence(d_two, act_one, slope_one, block, ends)
        by_y, by_x = own_swap(ends[0], 2), dp_swap(ends[1], 1)
    d_one, pack, sum_one = conv_two_back(d_two, act_one, slope_one, conv_second.T, pack)

    shape = cells.shape
    side = lax.axis_index("own") % 2
    rows_half = pack.shape[0] // 2
    if tuned:
        d_one, pack, block, by_x, by_y = fence(d_one, pack, block, by_x, by_y)
        side_x = jnp.concatenate([add_low(block[0, 4:6], by_y), block[0, 6:8]])
        side_y = jnp.concatenate([block[1, 0:2], add_low(block[1, 2:4], by_x)])
        block = block[0, 0:4]
    else:
        side_x = side_y = block = jnp.zeros((8, 128), BF)
    half = lax.dynamic_slice_in_dim(pack, side * rows_half, rows_half)
    gone = lax.dynamic_slice_in_dim(pack, (1 - side) * rows_half, rows_half)
    d_one, half, gone, block, side_x, side_y = fence(d_one, half, gone, block, side_x, side_y)
    if tuned:
        by_x, by_y = dp_swap(side_x, 1), own_swap(side_y, 2)
    came = own_swap(gone, 1)
    cuts = (0, 2, 5, 8, grid // 2 + 1)
    back, d_one, ring, band = frames_back(d_one, conv_first.T, shape, cuts[0], cuts[1], frames=cells)
    back, d_one, ring, half, came = fence(back, d_one, ring, half, came)
    half = add_low(half, came)
    back, d_one, ring, half = fence(back, d_one, ring, half)
    far_bits = bits_of(n_dp)[:0:-1]
    came = dp_swap(half, far_bits[0])
    pack_one, d_one, _ = conv_one_grad(cells, d_one, ring, sums, sum_heads, sum_one, sum_two)
    if tuned:
        pack_one, d_one, block, by_x, by_y = fence(pack_one, d_one, block, by_x, by_y)
        block = add_low(block, by_x, by_y)
    pack_one, d_one, half, came = fence(pack_one, d_one, half, came)

    half = add_low(half, came)
    pack_one, d_one, half, block = fence(pack_one, d_one, half, block)
    came_one = dp_swap(pack_one, far_bits[0])
    came = own_swap(half, 2)
    if tuned:
        parts = [block[0]] + [dp_swap(block[k], 2 * k) for k in (1, 2, 3)]
    else:
        parts = plain_scatter(keep, send, n_dp, n_own)
    back, d_one = frames_back(d_one, band, shape, cuts[1], cuts[2], back)
    back, d_one, half, came, pack_one, came_one = fence(back, d_one, half, came, pack_one, came_one)

    def join(pack, pack_one):
        return jnp.concatenate([pack.astype(BF), *split(pack_one)])

    def part(both):
        count = pack_one.shape[0]
        low = both[rows_half:].astype(F32)
        return both[:rows_half].astype(F32), low[:count] + low[count:]

    def add_up(both, came):
        a, b = part(both), part(came)
        return a[0] + b[0], a[1] + b[1]

    both = join(add_low(half, came), pack_one + came_one)
    back, d_one, both = fence(back, d_one, both)
    more = [1] + far_bits[1:]
    came = dp_swap(both, more[0])
    back, d_one = frames_back(d_one, band, shape, cuts[2], cuts[3], back)
    back, d_one, both, came = fence(back, d_one, both, came)
    both = join(*add_up(both, came))
    back, d_one, both = fence(back, d_one, both)
    came = dp_swap(both, more[1])
    back, d_one = frames_back(d_one, band, shape, cuts[3], cuts[4], back)
    for bit in more[2:]:
        both = join(*add_up(both, came))
        came = dp_swap(both, bit)
    back, parts, both, came = fence(back, parts, both, came)
    both = join(*add_up(both, came))
    parts, both = fence(parts, both)
    came = own_swap(both, 1)
    frames_grad = back.reshape(grid, grid, planes, tokens).transpose(3, 0, 1, 2)
    grad_dense, *wide_step = dense_step(
        dense_hidden, mean_dense, square_dense, right_dense, parts, RATE / math.sqrt(rows * n_dp)
    )
    grad_dense, both, came = fence(grad_dense, both, came)
    pack_one = add_up(both, came)[1]
    halves = (both[:rows_half], came[:rows_half])
    pack = jnp.concatenate([jnp.where(side == 0, *halves), jnp.where(side == 0, *halves[::-1])])
    pack_one, pack = fence(pack_one, pack)
    one = own_swap(pack_one, 2)
    late = steps(
        [pack],
        [(0, 0, 64, 576), (0, 64, 19, 512), (0, 96, 64, 512)],
        [
            (conv_third, mean_third, square_third, left_third, right_third),
            (dense_heads, mean_heads, square_heads, left_heads, right_heads),
            (conv_second, mean_second, square_second, left_second, right_second),
        ],
    )
    late, pack_one, one = fence(late, pack_one, one)
    pack_one = pack_one + one
    third, top, second = late[0:4], late[4:8], late[8:12]
    first_step = steps(
        [pack_one],
        [(0, 0, 16, 256)],
        [(conv_first, mean_first, square_first, left_first, right_first)],
    )
    line = pack_one[:, 512:]
    grad_bias = jnp.concatenate(
        [line[6, 0:32], line[5, 0:64], line[4, 0:64], line[0], line[1], line[2], line[3], line[7, 0:19]]
    )
    mom_bias, var_bias, bias_dir = adam_terms(grad_bias, mean_bias, square_bias)
    new_bias = bias_all - BIAS_RATE * bias_dir
    outs = [frames_grad]
    wide_step = [grad_dense] + list(wide_step)
    for index, bias_part in enumerate((grad_bias, mom_bias, var_bias, new_bias)):
        outs += [first_step[index].T, second[index].T, third[index].T, wide_step[index], top[index].T, bias_part]
    return tuple(outs)


def solution(mesh):
    n_dp, n_own = mesh.shape["dp"], mesh.shape["own"]
    both = ("dp", "own")
    rep = P()
    in_specs = (
        (P(both, None, None, None), P(both, None), P(both, None), P(both))
        + (P(both, None),) * 3
        + (rep, rep, rep, P("dp", "own"), rep, rep) * 3
        + (rep,) * 6
        + (P("own", None, None), rep, rep)
    )
    out_specs = (P(both, None, None, None),) + (rep, rep, rep, P("dp", "own"), rep, rep) * 4
    body = functools.partial(shards, n_dp=n_dp, n_own=n_own)
    return jax.shard_map(body, mesh=mesh, in_specs=in_specs, out_specs=out_specs, check_vma=False)
```

```python
import functools
import math

import jax
import jax.numpy as jnp
from jax import lax
from jax.experimental import pallas as pl
from jax.experimental.pallas import tpu as pltpu
from jax.sharding import PartitionSpec as P

STEP = 10
GAMMA = 0.99
LAMBDA = 0.95
CLIP = 0.1
ENTROPY_COEF = 0.01
VALUE_COEF = 0.5
BETA = 0.5
EPSILON = 1e-08
RATE = 1.0
BIAS_RATE = 0.1
HIGH = lax.Precision.HIGHEST
ROOT = math.sqrt(2.0 / math.pi)
CUBE = 0.044715
BF = jnp.bfloat16
F32 = jnp.float32
MIB = 2**20

NN = (((1,), (0,)), ((), ()))
NT = (((1,), (1,)), ((), ()))
TN = (((0,), (0,)), ((), ()))


def dot(a, b, dims=NN, precision=None):
    return lax.dot_general(a, b, dims, precision=precision, preferred_element_type=F32)


def params(limit=32, **more):
    return pltpu.CompilerParams(vmem_limit_bytes=limit * MIB, **more)


def cost(us):
    return pl.CostEstimate(flops=int(us * 1e9), bytes_accessed=0, transcendentals=0)


def near(shape, dtype):
    return pltpu.VMEM(shape, dtype)


def held(x):
    return pltpu.with_memory_space_constraint(x, pltpu.VMEM)


def far(x):
    return pltpu.with_memory_space_constraint(x, pltpu.HBM)


def vmem():
    return pl.BlockSpec(memory_space=pltpu.VMEM)


def smem():
    return pl.BlockSpec(memory_space=pltpu.SMEM)


def anywhere():
    return pl.BlockSpec(memory_space=pl.ANY)


def row_copy(source, target, sems, r):
    return pltpu.make_async_copy(source.at[r], target.at[r], sems.at[r])


def start_rows(source, target, sems):
    for r in range(source.shape[0]):
        row_copy(source, target, sems, r).start()


def wait_rows(source, target, sems):
    for r in range(source.shape[0]):
        row_copy(source, target, sems, r).wait()


def call(body, ins, outs, in_specs=None, out_specs=None, scratch=(), grid=None, us=5, name=None, aliases=None, limit=24):
    more = {} if grid is None else {"grid": (grid,)}
    return pl.pallas_call(
        body,
        out_shape=tuple(outs),
        in_specs=list(in_specs or [vmem()] * len(ins)),
        out_specs=tuple(out_specs or [vmem()] * len(outs)),
        scratch_shapes=list(scratch),
        input_output_aliases=aliases or {},
        compiler_params=params(limit),
        cost_estimate=cost(us),
        name=name,
        **more,
    )(*ins)


def dma(count):
    return pltpu.SemaphoreType.DMA((count,))


def gelu_both(x):
    x2 = x * x
    up = 1.0 + jnp.tanh(x * (ROOT + (ROOT * CUBE) * x2))
    h = 0.5 * x
    bend = h * (ROOT + (3.0 * ROOT * CUBE) * x2)
    return h * up, up * (0.5 + bend * (2.0 - up))


def wide(line, rows, n):
    k = line.shape[1]
    column = jnp.broadcast_to(line, (128, k)).T
    tall = jnp.concatenate([column] * (rows // k), axis=0) if rows > k else column
    return jnp.concatenate([tall] * (n // 128), axis=1)


def lanes(parts):
    return jnp.concatenate([p for p in parts if p.shape[1] > 0], axis=1)


def band_forward(w, kernel, feats, count):
    ch = w.shape[0]
    run = kernel * feats
    rows = []
    for j in range(count):
        parts = []
        for a in range(kernel):
            parts.append(jnp.zeros((ch, j * feats), F32))
            parts.append(w[:, a * run : (a + 1) * run])
            parts.append(jnp.zeros((ch, (count - 1 - j) * feats), F32))
        rows.append(lanes(parts))
    return jnp.concatenate(rows, axis=0).astype(BF)


def band_square(w, feats):
    ch = w.shape[0]
    rows = []
    for dy in range(2):
        for dx in range(2):
            lead = (dy * 3 + dx) * feats
            rows.append(
                lanes(
                    [
                        jnp.zeros((ch, lead), F32),
                        w[:, : 2 * feats],
                        jnp.zeros((ch, feats), F32),
                        w[:, 2 * feats :],
                        jnp.zeros((ch, 4 * feats - lead), F32),
                    ]
                )
            )
    return jnp.concatenate(rows, axis=0).astype(BF)


def band_back(w, kernel, feats, count):
    ch = w.shape[0]
    turned = w.T
    zero = jnp.zeros((feats, ch), F32)
    rows = []
    for i in range(count):
        parts = []
        for a in range(kernel):
            for j in range(kernel + count - 1):
                b = j - i
                if 0 <= b < kernel:
                    spot = ((kernel - 1 - a) * kernel + (kernel - 1 - b)) * feats
                    parts.append(turned[spot : spot + feats])
                else:
                    parts.append(zero)
        rows.append(lanes(parts))
    return jnp.concatenate(rows, axis=0).astype(BF)


def first_kernel(
    lengths_ref, dones_far_ref, rewards_far_ref, values_far_ref, weight_far_ref, frames_ref,
    adv_ref, piece_ref, cells_ref, dones_ref, rewards_ref, values_ref, weight_ref, sems, small_sems,
):
    near_refs = (dones_ref, rewards_ref, values_ref, weight_ref)
    far_refs = (dones_far_ref, rewards_far_ref, values_far_ref, weight_far_ref)
    small = [pltpu.make_async_copy(a, b, small_sems.at[k]) for k, (a, b) in enumerate(zip(far_refs, near_refs))]
    for copy in small:
        copy.start()
    for r in range(5):
        ring_copy(frames_ref, cells_ref, sems, r).start()
    for copy in small:
        copy.wait()
    n = rewards_ref.shape[1]
    length = lengths_ref[0]
    position = lax.broadcasted_iota(jnp.int32, (8, n), 1)
    live = position < length
    mask = jnp.where(live, 1.0, 0.0)
    next_live = jnp.where(position + 1 < length, 1.0, 0.0)
    values = jnp.broadcast_to(values_ref[...], (8, n))
    rewards = jnp.broadcast_to(rewards_ref[...], (8, n))
    going = 1.0 - jnp.broadcast_to(dones_ref[...], (8, n)).astype(F32)

    def ahead(v, k, fill):
        return jnp.concatenate([v[:, k:], jnp.full((8, k), fill, F32)], axis=1)

    delta = rewards + GAMMA * going * ahead(values, 1, 0.0) * next_live - values
    total = mask * delta
    carry = mask * (GAMMA * LAMBDA) * going
    k = 1
    while k < n:
        total = total + carry * ahead(total, k, 0.0)
        carry = carry * ahead(carry, k, 0.0)
        k *= 2
    adv_ref[...] = total[0:1]
    count = jnp.sum(mask, axis=1, keepdims=True)
    mean = jnp.sum(mask * total, axis=1, keepdims=True) / count
    spread = jnp.sum(mask * (total - mean) ** 2, axis=1, keepdims=True)
    lane = lax.broadcasted_iota(jnp.int32, (8, 128), 1)
    stat = jnp.where(lane == 0, count, jnp.where(lane == 1, mean, jnp.where(lane == 2, spread, 0.0)))
    top = stat.astype(BF).astype(F32)
    mid = (stat - top).astype(BF).astype(F32)
    low = ((stat - top) - mid).astype(BF).astype(F32)
    line = lax.broadcasted_iota(jnp.int32, (8, 128), 0)
    terms = jnp.where(line == 0, top, jnp.where(line == 1, mid, jnp.where(line == 2, low, 0.0)))
    rows = weight_ref.shape[0]
    tail = piece_ref.shape[0] - 16
    lead = max(rows - tail, 0)
    if tail > rows:
        piece_ref[rows // 16 * 16 : tail, :] = jnp.zeros((tail - rows // 16 * 16, 128), BF)
    piece_ref[0 : min(rows, tail), :] = weight_ref[0 : min(rows, tail), :].astype(BF)
    last = [weight_ref[rows - lead :, :]] if lead else []
    last += [jnp.zeros((8 - lead, 128), F32)] if lead < 8 else []
    piece_ref[tail:, :] = jnp.concatenate(last + [terms], axis=0).astype(BF)
    for r in range(5):
        ring_copy(frames_ref, cells_ref, sems, r).wait()


def first(lengths, dones, rewards, old_values, weight, frames):
    n = rewards.shape[1]
    rows = -(-weight.shape[0] // 16) * 16
    rows += 16 if weight.shape[0] - (rows - 16) > 8 else 0
    small = [dones, rewards, old_values, weight]
    return pl.pallas_call(
        first_kernel,
        out_shape=(
            jax.ShapeDtypeStruct((1, n), F32),
            jax.ShapeDtypeStruct((rows, 128), BF),
            near((RING,) + frames.shape[1:], BF),
        ),
        in_specs=[smem()] + [anywhere()] * 5,
        out_specs=(vmem(),) * 3,
        scratch_shapes=[pltpu.VMEM(a.shape, a.dtype) for a in small] + [dma(5), dma(4)],
        compiler_params=params(16),
        cost_estimate=cost(3),
        name="first",
    )(lengths, *[far(a) for a in small], far(frames))


RING = 10


def ring_copy(frames_ref, cells_ref, sems, r):
    slot = r % RING if isinstance(r, int) else lax.rem(r, RING)
    return pltpu.make_async_copy(frames_ref.at[r], cells_ref.at[slot], sems.at[slot])


def fetch_rows(frames_ref, cells_ref, sems, step, last):
    @pl.when(step < last)
    def _():
        for a in range(5, 9):
            ring_copy(frames_ref, cells_ref, sems, 4 * step + a).start()

    @pl.when(step >= 1)
    def _():
        for a in range(1, 5):
            ring_copy(frames_ref, cells_ref, sems, 4 * step + a).wait()

    return [lax.rem(4 * step + a, RING) for a in range(5)]


def conv_one_kernel(
    frames_ref, weight_ref, bias_ref, cells_in_ref, act_ref, slope_ref, cells_ref, band_ref, wide_ref, sems
):
    n = act_ref.shape[-1]
    half = act_ref.shape[0]
    step = pl.program_id(0)

    slots = fetch_rows(frames_ref, cells_ref, sems, step, half // 2 - 1)

    @pl.when(step == 0)
    def _():
        band_ref[...] = band_square(weight_ref[...], 64)
        wide_ref[...] = wide(bias_ref[:, 0:32], 128, n)

    for q in range(2):
        for col in range(half):
            span = slice(col * 128, col * 128 + 192)
            patch = jnp.concatenate([cells_ref[slot, span, :] for slot in slots[2 * q : 2 * q + 3]], axis=0)
            act, slope = gelu_both(dot(band_ref[...], patch) + wide_ref[...])
            act_ref[2 * step + q, col] = act.astype(BF)
            slope_ref[2 * step + q, col] = slope.astype(BF)


def conv_one(frames, weight, bias, cells):
    grid, _, n = frames.shape
    half = grid // 2
    shape = (half, half, 128, n)
    return call(
        conv_one_kernel,
        [far(frames), weight, bias, held(cells)],
        [near(shape, BF), near(shape, BF), near(cells.shape, BF)],
        in_specs=[anywhere()] + [vmem()] * 3,
        scratch=[pltpu.VMEM((128, 576), BF), pltpu.VMEM((128, n), F32), dma(RING)],
        grid=half // 2,
        us=12,
        name="conv_one",
        aliases={3: 2},
        limit=16,
    )


def conv_two_kernel(
    one_ref, slope_one_ref, weight_ref, bias_ref, act_ref, slope_ref, one_far_ref, slope_one_far_ref,
    band_ref, wide_ref, sems, slope_sems,
):
    n = act_ref.shape[-1]
    step = pl.program_id(0)

    @pl.when(step == 0)
    def _():
        start_rows(one_ref, one_far_ref, sems)
        start_rows(slope_one_ref, slope_one_far_ref, slope_sems)
        band_ref[...] = band_forward(weight_ref[...], 2, 128, 3)
        wide_ref[...] = wide(bias_ref[:, 32:96], 192, n)

    for row in range(9):
        for part in range(3):
            span = slice(3 * part, 3 * part + 4)
            patch = jnp.concatenate(
                [one_ref[row + a, span].reshape(512, n) for a in range(2)], axis=0
            )
            act, slope = gelu_both(dot(band_ref[...], patch) + wide_ref[...])
            rows = slice(part * 192, part * 192 + 192)
            act_ref[row, rows, :] = act.astype(BF)
            slope_ref[row, rows, :] = slope.astype(BF)

    @pl.when(step == 0)
    def _():
        wait_rows(one_ref, one_far_ref, sems)
        wait_rows(slope_one_ref, slope_one_far_ref, slope_sems)


def conv_two(act_one, slope_one, weight, bias):
    n = act_one.shape[-1]
    shape = (9, 576, n)
    return call(
        conv_two_kernel,
        [held(act_one), held(slope_one), weight, bias],
        [near(shape, BF)] * 2 + [pltpu.HBM(act_one.shape, BF)] * 2,
        out_specs=[vmem(), vmem(), anywhere(), anywhere()],
        scratch=[pltpu.VMEM((192, 1024), BF), pltpu.VMEM((192, n), F32), dma(10), dma(10)],
        grid=1,
        us=7,
        name="conv_two",
        limit=16,
    )


def conv_three_kernel(
    two_ref, slope_two_ref, weight_ref, bias_ref,
    flat_far_ref, slope_far_ref, two_far_ref, slope_two_far_ref,
    band_ref, wide_ref, flat_ref, slope_ref, two_sems, slope_two_sems, flat_sems, slope_sems,
):
    n = two_ref.shape[-1]
    start_rows(two_ref, two_far_ref, two_sems)
    start_rows(slope_two_ref, slope_two_far_ref, slope_two_sems)
    band_ref[...] = band_forward(weight_ref[...], 3, 64, 4)
    wide_ref[...] = wide(bias_ref[:, 96:160], 256, n)
    for row in range(7):
        for drop, start in ((0, 0), (1, 3)):
            patch = jnp.concatenate(
                [two_ref[row + a, start * 64 : start * 64 + 384, :] for a in range(3)], axis=0
            )
            pre = dot(band_ref[drop * 64 :, :], patch) + wide_ref[drop * 64 :, :]
            act, slope = gelu_both(pre)
            rows = slice((start + drop) * 64, (start + 4) * 64)
            flat_ref[row, rows, :] = act.astype(BF)
            slope_ref[row, rows, :] = slope.astype(BF)
        row_copy(flat_ref, flat_far_ref, flat_sems, row).start()
        row_copy(slope_ref, slope_far_ref, slope_sems, row).start()
    wait_rows(two_ref, two_far_ref, two_sems)
    wait_rows(slope_two_ref, slope_two_far_ref, slope_two_sems)
    wait_rows(flat_ref, flat_far_ref, flat_sems)
    wait_rows(slope_ref, slope_far_ref, slope_sems)


def conv_three(act_two, slope_two, weight, bias):
    n = act_two.shape[-1]
    shape = (7, 448, n)
    out, two = pltpu.HBM(shape, BF), pltpu.HBM(act_two.shape, BF)
    return call(
        conv_three_kernel,
        [held(act_two), held(slope_two), weight, bias],
        [out, out, two, two],
        out_specs=[anywhere()] * 4,
        scratch=[
            pltpu.VMEM((256, 1152), BF),
            pltpu.VMEM((256, n), F32),
            pltpu.VMEM(shape, BF),
            pltpu.VMEM(shape, BF),
            dma(9),
            dma(9),
            dma(7),
            dma(7),
        ],
        us=6,
        name="conv_three",
        limit=16,
    )


def head_gradient(heads, actions, adv, values, old_logp, mask, count, centre, var):
    rows, n = heads.shape
    acts = rows - 1
    norm_adv = (adv - centre) * lax.rsqrt(var + 1e-05)
    returns = adv + values
    index = lax.broadcasted_iota(jnp.int32, (rows, n), 0)
    is_logit = index < acts
    top = jnp.max(jnp.where(is_logit, heads, -jnp.inf), axis=0, keepdims=True)
    shifted = heads - top
    grown = jnp.where(is_logit, jnp.exp(jnp.where(is_logit, shifted, 0.0)), 0.0)
    total = jnp.sum(grown, axis=0, keepdims=True)
    logp_all = jnp.where(is_logit, shifted - jnp.log(total), 0.0)
    prob = jnp.where(is_logit, jnp.exp(logp_all), 0.0)
    chosen = jnp.where(index == actions, 1.0, 0.0)
    logp = jnp.sum(logp_all * chosen, axis=0, keepdims=True)
    plogp = jnp.sum(prob * logp_all, axis=0, keepdims=True)
    value = jnp.sum(jnp.where(index == acts, heads, 0.0), axis=0, keepdims=True)
    ratio = jnp.exp(logp - old_logp)
    bent = jnp.tanh((ratio - 1.0) / CLIP)
    soft = 1.0 + CLIP * bent
    plain = ratio * norm_adv
    clipped = soft * norm_adv
    share = jnp.where(plain < clipped, 1.0, jnp.where(plain > clipped, 0.0, 0.5))
    by_ratio = -norm_adv * (share + (1.0 - share) * (1.0 - bent * bent))
    scale = mask / count
    by_logp = by_ratio * ratio
    by_logit = by_logp * (chosen - prob) + ENTROPY_COEF * prob * (logp_all - plogp)
    by_value = VALUE_COEF * (value - returns)
    return jnp.where(is_logit, by_logit, by_value) * scale


def dense_kernel(*refs, places, n_dp, n_own, rows):
    place_ref, lengths_ref = refs[:2]
    small_far_refs, (flat_far_ref, slope_far_ref, two_far_ref) = refs[2:8], refs[8:11]
    piece_refs = refs[11 : 11 + len(places)]
    (
        d_three_far_ref, two_ref, keep_far_ref, send_far_ref, grad_heads_ref, sums_ref, sum_heads_ref,
        blocks_ref, weight_ref, d_dense_ref, flat_ref, slope_ref, keep_ref, send_ref, *small_refs,
        sems, two_sems, flat_sems, slope_sems, small_sems, out_sems,
    ) = refs[11 + len(places) :]
    heads_ref, bias_ref, actions_ref, adv_ref, values_ref, logp_ref = small_refs
    n = flat_ref.shape[-1]
    cols = 128
    dp, own = place_ref[0], place_ref[1]
    stats = []
    copies = []
    for ref, spots in zip(piece_refs, places):
        for k, (i, j) in enumerate(spots):
            copies.append(
                pltpu.make_async_copy(ref.at[k], blocks_ref.at[i ^ dp, j ^ own], sems.at[len(copies)])
            )
    for k in range(6):
        copies.append(pltpu.make_async_copy(small_far_refs[k], small_refs[k], small_sems.at[k]))
    for copy in copies:
        copy.start()
    start_rows(flat_far_ref, flat_ref, flat_sems)
    for copy in copies:
        copy.wait()
    start_rows(slope_far_ref, slope_ref, slope_sems)
    start_rows(two_far_ref, two_ref, two_sems)
    for i in range(n_dp):
        for j in range(n_own):
            tail = blocks_ref[i, j, blocks_ref.shape[2] - 16 :].astype(F32)
            stats.append((tail[8:9] + tail[9:10]) + tail[10:11])
    stats = jnp.concatenate(stats, axis=0)
    each = stats[:, 0:1]
    count = jnp.sum(each, axis=0, keepdims=True)
    centre = jnp.sum(each * stats[:, 1:2], axis=0, keepdims=True) / count
    gap = stats[:, 1:2] - centre
    var = jnp.sum(stats[:, 2:3] + each * gap * gap, axis=0, keepdims=True) / count
    for i in range(n_dp):
        for j in range(n_own):
            weight_ref[i * rows : (i + 1) * rows, j * cols : (j + 1) * cols] = blocks_ref[i, j, 0:rows]
    hid = n_own * cols
    bias_dense = wide(bias_ref[:, 160 : 160 + hid], hid, n)
    bias_heads = wide(bias_ref[:, 160 + hid : 160 + hid + 19], 19, n)
    wait_rows(flat_far_ref, flat_ref, flat_sems)
    flat = flat_ref[...].reshape(n_dp * rows, n)
    pre = dot(flat, weight_ref[...], TN).T + bias_dense
    hidden, slope = gelu_both(pre)
    hidden = hidden.astype(BF)
    head_weight = heads_ref[...].astype(BF)
    heads = dot(head_weight, hidden) + bias_heads
    position = lax.broadcasted_iota(jnp.int32, (1, n), 1)
    mask = jnp.where(position < lengths_ref[0], 1.0, 0.0)
    d_heads = head_gradient(
        heads, actions_ref[...], adv_ref[...], values_ref[...], logp_ref[...], mask, count, centre, var
    ).astype(BF)
    ones = jnp.ones((8, n), BF)
    grad_heads_ref[...] = dot(d_heads, hidden, NT)
    sum_heads_ref[...] = dot(ones, d_heads, NT)[0:1]
    d_dense = (dot(head_weight, d_heads, TN) * slope).astype(BF)
    sums_ref[0:1, 128 : 128 + hid] = dot(ones, d_dense, NT)[0:1]
    for j in range(n_own):
        d_dense_ref[j] = d_dense[j * cols : (j + 1) * cols]
    outs = []
    for half, ref, far_ref in ((1, send_ref, send_far_ref), (0, keep_ref, keep_far_ref)):
        for k in range(n_own // 4):
            both = [d_dense_ref[own ^ (4 * k + half)], d_dense_ref[own ^ (4 * k + 2 + half)]]
            block = dot(flat, jnp.concatenate(both, axis=0), NT).astype(BF)
            for i in range(n_dp):
                rel = i ^ dp
                spot = (rel % 2) * (n_dp // 2) + rel // 2
                for m in range(2):
                    ref[2 * k + m, spot] = block[i * rows : (i + 1) * rows, m * cols : (m + 1) * cols]
            for m in range(2 * k, 2 * k + 2):
                outs.append(pltpu.make_async_copy(ref.at[m], far_ref.at[m], out_sems.at[len(outs)]))
                outs[-1].start()
    wait_rows(slope_far_ref, slope_ref, slope_sems)
    total = jnp.zeros((64, n), F32)
    for part in range(7):
        span = slice(part * 448, part * 448 + 448)
        d_three = (dot(weight_ref[span, :], d_dense) * slope_ref[part].astype(F32)).astype(BF)
        slope_ref[part] = d_three
        row_copy(slope_ref, d_three_far_ref, slope_sems, part).start()
        back = d_three.astype(F32)
        for c in range(7):
            total = total + back[c * 64 : c * 64 + 64]
    sums_ref[0:1, 0:64] = dot(jnp.ones((8, n), F32), total, NT, HIGH)[0:1]
    sums_ref[0:1, 64:128] = jnp.zeros((1, 64), F32)
    wait_rows(two_far_ref, two_ref, two_sems)
    wait_rows(slope_ref, d_three_far_ref, slope_sems)
    for copy in outs:
        copy.wait()


def dense(
    place, lengths, heads, bias, actions, adv, values, logp, flat, slope_three, act_two,
    pieces, n_dp, n_own, rows,
):
    n = flat.shape[-1]
    hid = n_own * 128
    part = pltpu.HBM((n_own // 2, n_dp, rows, 128), BF)
    arrays = [far(p[0]) for p in pieces]
    small = [heads, bias, actions, adv, values, logp]
    body = functools.partial(
        dense_kernel, places=[p[1] for p in pieces], n_dp=n_dp, n_own=n_own, rows=rows
    )
    return call(
        body,
        [place, lengths] + [far(a) for a in small + [flat, slope_three, act_two]] + arrays,
        [
            pltpu.HBM(flat.shape, BF),
            near(act_two.shape, BF),
            part,
            part,
            jax.ShapeDtypeStruct(heads.shape, F32),
            jax.ShapeDtypeStruct((1, 128 + hid), F32),
            jax.ShapeDtypeStruct((1, heads.shape[0]), F32),
        ],
        in_specs=[smem(), smem()] + [anywhere()] * (9 + len(arrays)),
        out_specs=[anywhere(), vmem(), anywhere(), anywhere()] + [vmem()] * 3,
        scratch=[
            pltpu.VMEM((n_dp, n_own) + arrays[0].shape[1:], BF),
            pltpu.VMEM((n_dp * rows, hid), BF),
            pltpu.VMEM((n_own, 128, n), BF),
            pltpu.VMEM(flat.shape, BF),
            pltpu.VMEM(flat.shape, BF),
            pltpu.VMEM((n_own // 2, n_dp, rows, 128), BF),
            pltpu.VMEM((n_own // 2, n_dp, rows, 128), BF),
        ]
        + [pltpu.VMEM(a.shape, a.dtype) for a in small]
        + [dma(n_dp * n_own), dma(9), dma(7), dma(7), dma(6), dma(n_own)],
        us=10,
        name="dense",
        limit=32,
    )


def conv_three_back_kernel(
    act_ref, d_three_ref, slope_far_ref, one_far_ref, slope_one_far_ref, weight_ref, heads_ref,
    d_two_ref, one_ref, slope_one_ref, pack_ref, sum_ref,
    band_ref, pad_ref, acc_ref, tot_ref, slope_ref, one_sems, slope_one_sems, slope_sems, d_sems,
):
    n = act_ref.shape[-1]
    step = pl.program_id(0)

    def three_row(r):
        inner = pad_ref.at[r + 2, pl.ds(128, 448), :]
        return pltpu.make_async_copy(d_three_ref.at[r], inner, d_sems.at[r])

    @pl.when(step == 0)
    def _():
        for r in range(7):
            three_row(r).start()
        for r in range(11):
            if 2 <= r < 9:
                pad_ref[r, 0:128, :] = jnp.zeros((128, n), BF)
                pad_ref[r, 576:704, :] = jnp.zeros((128, n), BF)
            else:
                pad_ref[r] = jnp.zeros((704, n), BF)
        start_rows(slope_far_ref, slope_ref, slope_sems)
        band_ref[...] = band_back(weight_ref[...], 3, 64, 3)
        acc_ref[...] = jnp.zeros_like(acc_ref)
        tot_ref[...] = jnp.zeros_like(tot_ref)

    lines = [3 * step + q for q in range(3)]
    for line in lines:

        @pl.when(line < 7)
        def _(line=line):
            three_row(line).wait()

        row_copy(slope_far_ref, slope_ref, slope_sems, line).wait()

    @pl.when(step == 0)
    def _():
        start_rows(one_far_ref, one_ref, one_sems)
        start_rows(slope_one_far_ref, slope_one_ref, slope_one_sems)

    total = tot_ref[...]
    for line in lines:
        for part in range(3):
            patch = jnp.concatenate(
                [pad_ref[line + a, part * 192 : part * 192 + 320, :] for a in range(3)], axis=0
            )
            rows = slice(part * 192, part * 192 + 192)
            d_two = (dot(band_ref[...], patch) * slope_ref[line, rows, :].astype(F32)).astype(BF)
            d_two_ref[line, rows, :] = d_two
            back = d_two.astype(F32)
            total = total + (back[0:64] + back[64:128]) + back[128:192]
    tot_ref[...] = total

    def grads(line):
        row = pad_ref[line + 2, 128 : 128 + 448, :]
        second = jnp.concatenate([jnp.zeros((64, n), BF), row[256:448]], axis=0)
        for d_rows, start in ((row[0:256], 0), (second, 3)):
            span = slice(start * 64, start * 64 + 384)
            cells = jnp.concatenate([act_ref[line + a, span, :] for a in range(3)], axis=0)
            acc_ref[...] += dot(d_rows, cells, NT)

    grads(lines[0])

    @pl.when(step < 2)
    def _():
        grads(lines[1])
        grads(lines[2])

    @pl.when(step == 2)
    def _():
        wait_rows(one_far_ref, one_ref, one_sems)
        wait_rows(slope_one_far_ref, slope_one_ref, slope_one_sems)
        for a in range(3):
            out = None
            for c in range(4):
                piece = acc_ref[c * 64 : c * 64 + 64, a * 384 + c * 64 : a * 384 + c * 64 + 192]
                out = piece if out is None else out + piece
            pack_ref[0:64, a * 192 : a * 192 + 192] = out.astype(BF)
        pack_ref[0:64, 576:640] = jnp.zeros((64, 64), BF)
        pack_ref[64:80, 0:512] = heads_ref[0:16, :].astype(BF)
        pack_ref[80:96, 0:512] = jnp.concatenate(
            [heads_ref[16:19, :], jnp.zeros((13, 512), F32)], axis=0
        ).astype(BF)
        pack_ref[64:96, 512:640] = jnp.zeros((32, 128), BF)
        sum_ref[...] = dot(jnp.ones((8, n), F32), tot_ref[...], NT, HIGH)[0:1]


def conv_three_back(d_three, act_two, slope_two, act_one, slope_one, weight, heads):
    n = act_two.shape[-1]
    return call(
        conv_three_back_kernel,
        [held(act_two)] + [far(a) for a in (d_three, slope_two, act_one, slope_one)] + [weight, heads],
        [
            near(act_two.shape, BF),
            near(act_one.shape, BF),
            near(act_one.shape, BF),
            jax.ShapeDtypeStruct((96, 640), BF),
            jax.ShapeDtypeStruct((1, 64), F32),
        ],
        in_specs=[vmem()] + [anywhere()] * 4 + [vmem()] * 2,
        scratch=[
            pltpu.VMEM((192, 960), BF),
            pltpu.VMEM((11, 704, n), BF),
            pltpu.VMEM((256, 1152), F32),
            pltpu.VMEM((64, n), F32),
            pltpu.VMEM(act_two.shape, BF),
            dma(10),
            dma(10),
            dma(9),
            dma(7),
        ],
        grid=3,
        us=9,
        name="conv_three_back",
        limit=16,
    )


def conv_two_back_kernel(
    d_two_ref, act_ref, slope_ref, weight_ref, pack_ref, d_one_ref, grad_ref, sum_ref,
    band_ref, pad_ref, acc_ref, tot_ref,
):
    n = d_one_ref.shape[-1]
    step = pl.program_id(0)

    @pl.when(step == 0)
    def _():
        band_ref[...] = band_back(weight_ref[...], 2, 128, 1)
        pad_ref[0] = jnp.zeros((704, n), BF)
        pad_ref[10] = jnp.zeros((704, n), BF)
        for r in range(1, 10):
            pad_ref[r, 0:64, :] = jnp.zeros((64, n), BF)
            pad_ref[r, 640:704, :] = jnp.zeros((64, n), BF)
        acc_ref[...] = jnp.zeros_like(acc_ref)
        tot_ref[...] = jnp.zeros_like(tot_ref)

    lines = [5 * step + q for q in range(5)]
    for line in lines[:4]:
        pad_ref[line + 1, 64 : 64 + 576, :] = d_two_ref[line]

    @pl.when(step < 1)
    def _():
        pad_ref[lines[4] + 1, 64 : 64 + 576, :] = d_two_ref[lines[4]]

    total = tot_ref[...]
    for line in lines:
        for col in range(10):
            patch = jnp.concatenate(
                [pad_ref[line + a, col * 64 : col * 64 + 128, :] for a in range(2)], axis=0
            )
            d_one = (dot(band_ref[...], patch) * slope_ref[line, col].astype(F32)).astype(BF)
            d_one_ref[line, col] = d_one
            total = total + d_one.astype(F32)
    tot_ref[...] = total

    def grads(line):
        for part in range(3):
            span = slice(3 * part, 3 * part + 4)
            cells = jnp.concatenate(
                [act_ref[line + a, span].reshape(512, n) for a in range(2)], axis=0
            )
            rows = pad_ref[line + 1, 64 + part * 192 : 64 + part * 192 + 192, :]
            acc_ref[...] += dot(rows, cells, NT)

    for line in lines[:4]:
        grads(line)

    @pl.when(step < 1)
    def _():
        grads(lines[4])

    @pl.when(step == 1)
    def _():
        for a in range(2):
            out = None
            for c in range(3):
                piece = acc_ref[c * 64 : c * 64 + 64, a * 512 + c * 128 : a * 512 + c * 128 + 256]
                out = piece if out is None else out + piece
            grad_ref[96:160, a * 256 : a * 256 + 256] = out.astype(BF)
        grad_ref[0:96, :] = pack_ref[...]
        grad_ref[96:160, 512:640] = jnp.zeros((64, 128), BF)
        sums = dot(jnp.ones((8, n), F32), tot_ref[...], NT, HIGH)[0:1]
        sum_ref[...] = (sums[:, 0:32] + sums[:, 32:64]) + (sums[:, 64:96] + sums[:, 96:128])


def conv_two_back(d_two, act_one, slope_one, weight, pack):
    n = act_one.shape[-1]
    return call(
        conv_two_back_kernel,
        [held(d_two), held(act_one), held(slope_one), weight, pack],
        [
            near(act_one.shape, BF),
            jax.ShapeDtypeStruct((160, 640), BF),
            jax.ShapeDtypeStruct((1, 32), F32),
        ],
        scratch=[
            pltpu.VMEM((128, 256), BF),
            pltpu.VMEM((11, 704, n), BF),
            pltpu.VMEM((192, 1024), F32),
            pltpu.VMEM((128, n), F32),
        ],
        grid=2,
        us=11,
        name="conv_two_back",
        limit=16,
    )


def conv_one_grad_kernel(
    frames_ref, d_one_ref, cells_in_ref, dense_ref, heads_ref, one_ref, two_ref,
    grad_ref, d_out_ref, cells_ref, acc_ref, sems,
):
    n = d_one_ref.shape[-1]
    step = pl.program_id(0)
    half = pl.num_programs(0)

    slots = fetch_rows(frames_ref, cells_ref, sems, step, half - 1)

    @pl.when(step == 0)
    def _():
        acc_ref[...] = jnp.zeros_like(acc_ref)

    for q in range(2):
        for pair in range(5):
            span = slice(pair * 256, pair * 256 + 320)
            cells = jnp.concatenate([cells_ref[slot, span, :] for slot in slots[2 * q : 2 * q + 3]], axis=0)
            rows = d_one_ref[2 * step + q, 2 * pair : 2 * pair + 2].reshape(256, n)
            acc_ref[...] += dot(rows, cells, NT)

    @pl.when(step == half - 1)
    def _():
        for a in range(2):
            out = None
            for k in range(2):
                for dy in range(2):
                    for dx in range(2):
                        row = ((k * 2 + dy) * 2 + dx) * 32
                        lane = (dy + a) * 320 + (2 * k + dx) * 64
                        piece = acc_ref[row : row + 32, lane : lane + 128]
                        out = piece if out is None else out + piece
            grad_ref[:, a * 128 : a * 128 + 128] = out[0:16]
            grad_ref[:, 256 + a * 128 : 384 + a * 128] = out[16:32]
        grad_ref[:, 512:640] = jnp.zeros((16, 128), F32)
        for k in range(4):
            grad_ref[k : k + 1, 512:640] = dense_ref[0:1, 128 + k * 128 : 256 + k * 128]
        grad_ref[4:5, 512:576] = dense_ref[0:1, 0:64]
        grad_ref[5:6, 512:576] = two_ref[...]
        grad_ref[6:7, 512:544] = one_ref[...]
        grad_ref[7:8, 512:531] = heads_ref[...]


def conv_one_grad(frames, d_one, cells, sums, sum_heads, sum_one, sum_two):
    return pl.pallas_call(
        conv_one_grad_kernel,
        out_shape=(
            jax.ShapeDtypeStruct((16, 640), F32),
            near(d_one.shape, BF),
            near(cells.shape, BF),
        ),
        grid=(d_one.shape[0] // 2,),
        in_specs=[anywhere()] + [vmem()] * 6,
        out_specs=(vmem(),) * 3,
        scratch_shapes=[pltpu.VMEM((256, 960), F32), dma(RING)],
        input_output_aliases={1: 1, 2: 2},
        compiler_params=params(16),
        cost_estimate=cost(10),
        name="conv_one_grad",
    )(far(frames), held(d_one), held(cells), sums, sum_heads, sum_one, sum_two)


def frames_back_kernel(*refs, begin, end, total, ahead):
    d_one_ref, weight_ref = refs[:2]
    if ahead:
        frames_ref = refs[2]
        out_ref, d_out_ref, cells_ref, band_ref, rows_ref, sems, cell_sems = refs[-7:]
    else:
        band_ref = weight_ref
        out_ref, d_out_ref, rows_ref, sems = refs[-4:]
    n = rows_ref.shape[-1]
    cells = d_one_ref.shape[1]
    zero = jnp.zeros((32, n), BF)
    if ahead:
        for r in range(5):
            ring_copy(frames_ref, cells_ref, cell_sems, r).start()
        band_ref[...] = band_back(weight_ref[...], 2, 64, 3)

    def slab(line, first):
        parts = []
        for c in range(first, first + 4):
            if c < 0 or c >= 2 * cells or line < 0 or line >= 2 * cells:
                parts.append(zero)
            else:
                spot = (line % 2 * 2 + c % 2) * 32
                parts.append(d_one_ref[line // 2, c // 2, spot : spot + 32, :])
        return jnp.concatenate(parts, axis=0)

    def send(line):
        spot = line - 2 * begin
        return pltpu.make_async_copy(rows_ref.at[spot], out_ref.at[line], sems.at[spot])

    lines = range(2 * begin, min(2 * end, 2 * total - 1))
    for line in lines:
        for block in range(7):
            first = 3 * block - 1
            patch = jnp.concatenate([slab(line - 1, first), slab(line, first)], axis=0)
            rows = slice(block * 192, block * 192 + 192)
            rows_ref[line - 2 * begin, rows, :] = dot(band_ref[...], patch).astype(BF)
        send(line).start()
    for line in lines:
        send(line).wait()
    if ahead:
        for r in range(5):
            ring_copy(frames_ref, cells_ref, cell_sems, r).wait()


def frames_back(d_one, weight, shape, begin, end, so_far=None, frames=None):
    total = d_one.shape[0] + 1
    ahead = frames is not None
    more = [far(frames)] if ahead else [] if so_far is None else [so_far]
    count = end - begin
    cells = [near((RING,) + shape[1:], BF), jax.ShapeDtypeStruct((192, 256), BF)] if ahead else []
    return call(
        functools.partial(frames_back_kernel, begin=begin, end=end, total=total, ahead=ahead),
        [held(d_one), weight] + more,
        [pltpu.HBM(shape, BF), near(d_one.shape, BF)] + cells,
        in_specs=[vmem(), vmem()] + [anywhere()] * len(more),
        out_specs=[anywhere(), vmem()] + [vmem()] * len(cells),
        scratch=[pltpu.VMEM((2 * count,) + shape[1:], BF), dma(2 * count)] + [dma(5)] * ahead,
        us=count,
        name="frames_back",
        aliases={0: 1, 2: 0} if so_far is not None else {0: 1},
        limit=16,
    )


def adam_terms(grad, mean, square):
    momentum = BETA * mean + (1.0 - BETA) * grad
    variance = BETA * square + (1.0 - BETA) * grad * grad
    fix = 1.0 - BETA**STEP
    direction = momentum / fix / (jnp.sqrt(variance / fix) + EPSILON)
    return (momentum, variance, direction)


def split(x):
    top = x.astype(BF)
    return top, (x - top.astype(F32)).astype(BF)


def dot3(a, b, dims=NN):
    a_top, a_low = split(a)
    b_top, b_low = split(b)
    if dims == TN:
        return dot(a_top, b_top, dims) + (dot(a_top, b_low, dims) + dot(a_low, b_top, dims))
    rows = a.shape[0]
    both = dot(jnp.concatenate([a_top, a_low], axis=0), b_top, dims)
    return both[:rows] + (both[rows:] + dot(a_top, b_low, dims))


def dot2(a, b, dims=NN):
    rows = a.shape[0]
    both = dot(jnp.concatenate(split(a), axis=0), b, dims)
    return both[:rows] + both[rows:]


def turned_step(weight, grad, mean, square, left, right):
    rate = RATE / math.sqrt(weight.shape[1])
    left = left.astype(BF)
    turned = dot2(dot3(right, grad, TN), left)
    momentum, variance, direction = adam_terms(turned, mean, square)
    back = dot2(dot3(right, direction), left, NT)
    return momentum, variance, weight - rate * back


def steps_kernel(*refs, spots):
    count = len(spots)
    packs = 1 + max(spot[0] for spot in spots)
    ins, outs = refs[packs : packs + 5 * count], refs[packs + 5 * count :]
    for w, (pack, row, rows, cols) in enumerate(spots):
        grad = refs[pack][row : row + rows, 0:cols].astype(F32)
        if rows == 16:
            grad = jnp.concatenate([grad, refs[pack][row : row + rows, cols : 2 * cols]], axis=0)
        weight, mean, square, left, right = [ref[...] for ref in ins[5 * w : 5 * w + 5]]
        results = (grad,) + turned_step(weight, grad, mean, square, left, right)
        for ref, value in zip(outs[4 * w : 4 * w + 4], results):
            ref[...] = value


def steps(packs, spots, groups):
    arrays = []
    shapes = []
    for weight, mean, square, left, right in groups:
        arrays += [weight.T, mean.T, square.T, left, right]
        shapes += [jax.ShapeDtypeStruct(weight.shape[::-1], F32)] * 4
    return pl.pallas_call(
        functools.partial(steps_kernel, spots=spots),
        out_shape=tuple(shapes),
        in_specs=[vmem()] * (len(packs) + len(arrays)),
        out_specs=(vmem(),) * len(shapes),
        compiler_params=params(32),
        cost_estimate=cost(5),
        name="steps",
    )(*packs, *arrays)


def dense_step_kernel(*refs, rate):
    weight_ref, mean_ref, square_ref, block_ref = refs[:4]
    grad_ref, mom_ref, var_ref, new_ref = refs[-4:]
    grad = None
    for ref in refs[4:-4]:
        part = ref[...].astype(F32)
        grad = part if grad is None else grad + part
    grad_ref[...] = grad
    turned = dot3(grad, block_ref[0])
    momentum, variance, direction = adam_terms(turned, mean_ref[...], square_ref[...])
    mom_ref[...] = momentum
    var_ref[...] = variance
    new_ref[...] = weight_ref[...] - rate * dot3(direction, block_ref[0], NT)


def dense_step(weight, mean, square, block, parts, rate):
    shape = jax.ShapeDtypeStruct(weight.shape, F32)
    return pl.pallas_call(
        functools.partial(dense_step_kernel, rate=rate),
        out_shape=(shape,) * 4,
        in_specs=[vmem()] * (4 + len(parts)),
        out_specs=(vmem(),) * 4,
        compiler_params=params(),
        cost_estimate=cost(3),
        name="dense_step",
    )(weight, mean, square, block, *parts)


def swap(x, axis, bit, size):
    return lax.ppermute(x, axis, [(i, i ^ bit) for i in range(size)])


def bits_of(size):
    return [1 << b for b in range(size.bit_length() - 1)]


def fence(*values):
    leaves, tree = jax.tree.flatten(values)
    return jax.tree.unflatten(tree, lax.optimization_barrier(tuple(leaves)))


def add_low(*terms):
    total = terms[0].astype(F32)
    for term in terms[1:]:
        total = total + term.astype(F32)
    return total.astype(BF)


def plain_gather(piece, n_dp, n_own):
    pieces = piece[None]
    spots = [(0, 0)]
    for bit in bits_of(n_dp):
        pieces = jnp.concatenate([pieces, swap(pieces, "dp", bit, n_dp)], axis=0)
        spots = spots + [(i ^ bit, j) for i, j in spots]
    for bit in bits_of(n_own):
        pieces = jnp.concatenate([pieces, swap(pieces, "own", bit, n_own)], axis=0)
        spots = spots + [(i, j ^ bit) for i, j in spots]
    return [(pieces, spots)]


def plain_scatter(keep, send, n_dp, n_own):
    block = add_low(keep, swap(send, "own", 1, n_own))
    bit = n_own // 2
    while bit > 1:
        half = block.shape[0] // 2
        block = add_low(block[:half], swap(block[half:], "own", bit, n_own))
        bit //= 2
    block = block[0]
    for bit in [1] + bits_of(n_dp)[:0:-1]:
        half = block.shape[0] // 2
        block = add_low(block[:half], swap(block[half:], "dp", bit, n_dp))
    return [block[0]]


def shards(
    frames, actions, dones, lengths, rewards, old_values, old_logp,
    conv_first, conv_second, conv_third, dense_hidden, dense_heads, bias_all,
    mean_first, mean_second, mean_third, mean_dense, mean_heads, mean_bias,
    square_first, square_second, square_third, square_dense, square_heads, square_bias,
    left_first, right_first, left_second, right_second, left_third, right_third,
    right_dense, left_heads, right_heads, *, n_dp, n_own,
):
    tokens, grid = frames.shape[0], frames.shape[1]
    planes = frames.shape[3]
    rows = dense_hidden.shape[0]
    tuned = (n_dp, n_own) == (8, 4)
    own_swap = lambda x, bit: swap(x, "own", bit, n_own)
    dp_swap = lambda x, bit: swap(x, "dp", bit, n_dp)
    place = jnp.stack([lax.axis_index("dp"), lax.axis_index("own")]).astype(jnp.int32)
    bias_row = bias_all.reshape(1, -1)
    cells = frames.transpose(1, 2, 3, 0).reshape(grid, grid * planes, tokens)
    adv, piece, ring = first(lengths, dones, rewards, old_values, dense_hidden, cells)

    if tuned:
        along_z = [dp_swap(piece, 2 * k) for k in (1, 2, 3)]
    act_one, slope_one, _ = conv_one(cells, conv_first.T, bias_row, ring)
    if tuned:
        spots = [(2 * k, 0) for k in range(4)]
        act_one, slope_one, piece, along_z = fence(act_one, slope_one, piece, along_z)
        column = jnp.stack([piece] + along_z)
        act_one, slope_one, column = fence(act_one, slope_one, column)
        by_x, by_y = dp_swap(column, 1), own_swap(column, 2)
    else:
        pieces = plain_gather(piece, n_dp, n_own)
    act_two, slope_two, act_one_far, slope_one_far = conv_two(act_one, slope_one, conv_second.T, bias_row)
    if tuned:
        act_two, slope_two, column, by_x, by_y = fence(act_two, slope_two, column, by_x, by_y)
        halves = (by_x[0:2], by_y[2:4])
        plane = jnp.concatenate([column, by_x, by_y])
        act_two, slope_two, halves, plane = fence(act_two, slope_two, halves, plane)
        corner = [own_swap(halves[0], 2), dp_swap(halves[1], 1)]
        other = own_swap(plane, 1)
    flat, slope_three, act_two_far, slope_two_far = conv_three(act_two, slope_two, conv_third.T, bias_row)
    if tuned:
        flat, corner = fence(flat, corner)
        corner = jnp.concatenate(corner)
        plane_spots = [(i ^ x, j ^ y) for x, y in ((0, 0), (1, 0), (0, 2)) for i, j in spots]
        corner_spots = [(i ^ 1, j ^ 2) for i, j in spots]
        pieces = [(plane, plane_spots), (corner, corner_spots)]
        pieces += [
            (other, [(i, j ^ 1) for i, j in plane_spots]),
            (own_swap(corner, 1), [(i, j ^ 1) for i, j in corner_spots]),
        ]
    d_three, act_two, keep, send, here_heads, sums, sum_heads = dense(
        place, lengths, dense_heads.T, bias_row, actions, adv, old_values, old_logp,
        flat, slope_three, act_two_far, pieces, n_dp, n_own, rows,
    )

    came = own_swap(send, 1) if tuned else None
    d_two, act_one, slope_one, pack, sum_two = conv_three_back(
        d_three, act_two, slope_two_far, act_one_far, slope_one_far, conv_third.T, here_heads
    )
    if tuned:
        d_two, act_one, slope_one, keep, came = fence(d_two, act_one, slope_one, keep, came)
        block = add_low(keep, came)
        ends = (block[1, 4:6], block[1, 6:8])
        d_two, act_one, slope_one, block, ends = fence(d_two, act_one, slope_one, block, ends)
        by_y, by_x = own_swap(ends[0], 2), dp_swap(ends[1], 1)
    d_one, pack, sum_one = conv_two_back(d_two, act_one, slope_one, conv_second.T, pack)

    shape = cells.shape
    side = lax.axis_index("own") % 2
    rows_half = pack.shape[0] // 2
    if tuned:
        d_one, pack, block, by_x, by_y = fence(d_one, pack, block, by_x, by_y)
        side_x = jnp.concatenate([add_low(block[0, 4:6], by_y), block[0, 6:8]])
        side_y = jnp.concatenate([block[1, 0:2], add_low(block[1, 2:4], by_x)])
        block = block[0, 0:4]
    else:
        side_x = side_y = block = jnp.zeros((8, 128), BF)
    half = lax.dynamic_slice_in_dim(pack, side * rows_half, rows_half)
    gone = lax.dynamic_slice_in_dim(pack, (1 - side) * rows_half, rows_half)
    d_one, half, gone, block, side_x, side_y = fence(d_one, half, gone, block, side_x, side_y)
    if tuned:
        by_x, by_y = dp_swap(side_x, 1), own_swap(side_y, 2)
    came = own_swap(gone, 1)
    cuts = (0, 1, 4, 7, grid // 2 + 1)
    back, d_one, ring, band = frames_back(d_one, conv_first.T, shape, cuts[0], cuts[1], frames=cells)
    back, d_one, ring, half, came = fence(back, d_one, ring, half, came)
    half = add_low(half, came)
    back, d_one, ring, half = fence(back, d_one, ring, half)
    far_bits = bits_of(n_dp)[:0:-1]
    came = dp_swap(half, far_bits[0])
    pack_one, d_one, _ = conv_one_grad(cells, d_one, ring, sums, sum_heads, sum_one, sum_two)
    if tuned:
        pack_one, d_one, block, by_x, by_y = fence(pack_one, d_one, block, by_x, by_y)
        block = add_low(block, by_x, by_y)
    pack_one, d_one, half, came = fence(pack_one, d_one, half, came)

    half = add_low(half, came)
    pack_one, d_one, half, block = fence(pack_one, d_one, half, block)
    came_one = dp_swap(pack_one, far_bits[0])
    came = own_swap(half, 2)
    if tuned:
        parts = [block[0]] + [dp_swap(block[k], 2 * k) for k in (1, 2, 3)]
    else:
        parts = plain_scatter(keep, send, n_dp, n_own)
    back, d_one = frames_back(d_one, band, shape, cuts[1], cuts[2], back)
    back, d_one, half, came, pack_one, came_one = fence(back, d_one, half, came, pack_one, came_one)

    def join(pack, pack_one):
        return jnp.concatenate([pack.astype(BF), *split(pack_one)])

    def part(both):
        count = pack_one.shape[0]
        low = both[rows_half:].astype(F32)
        return both[:rows_half].astype(F32), low[:count] + low[count:]

    def add_up(both, came):
        a, b = part(both), part(came)
        return a[0] + b[0], a[1] + b[1]

    both = join(add_low(half, came), pack_one + came_one)
    back, d_one, both = fence(back, d_one, both)
    more = [1] + far_bits[1:]
    came = dp_swap(both, more[0])
    back, d_one = frames_back(d_one, band, shape, cuts[2], cuts[3], back)
    back, d_one, both, came = fence(back, d_one, both, came)
    both = join(*add_up(both, came))
    back, d_one, both = fence(back, d_one, both)
    came = dp_swap(both, more[1])
    back, d_one = frames_back(d_one, band, shape, cuts[3], cuts[4], back)
    for bit in more[2:]:
        both = join(*add_up(both, came))
        came = dp_swap(both, bit)
    back, parts, both, came = fence(back, parts, both, came)
    both = join(*add_up(both, came))
    parts, both = fence(parts, both)
    came = own_swap(both, 1)
    frames_grad = back.reshape(grid, grid, planes, tokens).transpose(3, 0, 1, 2)
    grad_dense, *wide_step = dense_step(
        dense_hidden, mean_dense, square_dense, right_dense, parts, RATE / math.sqrt(rows * n_dp)
    )
    grad_dense, both, came = fence(grad_dense, both, came)
    pack_one = add_up(both, came)[1]
    halves = (both[:rows_half], came[:rows_half])
    pack = jnp.concatenate([jnp.where(side == 0, *halves), jnp.where(side == 0, *halves[::-1])])
    pack_one, pack = fence(pack_one, pack)
    one = own_swap(pack_one, 2)
    late = steps(
        [pack],
        [(0, 0, 64, 576), (0, 64, 19, 512), (0, 96, 64, 512)],
        [
            (conv_third, mean_third, square_third, left_third, right_third),
            (dense_heads, mean_heads, square_heads, left_heads, right_heads),
            (conv_second, mean_second, square_second, left_second, right_second),
        ],
    )
    late, pack_one, one = fence(late, pack_one, one)
    pack_one = pack_one + one
    third, top, second = late[0:4], late[4:8], late[8:12]
    first_step = steps(
        [pack_one],
        [(0, 0, 16, 256)],
        [(conv_first, mean_first, square_first, left_first, right_first)],
    )
    line = pack_one[:, 512:]
    grad_bias = jnp.concatenate(
        [line[6, 0:32], line[5, 0:64], line[4, 0:64], line[0], line[1], line[2], line[3], line[7, 0:19]]
    )
    mom_bias, var_bias, bias_dir = adam_terms(grad_bias, mean_bias, square_bias)
    new_bias = bias_all - BIAS_RATE * bias_dir
    outs = [frames_grad]
    wide_step = [grad_dense] + list(wide_step)
    for index, bias_part in enumerate((grad_bias, mom_bias, var_bias, new_bias)):
        outs += [first_step[index].T, second[index].T, third[index].T, wide_step[index], top[index].T, bias_part]
    return tuple(outs)


def solution(mesh):
    n_dp, n_own = mesh.shape["dp"], mesh.shape["own"]
    both = ("dp", "own")
    rep = P()
    in_specs = (
        (P(both, None, None, None), P(both, None), P(both, None), P(both))
        + (P(both, None),) * 3
        + (rep, rep, rep, P("dp", "own"), rep, rep) * 3
        + (rep,) * 6
        + (P("own", None, None), rep, rep)
    )
    out_specs = (P(both, None, None, None),) + (rep, rep, rep, P("dp", "own"), rep, rep) * 4
    body = functools.partial(shards, n_dp=n_dp, n_own=n_own)
    return jax.shard_map(body, mesh=mesh, in_specs=in_specs, out_specs=out_specs, check_vma=False)
```
